32 devices in a mesh: group: 2 (over y), ctx: 4 (over x, core), exp: 4 (over z).
Axes of the slice: x: 2, y: 2, z: 4, core: 2. Of those that a mesh axis runs over, the one named last changes fastest.
Arguments:
- queries: bfloat16 [8, 512, 4608], P(('group', 'exp'), 'ctx'), parts along dimension 0, may hold values from -10 to 10
- latent_kv: bfloat16 [8, 512, 576], P(('group', 'exp'), 'ctx'), parts along dimension 0, may hold values from -8 to 8
- doc_lengths: int32 [8, 8], P(('group', 'exp')), parts along dimension 0, may hold values from 1 to 256, 512 in all within a row
- hidden_in: bfloat16 [8, 512, 1024], P(('group', 'exp'), 'ctx'), parts along dimension 0, may hold values from -6 to 6
- router_weight: bfloat16 [1024, 64], replicated, may hold values from -0.1875 to 0.1875
- expert_ids: int32 [8, 512, 6], P(('group', 'exp'), 'ctx'), parts along dimension 0, may hold values from 0 to 63, all different within a row; in each aligned block of 128 rows (0 to 127, 128 to 255, ..., all dimensions but the last counted through in order) at most 16 rows name the same one
- gate_up: bfloat16 [64, 704, 2, 1024], P('exp', 'ctx'), may hold values from -0.1875 to 0.1875
- w_down: bfloat16 [64, 704, 1024], P('exp', 'ctx'), may hold values from -0.21875 to 0.21875
Outputs:
- attn_context: bfloat16 [8, 512, 4096], P(('group', 'exp'), 'ctx'), parts along dimension 0
- expert_mix: bfloat16 [8, 512, 1024], P(('group', 'exp'), 'ctx'), parts along dimension 0
- balance: float32 [8, 8], P(('group', 'exp')), parts along dimension 0
The draws below stay inside these ranges and needn't reach their ends.
There are 2 independent parts, one for each index of `group`. The reference program is written for one: setup_inputs(seed, part) draws one part's arguments, and reference() takes and returns one part's arrays. A program takes and returns all parts, laid end to end along the dimension named above; an argument that names none is the same for every part. Nothing has to cross between parts.
Inputs may be any that keep to these rules, and one draw needn't show every extreme that they name: `doc_lengths`: the 8 lengths of a row add up to 512; in every row the longest is exactly 256. `expert_ids`: each position names 6 different experts; among the positions of one device no expert is named more than 16 times, a bound that some block reaches.
All inputs are finite; a program needn't handle non-finite values.
Results may differ from the reference program's by a relative error of at most 0.008.
Values may be sent and summed in bfloat16 or wider, within the bound.
No kernel may reach another device: no remote copies, remote signals or barrier semaphores. Data moves between devices by JAX's collectives and lax.ppermute only.
A program may use at most 256 MiB of HBM per device.

```python
import math
import jax
import jax.numpy as jnp
import numpy as np
from jax import lax

D = 1024
FF = 704
EXPERTS = 64
TOPK = 6
HEADS = 8
LATENT = 512
CAP = 16
NDOC = 8
TOK_DEV = 128
KDIM = 576
LEN = 512
ROWS = 4
DOC_MOST = 256
N_CTX = 4
N_EXP = 4


def draw_latent_kv(key, part):
    key = jax.random.fold_in(key, 3)
    drawn = jnp.clip(jax.random.normal(key, (ROWS, LEN, KDIM), jnp.float32), -6.0, 6.0)
    return drawn.astype(jnp.bfloat16)


def draw_queries(key, part):
    key = jax.random.fold_in(key, 5)
    drawn = jnp.clip(jax.random.normal(key, (ROWS, LEN, HEADS * KDIM), jnp.float32), -6.0, 6.0)
    return drawn.astype(jnp.bfloat16)


def levels(stream_key, extent, split, low, high):
    def one(position, blocks):
        draws = jax.random.uniform(jax.random.fold_in(jax.random.fold_in(stream_key, 6), position), (blocks,), jnp.float32, low / len(split), high / len(split))
        return jnp.repeat(jnp.exp(draws), extent[position] // blocks).reshape((-1,) + (1,) * (len(extent) - position - 1))

    factor_of = one(*split[0])
    for cut in split[1:]:
        factor_of = factor_of * one(*cut)
    return factor_of


def split_up(count, total, reach, slope):
    portions = [(1 << 20) // math.isqrt(standing ** slope) + 1 for standing in range(2, count + 1)]
    surplus, holding = total - reach - (count - 1), [1] * (count - 1)
    while surplus > 0:
        candidates = [i for i in range(count - 1) if holding[i] < reach]
        pool, left = sum([portions[i] for i in candidates]), surplus
        for i in candidates:
            addition = min(reach - holding[i], max(1, left * portions[i] // pool), surplus)
            holding[i] = holding[i] + addition
            surplus = surplus - addition
    return np.array([reach] + holding)


def uneven(rng, number_of, total, reach, lean):
    if number_of == 2:
        one = jax.random.randint(rng, (), max(1, total - reach), min(reach, total - 1) + 1)
        return jnp.stack([one, total - one])
    tallies = jnp.asarray(split_up(number_of, total, reach, lean), jnp.int32)
    pairs = (number_of - 1) // 2
    source_of, receiver = tallies[1:1 + 2 * pairs:2], tallies[2:2 + 2 * pairs:2]
    margin = jnp.minimum(source_of - 1, reach - receiver)
    moved = jax.random.randint(jax.random.fold_in(rng, 1), (pairs,), 0, 1 << 20) % (margin + 1)
    tallies = tallies.at[1:1 + 2 * pairs:2].set(source_of - moved).at[2:2 + 2 * pairs:2].set(receiver + moved)
    return tallies[jax.random.permutation(jax.random.fold_in(rng, 2), number_of)]


def deal_out(rng, own, number, rows, count, top, most, lean):
    order = jax.random.permutation(rng, count)
    heavy_load, ordinary = load_shares(count, rows * top, most, lean, True), load_shares(count, rows * top, most, lean, False)
    places = jnp.arange(count)

    def named(tallies, offset_by):
        used = int((tallies > 0).sum())
        fixed = max(1, used // 4)
        moved = fixed + (places - fixed + offset_by * (used - fixed)) % max(1, count - fixed)
        return jnp.zeros((count,), jnp.int32).at[order[jnp.where(places < fixed, places, moved)]].set(jnp.asarray(tallies, jnp.int32))

    tallies = jnp.where(number % 4 == 0, named(heavy_load, number // 4), named(ordinary, number - number // 4 - 1))
    mixed = jax.random.permutation(jax.random.fold_in(own, 3), count)
    donor, sink = mixed[0:count // 2 * 2:2], mixed[1:count // 2 * 2:2]
    slack = jnp.minimum(tallies[donor] - 1, most - tallies[sink]) // 2
    slack = jnp.where((donor == order[0]) | (sink == order[0]) | (tallies[sink] == 0), 0, jnp.maximum(slack, 0))
    moved = jax.random.randint(jax.random.fold_in(own, 4), (count // 2,), 0, 1 << 20) % (slack + 1)
    tallies = tallies.at[donor].add(-moved).at[sink].add(moved)
    members = jnp.searchsorted(jnp.cumsum(tallies), jnp.arange(rows * top), side="right").astype(jnp.int32)
    table = members.reshape(top, rows).T
    table = table[jax.random.permutation(jax.random.fold_in(own, 1), rows)]
    offset_by = jax.random.randint(jax.random.fold_in(own, 2), (rows, 1), 0, top)
    return jnp.take_along_axis(table, (jnp.arange(top)[None, :] + offset_by) % top, axis=1)


def load_shares(number_of, total, bound, lean, full):
    weights = [(1 << 20) // math.isqrt(grade ** lean) + 1 for grade in range(1, number_of + 1)]
    largest = bound if full else min(bound, max(-(-total // number_of), total * weights[0] // sum(weights)))
    least = 1 if total - largest >= number_of - 1 else 0
    holding, surplus = [largest] + [least] * (number_of - 1), total - largest - least * (number_of - 1)
    while surplus > 0:
        free = [i for i in range(1, number_of) if holding[i] < largest] or [i for i in range(1, number_of) if holding[i] < bound]
        whole, remaining = sum([weights[i] for i in free]), surplus
        for i in free:
            addition = min(bound - holding[i], max(1, remaining * weights[i] // whole), surplus)
            holding[i] = holding[i] + addition
            surplus = surplus - addition
    return np.array(holding)


def normal_values(own_key, dims, width, bound, split=(), kind=jnp.bfloat16):
    values = width * jax.random.normal(own_key, dims, jnp.float32)
    if split:
        values = values * levels(own_key, dims, split, -0.22, 0.18)
    return jnp.clip(values, -bound, bound).astype(kind)


def setup_inputs(seed: int = 0, part: int = 0) -> dict:
    arg_keys = jax.random.split(jax.random.key(seed), 9)
    part_keys = jax.random.split(jax.random.fold_in(arg_keys[8], part), 9)
    queries = draw_queries(jax.random.fold_in(jax.random.fold_in(arg_keys[8], part), 71), part)
    latent_kv = draw_latent_kv(jax.random.fold_in(jax.random.fold_in(arg_keys[8], part), 71), part)
    doc_lengths = jax.vmap(lambda own: uneven(own, NDOC, LEN, DOC_MOST, 2))(jax.random.split(part_keys[2], ROWS)).reshape((ROWS, NDOC)).astype(jnp.int32)
    hidden_in = normal_values(part_keys[3], (ROWS, LEN, D), 1.0, 6.0, ((0, 4), (1, 4)))
    router_weight = normal_values(arg_keys[4], (D, EXPERTS), D ** -0.5, 0.1875)
    expert_ids_keys = jax.random.split(jax.random.fold_in(part_keys[5], 1), ROWS * LEN // TOK_DEV)
    expert_ids_turns = jax.random.permutation(jax.random.fold_in(part_keys[5], 3), ROWS * LEN // TOK_DEV)
    expert_ids = jax.vmap(lambda own, number: deal_out(jax.random.fold_in(part_keys[5], 2), own, number, TOK_DEV, EXPERTS, TOPK, CAP, 2))(expert_ids_keys, expert_ids_turns).reshape((ROWS, LEN, TOPK))
    gate_up = normal_values(arg_keys[6], (EXPERTS, FF, 2, D), D ** -0.5, 0.1875, ((0, 4), (1, 4)))
    w_down = normal_values(arg_keys[7], (EXPERTS, FF, D), FF ** -0.5, 0.21875, ((0, 4), (1, 4)))
    return {"queries": queries, "latent_kv": latent_kv, "doc_lengths": doc_lengths, "hidden_in": hidden_in, "router_weight": router_weight, "expert_ids": expert_ids, "gate_up": gate_up, "w_down": w_down}


qk_scale = 192.0 ** -0.5


def segment_of(positions, lengths):
    ends = jnp.cumsum(lengths)
    return jnp.sum((positions[:, None] >= ends[None, :]).astype(jnp.int32), axis=1)


def attend_row(packed):
    queries_row, keys_row, lengths_row = packed
    length = keys_row.shape[0]
    positions = jnp.arange(length, dtype=jnp.int32)
    segs = segment_of(positions, lengths_row)
    allowed = (segs[:, None] == segs[None, :]) & (positions[None, :] <= positions[:, None])
    heads_q = queries_row.reshape(length, HEADS, KDIM)
    scores = jnp.einsum("thd,kd->htk", heads_q.astype(jnp.float32), keys_row.astype(jnp.float32)) * qk_scale
    scores = jnp.where(allowed[None], scores, -1e30)
    top = jnp.max(scores, axis=-1, keepdims=True)
    expo = jnp.exp(scores - top)
    weights = (expo / jnp.sum(expo, axis=-1, keepdims=True)).astype(jnp.bfloat16)
    values = keys_row[:, :LATENT]
    context = jnp.einsum("htk,kl->thl", weights.astype(jnp.float32), values.astype(jnp.float32))
    return context.astype(jnp.bfloat16).reshape(length, HEADS * LATENT)


def reference(queries, latent_kv, doc_lengths, hidden_in, router_weight, expert_ids, gate_up, w_down):
    attn_context = lax.map(attend_row, (queries, latent_kv, doc_lengths))
    tokens = hidden_in.reshape(-1, D)
    logits = jnp.dot(tokens, router_weight, preferred_element_type=jnp.float32)
    router = jax.nn.softmax(logits, axis=-1)
    ids = expert_ids.reshape(-1, TOPK)
    onehot = (ids[:, :, None] == jnp.arange(EXPERTS, dtype=jnp.int32)[None, None, :]).astype(jnp.float32)
    chosen = jnp.sum(onehot * router[:, None, :], axis=-1)
    gates = chosen / jnp.sum(chosen, axis=-1, keepdims=True)
    flat_ids = ids.reshape(-1)
    pairs = flat_ids.shape[0]
    most = N_EXP * N_CTX * CAP

    def one_expert(expert):
        index = jnp.nonzero(flat_ids == expert, size=most, fill_value=pairs)[0].astype(jnp.int32)
        rows = tokens[jnp.minimum(index, pairs - 1) // TOPK]
        both = jnp.einsum("sd,fzd->zsf", rows.astype(jnp.float32), gate_up[expert].astype(jnp.float32))
        inner = (jax.nn.silu(both[0]) * both[1]).astype(jnp.bfloat16)
        return jnp.dot(inner, w_down[expert], preferred_element_type=jnp.float32).astype(jnp.bfloat16), index

    outs, indices = lax.map(one_expert, jnp.arange(EXPERTS, dtype=jnp.int32))
    board = jnp.zeros((pairs + 1, D), jnp.bfloat16).at[indices.reshape(-1)].set(outs.reshape(-1, D))
    pair_out = board[:pairs].reshape(-1, TOPK, D)
    mix = jnp.zeros((tokens.shape[0], D), jnp.float32)
    for slot in range(TOPK):
        mix = mix + gates[:, slot, None] * pair_out[:, slot].astype(jnp.float32)
    expert_mix = mix.astype(jnp.bfloat16).reshape(ROWS, LEN, D)
    positions = jnp.arange(LEN, dtype=jnp.int32)
    segs = jax.vmap(lambda lengths_row: segment_of(positions, lengths_row))(doc_lengths)
    seg_hot = (segs[:, :, None] == jnp.arange(NDOC, dtype=jnp.int32)[None, None, :]).astype(jnp.float32)
    tok_exp = jnp.sum(onehot, axis=1).reshape(ROWS, LEN, EXPERTS)
    counts = jnp.einsum("rld,rle->rde", seg_hot, tok_exp, precision=lax.Precision.HIGHEST)
    mass = jnp.einsum("rld,rle->rde", seg_hot, router.reshape(ROWS, LEN, EXPERTS), precision=lax.Precision.HIGHEST)
    sizes_f = doc_lengths.astype(jnp.float32)[:, :, None]
    balance = jnp.sum((EXPERTS * counts / (TOPK * sizes_f)) * (mass / sizes_f), axis=-1)
    return attn_context, expert_mix, balance
```

```python
import functools

import jax
import jax.numpy as jnp
from jax import lax
from jax.experimental import pallas as pl
from jax.experimental.pallas import tpu as pltpu
from jax.sharding import PartitionSpec as P

EXPERTS = 64
HEADS = 8
LATENT = 512
CAP = 16
NDOC = 8
BLOCK = 128
LANES = 128
CHUNK_BLOCKS = 16
VMEM = 56 * 2**20

qk_scale = 192.0 ** (-0.5)


def moe_kernel(n_parts, with_balance, *refs):
    parts, refs = refs[:n_parts], refs[n_parts:]
    ids_ref, rw_ref, seg_ref, scale_ref, gate_ref, up_ref, down_ref = refs[:7]
    outs, refs = refs[7 : 7 + n_parts], refs[7 + n_parts :]
    bal_ref = refs[0]
    x, y, keys, gates, picks, rows, weight, made, in_sem, out_sem = refs[1:]
    chunk, e = pl.program_id(0), pl.program_id(1)
    n_exp = pl.num_programs(1)
    tokens = x.shape[0]
    blocks = tokens // BLOCK
    share = tokens // n_parts
    local = rows.shape[0]
    slots = local * CAP

    def part_of(ref):
        return ref.at[pl.ds(pl.multiple_of(chunk * share, share), share), :]

    @pl.when(e == 0)
    def _():
        copies = [
            pltpu.make_async_copy(
                part_of(parts[i]), x.at[pl.ds(i * share, share), :], in_sem.at[i]
            )
            for i in range(n_parts)
        ]
        for copy in copies:
            copy.start()
        for copy in copies:
            copy.wait()
        logits = lax.dot_general(
            rw_ref[...], x[...], (((1,), (1,)), ((), ())), preferred_element_type=jnp.float32
        )
        expo = jnp.exp(logits - jnp.max(logits, axis=0, keepdims=True))
        router = expo / jnp.sum(expo, axis=0, keepdims=True)
        names = lax.broadcasted_iota(jnp.int32, (EXPERTS, BLOCK), 0)
        before = (
            lax.broadcasted_iota(jnp.int32, (BLOCK, BLOCK), 0)
            < lax.broadcasted_iota(jnp.int32, (BLOCK, BLOCK), 1)
        ).astype(jnp.bfloat16)
        hots, probs = [], []
        for b in range(blocks):
            ids = ids_ref[b]
            hot = names == ids[0:1]
            for k in range(1, ids.shape[0]):
                hot = hot | (names == ids[k : k + 1])
            hot = hot.astype(jnp.float32)
            prob = router[:, b * BLOCK : (b + 1) * BLOCK]
            chosen = prob * hot
            total = jnp.sum(chosen, axis=0, keepdims=True)
            own = hot[:local]
            rank = jnp.dot(own.astype(jnp.bfloat16), before, preferred_element_type=jnp.float32)
            keys[b] = jnp.where(own > 0.0, rank, -1.0)
            gates[b] = chosen[:local] / total
            hots.append(hot)
            probs.append(prob)
        if with_balance:
            n_row = seg_ref.shape[0]
            for d in range(NDOC):
                counts = jnp.zeros((EXPERTS, BLOCK), jnp.float32)
                mass = jnp.zeros((EXPERTS, BLOCK), jnp.float32)
                for b in range(n_row):
                    inside = seg_ref[b] == d
                    counts = counts + jnp.where(inside, hots[b], 0.0)
                    mass = mass + jnp.where(inside, probs[b], 0.0)
                both = jnp.sum(counts, axis=1, keepdims=True) * jnp.sum(
                    mass, axis=1, keepdims=True
                )
                bal_ref[d : d + 1, :] = (
                    jnp.broadcast_to(jnp.sum(both, axis=0, keepdims=True), (1, LANES))
                    * scale_ref[d : d + 1, :]
                )
        else:
            bal_ref[...] = jnp.zeros_like(bal_ref)

        slot = lax.broadcasted_iota(jnp.int32, (local, CAP, BLOCK), 1).astype(jnp.float32)

        @pl.loop(0, blocks)
        def _(b):
            pick = (keys[b][:, None, :] == slot).astype(jnp.float32)
            gate = jnp.sum(pick * gates[b][:, None, :], axis=-1, keepdims=True)
            at = pl.ds(pl.multiple_of(b * CAP, CAP), CAP)
            weight[:, at, :] = jnp.broadcast_to(gate, (local, CAP, LANES))
            pick = pick.reshape(slots, BLOCK).astype(jnp.bfloat16)
            picks[b] = pick
            taken = jnp.dot(
                pick,
                x[pl.ds(pl.multiple_of(b * BLOCK, BLOCK), BLOCK), :],
                preferred_element_type=jnp.float32,
            )
            rows[:, at, :] = taken.astype(jnp.bfloat16).reshape(local, CAP, x.shape[1])

    held = rows[e]
    nt = (((1,), (1,)), ((), ()))
    g = lax.dot_general(held, gate_ref[0], nt, preferred_element_type=jnp.float32)
    u = lax.dot_general(held, up_ref[0], nt, preferred_element_type=jnp.float32)
    width = g.shape[1]
    w = jnp.concatenate([weight[e]] * pl.cdiv(width, LANES), axis=1)[:, :width]
    inner = (g * lax.logistic(g) * u * w).astype(jnp.bfloat16)
    made[e] = jnp.dot(inner, down_ref[0], preferred_element_type=jnp.float32).astype(jnp.bfloat16)

    @pl.when(e == n_exp - 1)
    def _():
        @pl.loop(0, blocks)
        def _(b):
            at = pl.ds(pl.multiple_of(b * CAP, CAP), CAP)
            mix = lax.dot_general(
                picks[b],
                made[:, at, :].reshape(slots, x.shape[1]),
                (((0,), (0,)), ((), ())),
                preferred_element_type=jnp.float32,
            )
            y[pl.ds(pl.multiple_of(b * BLOCK, BLOCK), BLOCK), :] = mix.astype(jnp.bfloat16)

        copies = [
            pltpu.make_async_copy(
                y.at[pl.ds(i * share, share), :], part_of(outs[i]), out_sem.at[i]
            )
            for i in range(n_parts)
        ]
        for copy in copies:
            copy.start()
        for copy in copies:
            copy.wait()


def moe(parts, ids, rw, seg, scale, gate, up, down, with_balance):
    n_parts = len(parts)
    part_rows, width = parts[0].shape
    local, hidden, _ = gate.shape
    share = min(part_rows, max(CHUNK_BLOCKS // n_parts, 1) * BLOCK)
    chunks = part_rows // share
    tokens = n_parts * share
    blocks = tokens // BLOCK
    anywhere = pl.BlockSpec(memory_space=pl.ANY)

    def whole(a):
        return pl.BlockSpec(a.shape, lambda c, e: (0,) * a.ndim)

    def expert(a):
        return pl.BlockSpec((1,) + a.shape[1:], lambda c, e: (e, 0, 0))

    rounds = chunks * local
    flops = 2 * rounds * blocks * CAP * width * (3 * hidden + 2 * BLOCK)
    moved = 6 * local * hidden * width + 4 * chunks * tokens * width
    result = pl.pallas_call(
        functools.partial(moe_kernel, n_parts, with_balance),
        grid=(chunks, local),
        in_specs=[anywhere] * n_parts
        + [
            pl.BlockSpec((blocks,) + ids.shape[1:], lambda c, e: (c, 0, 0)),
            whole(rw),
            whole(seg),
            whole(scale),
            expert(gate),
            expert(up),
            expert(down),
        ],
        out_specs=[anywhere] * n_parts + [pl.BlockSpec((NDOC, LANES), lambda c, e: (0, 0))],
        out_shape=[jax.ShapeDtypeStruct(p.shape, jnp.bfloat16) for p in parts]
        + [jax.ShapeDtypeStruct((NDOC, LANES), jnp.float32)],
        scratch_shapes=[
            pltpu.VMEM((tokens, width), jnp.bfloat16),
            pltpu.VMEM((tokens, width), jnp.bfloat16),
            pltpu.VMEM((blocks, local, BLOCK), jnp.float32),
            pltpu.VMEM((blocks, local, BLOCK), jnp.float32),
            pltpu.VMEM((blocks, local * CAP, BLOCK), jnp.bfloat16),
            pltpu.VMEM((local, blocks * CAP, width), jnp.bfloat16),
            pltpu.VMEM((local, blocks * CAP, LANES), jnp.float32),
            pltpu.VMEM((local, blocks * CAP, width), jnp.bfloat16),
            pltpu.SemaphoreType.DMA((n_parts,)),
            pltpu.SemaphoreType.DMA((n_parts,)),
        ],
        compiler_params=pltpu.CompilerParams(
            dimension_semantics=("arbitrary", "arbitrary"), vmem_limit_bytes=VMEM
        ),
        cost_estimate=pl.CostEstimate(flops=flops, bytes_accessed=moved, transcendentals=0),
        name="experts",
    )(*parts, ids, rw, seg, scale, gate, up, down)
    return list(result[:n_parts]), result[n_parts]


def attend_kernel(first_ref, last_ref, q_ref, kv_ref, out_ref, even, odd):
    length, kdim = kv_ref.shape
    wide = even.shape[1]
    half = wide - kdim

    @pl.when(pl.program_id(0) == 0)
    def _():
        pad = jnp.zeros((length, half), jnp.bfloat16)
        even[...] = jnp.concatenate([kv_ref[...], pad], axis=1)
        odd[...] = jnp.concatenate([pad, kv_ref[...]], axis=1)

    rows = q_ref.shape[0]
    kpos = lax.broadcasted_iota(jnp.int32, (rows, length), 1)
    allowed = (kpos >= first_ref[...]) & (kpos <= last_ref[...])
    for i, keys in enumerate((even, odd)):
        at = i * (kdim - half)
        scores = lax.dot_general(
            q_ref[:, at : at + wide],
            keys[...],
            (((1,), (1,)), ((), ())),
            preferred_element_type=jnp.float32,
        )
        scores = jnp.where(allowed, scores * qk_scale, -1e30)
        expo = jnp.exp(scores - jnp.max(scores, axis=-1, keepdims=True))
        probs = (expo / jnp.sum(expo, axis=-1, keepdims=True)).astype(jnp.bfloat16)
        out_ref[:, i * LATENT : (i + 1) * LATENT] = jnp.dot(
            probs, kv_ref[:, :LATENT], preferred_element_type=jnp.float32
        ).astype(jnp.bfloat16)


def attend(queries, kv, first, last):
    rows = queries.shape[0]
    length, kdim = kv.shape
    wide = -(-kdim // LANES) * LANES
    return pl.pallas_call(
        attend_kernel,
        grid=(HEADS // 2,),
        in_specs=[
            pl.BlockSpec((rows, 1), lambda h: (0, 0)),
            pl.BlockSpec((rows, 1), lambda h: (0, 0)),
            pl.BlockSpec((rows, 2 * kdim), lambda h: (0, h)),
            pl.BlockSpec((length, kdim), lambda h: (0, 0)),
        ],
        out_specs=pl.BlockSpec((rows, 2 * LATENT), lambda h: (0, h)),
        out_shape=jax.ShapeDtypeStruct((rows, HEADS * LATENT), jnp.bfloat16),
        scratch_shapes=[pltpu.VMEM((length, wide), jnp.bfloat16)] * 2,
        compiler_params=pltpu.CompilerParams(
            dimension_semantics=("arbitrary",), vmem_limit_bytes=VMEM // 2
        ),
        cost_estimate=pl.CostEstimate(
            flops=2 * HEADS * rows * length * (wide + LATENT),
            bytes_accessed=2 * rows * HEADS * (kdim + LATENT),
            transcendentals=HEADS * rows * length,
        ),
        name="attention",
    )(first, last, queries, kv)


def add(a, b):
    return (a.astype(jnp.float32) + b.astype(jnp.float32)).astype(jnp.bfloat16)


def shards(queries, latent_kv, doc_lengths, hidden_in, router_weight, expert_ids, gate_up, w_down):
    tok_rows = hidden_in.shape[1]
    n_ctx, n_exp = lax.axis_size("ctx"), lax.axis_size("exp")
    ctx, exp = lax.axis_index("ctx"), lax.axis_index("exp")
    local = gate_up.shape[0]
    flips = [1 << i for i in range(n_ctx.bit_length() - 1)]
    shifts = range(n_exp) if n_exp <= 4 else (0,)
    tokens = hidden_in[0]

    def flip(a, bit):
        return lax.ppermute(a, "ctx", [(i, i ^ bit) for i in range(n_ctx)])

    def shift(a, d):
        return lax.ppermute(a, "exp", [(i, (i + d) % n_exp) for i in range(n_exp)])

    if n_exp <= 4:
        spread = [[tokens if d == 0 else shift(tokens, d)] for d in shifts]
    else:
        spread = [[lax.all_gather(tokens, "exp", axis=0, tiled=True)]]
    for bit in reversed(flips):
        spread = [held + [flip(a, bit) for a in held] for held in spread]
    masks = [0]
    for bit in reversed(flips):
        masks = masks + [m ^ bit for m in masks]

    picks = jnp.swapaxes(expert_ids[0].reshape(tok_rows // BLOCK, BLOCK, -1), 1, 2)
    all_picks = lax.all_gather(picks, ("exp", "ctx"), axis=0, tiled=False)
    all_picks = jnp.mod(all_picks - exp * local, EXPERTS)
    all_picks = all_picks.reshape((n_exp, n_ctx) + picks.shape)
    order = jnp.stack([ctx ^ m for m in masks])
    all_picks = jnp.take(all_picks, order, axis=1)

    lengths = doc_lengths[0]
    ends = jnp.cumsum(lengths)
    row_pos = (order[:, None] * tok_rows + jnp.arange(tok_rows, dtype=jnp.int32)[None, :]).reshape(
        -1, 1, BLOCK
    )
    seg = jnp.sum((row_pos[..., None] >= ends).astype(jnp.int32), axis=-1)
    sizes = lengths.astype(jnp.float32)
    scale = jnp.broadcast_to((EXPERTS / (expert_ids.shape[2] * sizes * sizes))[:, None], (NDOC, LANES))

    rw = jnp.roll(router_weight.T, -exp * local, axis=0)
    gate, up = gate_up[:, :, 0, :], gate_up[:, :, 1, :]
    if n_exp <= 4:
        back = jnp.stack([jnp.mod(exp - d, n_exp) for d in shifts])
        ids = jnp.take(all_picks, back, axis=0).reshape(-1, picks.shape[1], BLOCK)
        flat = [a for held in spread for a in held]
        made, balance = moe(flat, ids, rw, seg, scale, gate, up, w_down, True)
        made = [made[i * n_ctx : (i + 1) * n_ctx] for i in range(n_exp)]
    else:
        made = []
        for i, a in enumerate(spread[0]):
            ids = all_picks[:, i].reshape(-1, picks.shape[1], BLOCK)
            made.append(moe([a], ids, rw, seg, scale, gate, up, w_down, False)[0][0])
        made = [made]
        balance = None

    for bit in flips:
        half = len(made[0]) // 2
        made = [[add(h[i], flip(h[half + i], bit)) for i in range(half)] for h in made]
    if n_exp <= 4:
        total = made[0][0].astype(jnp.float32)
        for d in shifts[1:]:
            total = total + shift(made[d][0], -d).astype(jnp.float32)
        expert_mix = total.astype(jnp.bfloat16)
    else:
        expert_mix = lax.psum_scatter(made[0][0], "exp", scatter_dimension=0, tiled=True)

    kv = lax.all_gather(latent_kv[0], "ctx", axis=0, tiled=True)
    pos = ctx * tok_rows + jnp.arange(tok_rows, dtype=jnp.int32)
    passed = pos[:, None] >= ends[None, :]
    first = jnp.max(jnp.where(passed, ends[None, :], 0), axis=1)
    context = attend(queries[0], kv, first[:, None], pos[:, None])

    if balance is None:
        row = lax.all_gather(tokens, "ctx", axis=0, tiled=True)
        router = jax.nn.softmax(
            jnp.dot(row, router_weight, preferred_element_type=jnp.float32), axis=-1
        )
        row_ids = lax.all_gather(expert_ids[0], "ctx", axis=0, tiled=True)
        hot = (row_ids[:, :, None] == jnp.arange(EXPERTS, dtype=jnp.int32)).astype(jnp.float32)
        at = jnp.arange(row.shape[0], dtype=jnp.int32)
        seg_at = jnp.sum((at[:, None] >= ends[None, :]).astype(jnp.int32), axis=1)
        seg_hot = (seg_at[:, None] == jnp.arange(NDOC, dtype=jnp.int32)).astype(jnp.float32)
        exact = lax.Precision.HIGHEST
        counts = jnp.dot(seg_hot.T, hot.sum(axis=1), precision=exact)
        mass = jnp.dot(seg_hot.T, router, precision=exact)
        per_doc = jnp.sum(counts * mass, axis=1) * scale[:, 0]
    else:
        per_doc = balance[:, 0]
    return context[None], expert_mix[None], per_doc.reshape(1, NDOC)


def solution(mesh):
    rows = P(("group", "exp"), "ctx", None)
    docs = P(("group", "exp"), None)
    return jax.shard_map(
        shards,
        mesh=mesh,
        in_specs=(rows, rows, docs, rows, P(), rows, P("exp", "ctx", None, None), P("exp", "ctx", None)),
        out_specs=(rows, rows, docs),
        check_vma=False,
    )
```

```python
import functools

import jax
import jax.numpy as jnp
from jax import lax
from jax.experimental import pallas as pl
from jax.experimental.pallas import tpu as pltpu
from jax.sharding import PartitionSpec as P

EXPERTS = 64
HEADS = 8
LATENT = 512
CAP = 16
NDOC = 8
BLOCK = 128
LANES = 128
EXPERT_ROWS = 256
VMEM = 48 * 2**20
PEAK = 1.1e9

qk_scale = 192.0 ** (-0.5)
NT = (((1,), (1,)), ((), ()))
TN = (((0,), (0,)), ((), ()))


def call(kernel, micros, grid, in_specs, out_specs, out_shape, scratch, name):
    return pl.pallas_call(
        kernel,
        grid=grid,
        in_specs=in_specs,
        out_specs=out_specs,
        out_shape=out_shape,
        scratch_shapes=scratch,
        compiler_params=pltpu.CompilerParams(
            dimension_semantics=("arbitrary",) * len(grid), vmem_limit_bytes=VMEM
        ),
        cost_estimate=pl.CostEstimate(
            flops=int(micros * PEAK), bytes_accessed=0, transcendentals=0
        ),
        name=name,
    )


def dispatch_kernel(n_parts, n_row, base_ref, ids_ref, rw_ref, *refs):
    parts, refs = refs[:n_parts], refs[n_parts:]
    if n_row:
        seg_ref, scale_ref = refs[:2]
        refs = refs[2:]
    rows_ref, weight_ref, picks_ref = refs[:3]
    local = rows_ref.shape[0]
    width = rows_ref.shape[2]
    names = lax.broadcasted_iota(jnp.int32, (EXPERTS, BLOCK), 0)
    before = (
        lax.broadcasted_iota(jnp.int32, (BLOCK, BLOCK), 0)
        < lax.broadcasted_iota(jnp.int32, (BLOCK, BLOCK), 1)
    ).astype(jnp.bfloat16)
    slot = lax.broadcasted_iota(jnp.int32, (local, CAP, BLOCK), 1).astype(jnp.float32)
    hots, probs = [], []
    for p in range(n_parts):
        x = parts[p][...]
        logits = lax.dot_general(rw_ref[...], x, NT, preferred_element_type=jnp.float32)
        expo = jnp.exp(logits - jnp.max(logits, axis=0, keepdims=True))
        prob = expo / jnp.sum(expo, axis=0, keepdims=True)
        ids = ids_ref[p] - base_ref[0]
        ids = jnp.where(ids < 0, ids + EXPERTS, ids)
        hot = names == ids[0:1]
        for k in range(1, ids.shape[0]):
            hot = hot | (names == ids[k : k + 1])
        hot = hot.astype(jnp.float32)
        chosen = prob * hot
        gate = chosen[:local] / jnp.sum(chosen, axis=0, keepdims=True)
        own = hot[:local]
        rank = jnp.dot(own.astype(jnp.bfloat16), before, preferred_element_type=jnp.float32)
        key = jnp.where(own > 0.0, rank, -1.0)
        pick = (key[:, None, :] == slot).astype(jnp.float32)
        at = slice(p * CAP, (p + 1) * CAP)
        weight_ref[:, at, :] = jnp.broadcast_to(
            jnp.sum(pick * gate[:, None, :], axis=-1, keepdims=True), (local, CAP, LANES)
        )
        pick = pick.reshape(local * CAP, BLOCK).astype(jnp.bfloat16)
        picks_ref[p] = pick
        taken = jnp.dot(pick, x, preferred_element_type=jnp.float32)
        rows_ref[:, at, :] = taken.astype(jnp.bfloat16).reshape(local, CAP, width)
        hots.append(hot)
        probs.append(prob)
    if n_row:
        bal_ref = refs[3]
        for d in range(NDOC):
            counts = jnp.zeros((EXPERTS, BLOCK), jnp.float32)
            mass = jnp.zeros((EXPERTS, BLOCK), jnp.float32)
            for p in range(n_row):
                inside = seg_ref[p] == d
                counts = counts + jnp.where(inside, hots[p], 0.0)
                mass = mass + jnp.where(inside, probs[p], 0.0)
            both = jnp.sum(counts, axis=1, keepdims=True) * jnp.sum(mass, axis=1, keepdims=True)
            bal_ref[d : d + 1, :] = (
                jnp.broadcast_to(jnp.sum(both, axis=0, keepdims=True), (1, LANES))
                * scale_ref[d : d + 1, :]
            )


def whole(a):
    return pl.BlockSpec(a.shape, lambda *i: (0,) * a.ndim)


def dispatch(parts, ids, base, rw, local, row=None):
    n_parts = len(parts)
    n, width = parts[0].shape[0] // BLOCK, parts[0].shape[1]
    slots = n_parts * CAP
    in_specs = [
        pl.BlockSpec(memory_space=pltpu.SMEM),
        pl.BlockSpec((n_parts,) + ids.shape[1:], lambda i: (i, 0, 0)),
        whole(rw),
    ] + [pl.BlockSpec((BLOCK, width), lambda i: (i, 0))] * n_parts
    out_specs = [
        pl.BlockSpec((local, slots, width), lambda i: (0, i, 0)),
        pl.BlockSpec((local, slots, LANES), lambda i: (0, i, 0)),
        pl.BlockSpec((n_parts, local * CAP, BLOCK), lambda i: (i, 0, 0)),
    ]
    out_shape = [
        jax.ShapeDtypeStruct((local, n * slots, width), jnp.bfloat16),
        jax.ShapeDtypeStruct((local, n * slots, LANES), jnp.float32),
        jax.ShapeDtypeStruct((n * n_parts, local * CAP, BLOCK), jnp.bfloat16),
    ]
    extra = ()
    if row is not None:
        extra = row
        in_specs += [whole(a) for a in row]
        out_specs.append(pl.BlockSpec((NDOC, LANES), lambda i: (0, 0)))
        out_shape.append(jax.ShapeDtypeStruct((NDOC, LANES), jnp.float32))
    return call(
        functools.partial(dispatch_kernel, n_parts, n_parts if row is not None else 0),
        3 * n,
        (n,),
        in_specs,
        out_specs,
        out_shape,
        [],
        "dispatch",
    )(base, ids, rw, *parts, *extra)


def expert_kernel(n, *refs):
    rows, weights = refs[:n], refs[n : 2 * n]
    gu_ref, down_ref = refs[2 * n : 2 * n + 2]
    outs = refs[2 * n + 2 : 3 * n + 2]
    both = refs[3 * n + 2]
    held = jnp.concatenate([r[0] for r in rows], axis=0)
    hidden = lax.dot_general(gu_ref[0], held, NT, preferred_element_type=jnp.float32)
    half = both.shape[1] // 2
    inner = []
    for c in range(both.shape[0]):
        both[c] = hidden[:, c * LANES : (c + 1) * LANES]
        g = both[c, pl.ds(0, half, stride=2), :]
        u = both[c, pl.ds(1, half, stride=2), :]
        inner.append((g * lax.logistic(g) * u).astype(jnp.bfloat16))
    inner = jnp.concatenate(inner, axis=1)
    made = lax.dot_general(inner, down_ref[0], TN, preferred_element_type=jnp.float32)
    size = rows[0].shape[1]
    for i in range(n):
        w = weights[i][0]
        part = made[i * size : (i + 1) * size]
        for c in range(part.shape[1] // LANES):
            at = slice(c * LANES, (c + 1) * LANES)
            outs[i][0, :, at] = (part[:, at] * w).astype(jnp.bfloat16)


def experts(rows, weights, gate_up, down):
    n = len(rows)
    local, slots, width = rows[0].shape
    size = min(slots, EXPERT_ROWS)
    hidden = down.shape[1]
    rows_spec = pl.BlockSpec((1, size, width), lambda e, i: (e, i, 0))
    weight_spec = pl.BlockSpec((1, size, LANES), lambda e, i: (e, i, 0))
    return call(
        functools.partial(expert_kernel, n),
        10,
        (local, slots // size),
        [rows_spec] * n
        + [weight_spec] * n
        + [
            pl.BlockSpec((1, 2 * hidden, width), lambda e, i: (e, 0, 0)),
            pl.BlockSpec((1, hidden, width), lambda e, i: (e, 0, 0)),
        ],
        [rows_spec] * n,
        [jax.ShapeDtypeStruct(r.shape, jnp.bfloat16) for r in rows],
        [pltpu.VMEM((n * size // LANES, 2 * hidden, LANES), jnp.float32)],
        "experts",
    )(*rows, *weights, gate_up, down)


def combine_kernel(groups, picks_ref, made_ref, *outs):
    local, _, width = made_ref.shape
    per = outs[0].shape[1] // BLOCK
    for p in range(picks_ref.shape[0]):
        held = made_ref[:, p * CAP : (p + 1) * CAP, :].reshape(local * CAP, width)
        mix = lax.dot_general(picks_ref[p], held, TN, preferred_element_type=jnp.float32)
        out, at = outs[p // per], p % per
        out[0, at * BLOCK : (at + 1) * BLOCK, :] = mix.astype(jnp.bfloat16)


def combine(picks, made, n_parts):
    n = picks.shape[0] // n_parts
    local, _, width = made.shape
    slots = n_parts * CAP
    half = n_parts // 2 * BLOCK
    out = pl.BlockSpec((1, half, width), lambda i: (i, 0, 0))
    return call(
        functools.partial(combine_kernel, 2),
        2 * n,
        (n,),
        [
            pl.BlockSpec((n_parts,) + picks.shape[1:], lambda i: (i, 0, 0)),
            pl.BlockSpec((local, slots, width), lambda i: (0, i, 0)),
        ],
        [out, out],
        [jax.ShapeDtypeStruct((n, half, width), jnp.bfloat16)] * 2,
        [],
        "combine",
    )(picks, made)


def attend_kernel(n, first_ref, last_ref, kpos_ref, q_ref, *refs):
    parts, (out_ref, even, odd) = refs[:n], refs[n:]
    rows, kdim = parts[0].shape
    wide = even.shape[1]
    half = wide - kdim

    @pl.when(pl.program_id(0) == 0)
    def _():
        pad = jnp.zeros((rows, half), jnp.bfloat16)
        for i in range(n):
            at = slice(i * rows, (i + 1) * rows)
            even[at, :] = jnp.concatenate([parts[i][...], pad], axis=1)
            odd[at, :] = jnp.concatenate([pad, parts[i][...]], axis=1)

    allowed = (kpos_ref[...] >= first_ref[...]) & (kpos_ref[...] <= last_ref[...])
    for i, keys in enumerate((even, odd)):
        at = i * (kdim - half)
        scores = lax.dot_general(
            q_ref[:, at : at + wide], keys[...], NT, preferred_element_type=jnp.float32
        )
        scores = jnp.where(allowed, scores * qk_scale, -1e30)
        expo = jnp.exp(scores - jnp.max(scores, axis=-1, keepdims=True))
        probs = (expo / jnp.sum(expo, axis=-1, keepdims=True)).astype(jnp.bfloat16)
        out_ref[:, i * LATENT : (i + 1) * LATENT] = jnp.dot(
            probs, even[:, :LATENT], preferred_element_type=jnp.float32
        ).astype(jnp.bfloat16)


def attend(queries, parts, first, last, kpos):
    n = len(parts)
    rows, kdim = parts[0].shape
    wide = -(-kdim // LANES) * LANES
    return call(
        functools.partial(attend_kernel, n),
        6,
        (HEADS // 2,),
        [whole(first), whole(last), whole(kpos)]
        + [pl.BlockSpec((rows, 2 * kdim), lambda h: (0, h))]
        + [whole(p) for p in parts],
        pl.BlockSpec((rows, 2 * LATENT), lambda h: (0, h)),
        jax.ShapeDtypeStruct((rows, HEADS * LATENT), jnp.bfloat16),
        [pltpu.VMEM((n * rows, wide), jnp.bfloat16)] * 2,
        "attention",
    )(first, last, kpos, queries, *parts)


def added(*terms):
    total = terms[0].astype(jnp.float32)
    for term in terms[1:]:
        total = total + term.astype(jnp.float32)
    return total.astype(jnp.bfloat16)


def shards(queries, latent_kv, doc_lengths, hidden_in, router_weight, expert_ids, gate_up, w_down):
    tok_rows, width = hidden_in.shape[1:]
    n_ctx, n_exp = lax.axis_size("ctx"), lax.axis_size("exp")
    ctx, exp = lax.axis_index("ctx"), lax.axis_index("exp")
    local = gate_up.shape[0]
    near = n_exp <= 4
    shifts = [0, 1, 3, 2][:n_exp] if near else [0]
    flips = (2, 1)
    tokens = hidden_in[0]

    def flip(a, bit):
        return lax.ppermute(a, "ctx", [(i, i ^ bit) for i in range(n_ctx)])

    def shift(a, d):
        return lax.ppermute(a, "exp", [(i, (i + d) % n_exp) for i in range(n_exp)])

    def along_exp(a):
        if near:
            return [a if d == 0 else shift(a, d) for d in shifts]
        return [lax.all_gather(a, "exp", axis=0, tiled=True)]

    masks = [0, 2, 1, 3]
    order = jnp.stack([ctx ^ m for m in masks])

    picks = jnp.swapaxes(expert_ids[0].reshape(tok_rows // BLOCK, BLOCK, -1), 1, 2)
    ids = jnp.stack(along_exp(picks))
    ids = jnp.stack([ids, flip(ids, 2)], axis=2)
    ids = jnp.concatenate([ids, flip(ids, 1)], axis=2)
    ids = ids.reshape((len(shifts), -1) + picks.shape[1:])

    spread = [[a] for a in along_exp(tokens)]
    spread = [held + [flip(a, 2) for a in held] for held in spread]
    spread = [held + [flip(a, 1) for a in held] for held in spread]
    kv = [latent_kv[0]]
    for bit in flips:
        kv = kv + [flip(a, bit) for a in kv]

    lengths = doc_lengths[0]
    ends = jnp.cumsum(lengths)
    row_pos = order[:, None] * tok_rows + jnp.arange(tok_rows, dtype=jnp.int32)[None, :]
    pos = row_pos[0]
    passed = pos[:, None] >= ends[None, :]
    first = jnp.max(jnp.where(passed, ends[None, :], 0), axis=1)
    context = attend(queries[0], kv, first[:, None], pos[:, None], row_pos.reshape(1, -1))

    seg = jnp.sum((row_pos[..., None] >= ends).astype(jnp.int32), axis=-1)
    sizes = lengths.astype(jnp.float32)
    scale = jnp.broadcast_to((EXPERTS / (expert_ids.shape[2] * sizes * sizes))[:, None], (NDOC, LANES))

    base = (exp * local).reshape(1).astype(jnp.int32)
    rw = jnp.roll(router_weight.T, -exp * local, axis=0)
    gu = gate_up.reshape(local, -1, width)
    balance = None
    sent = []
    for i, held in enumerate(spread):
        row = (seg.reshape(-1, 1, BLOCK), scale) if near and i == 0 else None
        out = dispatch(held, ids[i], base, rw, local, row)
        sent.append(out[:3])
        if row is not None:
            balance = out[3]
    made = experts([s[0] for s in sent], [s[1] for s in sent], gu, w_down)

    back = []
    for i in reversed(range(len(shifts))):
        keep, give = combine(sent[i][2], made[i], n_ctx)
        got = flip(give, 1)
        far = added(keep[:, tok_rows:], got[:, tok_rows:])
        terms = [keep[:, :tok_rows], got[:, :tok_rows], flip(far, 2)]
        if i:
            back.append(shift(added(*terms), -shifts[i]))
        else:
            back = back + terms
    if near:
        expert_mix = added(*back)
    else:
        expert_mix = lax.psum_scatter(
            added(*back).reshape(-1, width), "exp", scatter_dimension=0, tiled=True
        ).reshape(1, tok_rows, width)

    if balance is None:
        row = lax.all_gather(tokens, "ctx", axis=0, tiled=True)
        router = jax.nn.softmax(
            jnp.dot(row, router_weight, preferred_element_type=jnp.float32), axis=-1
        )
        row_ids = lax.all_gather(expert_ids[0], "ctx", axis=0, tiled=True)
        hot = (row_ids[:, :, None] == jnp.arange(EXPERTS, dtype=jnp.int32)).astype(jnp.float32)
        at = jnp.arange(row.shape[0], dtype=jnp.int32)
        seg_at = jnp.sum((at[:, None] >= ends[None, :]).astype(jnp.int32), axis=1)
        seg_hot = (seg_at[:, None] == jnp.arange(NDOC, dtype=jnp.int32)).astype(jnp.float32)
        exact = lax.Precision.HIGHEST
        counts = jnp.dot(seg_hot.T, hot.sum(axis=1), precision=exact)
        mass = jnp.dot(seg_hot.T, router, precision=exact)
        per_doc = jnp.sum(counts * mass, axis=1) * scale[:, 0]
    else:
        per_doc = balance[:, 0]
    return context[None], expert_mix, per_doc.reshape(1, NDOC)


def solution(mesh):
    rows = P(("group", "exp"), "ctx", None)
    docs = P(("group", "exp"), None)
    return jax.shard_map(
        shards,
        mesh=mesh,
        in_specs=(rows, rows, docs, rows, P(), rows, P("exp", "ctx", None, None), P("exp", "ctx", None)),
        out_specs=(rows, rows, docs),
        check_vma=False,
    )
```

```python
import functools

import jax
import jax.numpy as jnp
from jax import lax
from jax.experimental import pallas as pl
from jax.experimental.pallas import tpu as pltpu
from jax.sharding import PartitionSpec as P

EXPERTS = 64
HEADS = 8
LATENT = 512
CAP = 16
NDOC = 8
BLOCK = 128
LANES = 128
EXPERT_ROWS = 256
EXTRA = 16
VMEM = 20 * 2**20
PEAK = 1.1e9

qk_scale = 192.0 ** (-0.5)
NT = (((1,), (1,)), ((), ()))
TN = (((0,), (0,)), ((), ()))


def call(kernel, micros, grid, in_specs, out_specs, out_shape, scratch, name):
    return pl.pallas_call(
        kernel,
        grid=grid,
        in_specs=in_specs,
        out_specs=out_specs,
        out_shape=out_shape,
        scratch_shapes=scratch,
        compiler_params=pltpu.CompilerParams(
            dimension_semantics=("arbitrary",) * len(grid), vmem_limit_bytes=VMEM
        ),
        cost_estimate=pl.CostEstimate(
            flops=int(micros * PEAK), bytes_accessed=0, transcendentals=0
        ),
        name=name,
    )


def dispatch_kernel(n_parts, n_row, top, base_ref, rw_ref, *refs):
    parts, refs = refs[:n_parts], refs[n_parts:]
    if n_row:
        seg_ref, scale_ref = refs[:2]
        refs = refs[2:]
    rows_ref, weight_ref, picks_ref = refs[:3]
    local = rows_ref.shape[0]
    width = rows_ref.shape[2]
    names = lax.broadcasted_iota(jnp.int32, (EXPERTS, BLOCK), 0).astype(jnp.float32)
    base = base_ref[0].astype(jnp.float32)
    before = (
        lax.broadcasted_iota(jnp.int32, (BLOCK, BLOCK), 0)
        < lax.broadcasted_iota(jnp.int32, (BLOCK, BLOCK), 1)
    ).astype(jnp.bfloat16)
    slot = lax.broadcasted_iota(jnp.int32, (local, CAP, BLOCK), 1).astype(jnp.float32)
    hots, probs = [], []
    for p in range(n_parts):
        x = parts[p][:BLOCK, :]
        ids = parts[p][BLOCK : BLOCK + EXTRA, :].astype(jnp.float32)[0:1] - base
        ids = jnp.where(ids < 0.0, ids + EXPERTS, ids)
        logits = lax.dot_general(rw_ref[...], x, NT, preferred_element_type=jnp.float32)
        expo = jnp.exp(logits - jnp.max(logits, axis=0, keepdims=True))
        prob = expo / jnp.sum(expo, axis=0, keepdims=True)
        hot = names == ids[:, :BLOCK]
        for k in range(1, top):
            hot = hot | (names == ids[:, k * BLOCK : (k + 1) * BLOCK])
        hot = hot.astype(jnp.float32)
        chosen = prob * hot
        gate = chosen[:local] / jnp.sum(chosen, axis=0, keepdims=True)
        own = hot[:local]
        rank = jnp.dot(own.astype(jnp.bfloat16), before, preferred_element_type=jnp.float32)
        key = jnp.where(own > 0.0, rank, -1.0)
        pick = (key[:, None, :] == slot).astype(jnp.float32)
        at = slice(p * CAP, (p + 1) * CAP)
        weight_ref[:, at, :] = jnp.broadcast_to(
            jnp.sum(pick * gate[:, None, :], axis=-1, keepdims=True), (local, CAP, LANES)
        )
        pick = pick.reshape(local * CAP, BLOCK).astype(jnp.bfloat16)
        picks_ref[p] = pick
        taken = jnp.dot(pick, x, preferred_element_type=jnp.float32)
        rows_ref[:, at, :] = taken.astype(jnp.bfloat16).reshape(local, CAP, width)
        hots.append(hot)
        probs.append(prob)
    if n_row:
        bal_ref = refs[3]
        for d in range(NDOC):
            counts = jnp.zeros((EXPERTS, BLOCK), jnp.float32)
            mass = jnp.zeros((EXPERTS, BLOCK), jnp.float32)
            for p in range(n_row):
                inside = seg_ref[p] == d
                counts = counts + jnp.where(inside, hots[p], 0.0)
                mass = mass + jnp.where(inside, probs[p], 0.0)
            both = jnp.sum(counts, axis=1, keepdims=True) * jnp.sum(mass, axis=1, keepdims=True)
            bal_ref[d : d + 1, :] = (
                jnp.broadcast_to(jnp.sum(both, axis=0, keepdims=True), (1, LANES))
                * scale_ref[d : d + 1, :]
            )


def whole(a):
    return pl.BlockSpec(a.shape, lambda *i: (0,) * a.ndim)


def dispatch(parts, top, base, rw, local, row=None):
    n_parts = len(parts)
    n, width = parts[0].shape[0] // (BLOCK + EXTRA), parts[0].shape[1]
    slots = n_parts * CAP
    in_specs = [
        pl.BlockSpec(memory_space=pltpu.SMEM),
        whole(rw),
    ] + [pl.BlockSpec((BLOCK + EXTRA, width), lambda i: (i, 0))] * n_parts
    out_specs = [
        pl.BlockSpec((local, slots, width), lambda i: (0, i, 0)),
        pl.BlockSpec((local, slots, LANES), lambda i: (0, i, 0)),
        pl.BlockSpec((n_parts, local * CAP, BLOCK), lambda i: (i, 0, 0)),
    ]
    out_shape = [
        jax.ShapeDtypeStruct((local, n * slots, width), jnp.bfloat16),
        jax.ShapeDtypeStruct((local, n * slots, LANES), jnp.float32),
        jax.ShapeDtypeStruct((n * n_parts, local * CAP, BLOCK), jnp.bfloat16),
    ]
    extra = ()
    if row is not None:
        extra = row
        in_specs += [whole(a) for a in row]
        out_specs.append(pl.BlockSpec((NDOC, LANES), lambda i: (0, 0)))
        out_shape.append(jax.ShapeDtypeStruct((NDOC, LANES), jnp.float32))
    return call(
        functools.partial(dispatch_kernel, n_parts, n_parts if row is not None else 0, top),
        3 * n,
        (n,),
        in_specs,
        out_specs,
        out_shape,
        [],
        "dispatch",
    )(base, rw, *parts, *extra)


def expert_kernel(n, *refs):
    rows, weights = refs[:n], refs[n : 2 * n]
    gu_ref, down_ref = refs[2 * n : 2 * n + 2]
    outs, wide = refs[2 * n + 2 : 3 * n + 2], refs[3 * n + 2]
    group, hidden, width = down_ref.shape
    size = rows[0].shape[1]
    chunks = width // LANES
    for e in range(group):
        wide[e] = gu_ref[e].astype(jnp.float32)
        gu = jnp.concatenate(
            [
                jnp.concatenate(
                    [
                        wide[e, pl.ds(2 * c + z, hidden, stride=2 * chunks), :].astype(jnp.bfloat16)
                        for c in range(chunks)
                    ],
                    axis=1,
                )
                for z in range(2)
            ],
            axis=0,
        )
        held = jnp.concatenate([r[e] for r in rows], axis=0)
        both = lax.dot_general(gu, held, NT, preferred_element_type=jnp.float32)
        g, u = both[:hidden], both[hidden:]
        inner = (g * lax.logistic(g) * u).astype(jnp.bfloat16)
        made = lax.dot_general(inner, down_ref[e], TN, preferred_element_type=jnp.float32)
        for i in range(n):
            w = weights[i][e]
            part = made[i * size : (i + 1) * size]
            for c in range(chunks):
                at = slice(c * LANES, (c + 1) * LANES)
                outs[i][e, :, at] = (part[:, at] * w).astype(jnp.bfloat16)


def experts(rows, weights, gate_up, down):
    n = len(rows)
    local, slots, width = rows[0].shape
    size = min(slots, EXPERT_ROWS)
    hidden = down.shape[1]
    group = 2 if local % 2 == 0 else 1
    chunks = width // LANES
    gu = gate_up.reshape(local, hidden, 2, chunks, LANES).swapaxes(2, 3)
    gu = gu.reshape(local, hidden * 2 * chunks, LANES)
    rows_spec = pl.BlockSpec((group, size, width), lambda e, i: (e, i, 0))
    weight_spec = pl.BlockSpec((group, size, LANES), lambda e, i: (e, i, 0))
    return call(
        functools.partial(expert_kernel, n),
        10,
        (local // group, slots // size),
        [rows_spec] * n
        + [weight_spec] * n
        + [
            pl.BlockSpec((group,) + gu.shape[1:], lambda e, i: (e, 0, 0)),
            pl.BlockSpec((group, hidden, width), lambda e, i: (e, 0, 0)),
        ],
        [rows_spec] * n,
        [jax.ShapeDtypeStruct(r.shape, jnp.bfloat16) for r in rows],
        [pltpu.VMEM((group,) + gu.shape[1:], jnp.float32)],
        "experts",
    )(*rows, *weights, gu, down)


def combine_kernel(groups, picks_ref, made_ref, *outs):
    local, _, width = made_ref.shape
    per = outs[0].shape[1] // BLOCK
    for p in range(picks_ref.shape[0]):
        held = made_ref[:, p * CAP : (p + 1) * CAP, :].reshape(local * CAP, width)
        mix = lax.dot_general(picks_ref[p], held, TN, preferred_element_type=jnp.float32)
        out, at = outs[p // per], p % per
        out[0, at * BLOCK : (at + 1) * BLOCK, :] = mix.astype(jnp.bfloat16)


def combine(picks, made, n_parts):
    n = picks.shape[0] // n_parts
    local, _, width = made.shape
    slots = n_parts * CAP
    half = n_parts // 2 * BLOCK
    out = pl.BlockSpec((1, half, width), lambda i: (i, 0, 0))
    return call(
        functools.partial(combine_kernel, 2),
        2 * n,
        (n,),
        [
            pl.BlockSpec((n_parts,) + picks.shape[1:], lambda i: (i, 0, 0)),
            pl.BlockSpec((local, slots, width), lambda i: (0, i, 0)),
        ],
        [out, out],
        [jax.ShapeDtypeStruct((n, half, width), jnp.bfloat16)] * 2,
        [],
        "combine",
    )(picks, made)


def attend_kernel(n, first_ref, last_ref, kpos_ref, q_ref, *refs):
    parts, (out_ref, even, odd) = refs[:n], refs[n:]
    rows, kdim = parts[0].shape
    wide = even.shape[1]
    half = wide - kdim

    @pl.when(pl.program_id(0) == 0)
    def _():
        pad = jnp.zeros((rows, half), jnp.bfloat16)
        for i in range(n):
            at = slice(i * rows, (i + 1) * rows)
            even[at, :] = jnp.concatenate([parts[i][...], pad], axis=1)
            odd[at, :] = jnp.concatenate([pad, parts[i][...]], axis=1)

    allowed = (kpos_ref[...] >= first_ref[...]) & (kpos_ref[...] <= last_ref[...])
    for i, keys in enumerate((even, odd)):
        at = i * (kdim - half)
        scores = lax.dot_general(
            q_ref[:, at : at + wide], keys[...], NT, preferred_element_type=jnp.float32
        )
        scores = jnp.where(allowed, scores * qk_scale, -1e30)
        expo = jnp.exp(scores - jnp.max(scores, axis=-1, keepdims=True))
        probs = (expo / jnp.sum(expo, axis=-1, keepdims=True)).astype(jnp.bfloat16)
        out_ref[:, i * LATENT : (i + 1) * LATENT] = jnp.dot(
            probs, even[:, :LATENT], preferred_element_type=jnp.float32
        ).astype(jnp.bfloat16)


def attend(queries, parts, first, last, kpos):
    n = len(parts)
    rows, kdim = parts[0].shape
    wide = -(-kdim // LANES) * LANES
    return call(
        functools.partial(attend_kernel, n),
        6,
        (HEADS // 2,),
        [whole(first), whole(last), whole(kpos)]
        + [pl.BlockSpec((rows, 2 * kdim), lambda h: (0, h))]
        + [whole(p) for p in parts],
        pl.BlockSpec((rows, 2 * LATENT), lambda h: (0, h)),
        jax.ShapeDtypeStruct((rows, HEADS * LATENT), jnp.bfloat16),
        [pltpu.VMEM((n * rows, wide), jnp.bfloat16)] * 2,
        "attention",
    )(first, last, kpos, queries, *parts)


def added(*terms):
    total = terms[0].astype(jnp.float32)
    for term in terms[1:]:
        total = total + term.astype(jnp.float32)
    return total.astype(jnp.bfloat16)


def shards(queries, latent_kv, doc_lengths, hidden_in, router_weight, expert_ids, gate_up, w_down):
    tok_rows, width = hidden_in.shape[1:]
    n_ctx, n_exp = lax.axis_size("ctx"), lax.axis_size("exp")
    ctx, exp = lax.axis_index("ctx"), lax.axis_index("exp")
    local = gate_up.shape[0]
    near = n_exp <= 4
    shifts = [0, 1, 3, 2][:n_exp] if near else [0]
    flips = (2, 1)
    tokens = hidden_in[0]

    def flip(a, bit):
        return lax.ppermute(a, "ctx", [(i, i ^ bit) for i in range(n_ctx)])

    def shift(a, d):
        return lax.ppermute(a, "exp", [(i, (i + d) % n_exp) for i in range(n_exp)])

    def along_exp(a):
        if near:
            return [a if d == 0 else shift(a, d) for d in shifts]
        return [lax.all_gather(a, "exp", axis=0, tiled=True)]

    masks = [0, 2, 1, 3]
    order = jnp.stack([ctx ^ m for m in masks])

    top = expert_ids.shape[2]
    picks = expert_ids[0].T.astype(jnp.bfloat16).reshape(1, top * tok_rows)
    picks = jnp.pad(picks, ((0, EXTRA - 1), (0, width - top * tok_rows)))
    packed = jnp.concatenate([tokens, picks], axis=0)

    near_parts = along_exp(packed)
    spread = [[a] for a in near_parts]
    spread = [held + [flip(a, 2) for a in held] for held in spread]
    spread = [held + [flip(a, 1) for a in held] for held in spread]
    kv = [latent_kv[0]]
    for bit in flips:
        kv = kv + [flip(a, bit) for a in kv]

    lengths = doc_lengths[0]
    ends = jnp.cumsum(lengths)
    row_pos = order[:, None] * tok_rows + jnp.arange(tok_rows, dtype=jnp.int32)[None, :]
    pos = row_pos[0]
    passed = pos[:, None] >= ends[None, :]
    first = jnp.max(jnp.where(passed, ends[None, :], 0), axis=1)
    context = attend(queries[0], kv, first[:, None], pos[:, None], row_pos.reshape(1, -1))

    seg = jnp.sum((row_pos[..., None] >= ends).astype(jnp.int32), axis=-1)
    sizes = lengths.astype(jnp.float32)
    scale = jnp.broadcast_to((EXPERTS / (top * sizes * sizes))[:, None], (NDOC, LANES))

    base = (exp * local).reshape(1).astype(jnp.int32)
    rw = jnp.roll(router_weight.T, -exp * local, axis=0)
    balance = None
    sent = []
    for i, held in enumerate(spread):
        row = (seg.reshape(-1, 1, BLOCK), scale) if near and i == 0 else None
        out = dispatch(held, top, base, rw, local, row)
        sent.append(out[:3])
        if row is not None:
            balance = out[3]
    made = experts([s[0] for s in sent], [s[1] for s in sent], gate_up, w_down)

    back = []
    for i in reversed(range(len(shifts))):
        keep, give = combine(sent[i][2], made[i], n_ctx)
        got = flip(give, 1)
        far = added(keep[:, tok_rows:], got[:, tok_rows:])
        terms = [keep[:, :tok_rows], got[:, :tok_rows], flip(far, 2)]
        if i:
            back.append(shift(added(*terms), -shifts[i]))
        else:
            back = back + terms
    if near:
        expert_mix = added(*back)
    else:
        expert_mix = lax.psum_scatter(
            added(*back).reshape(-1, width), "exp", scatter_dimension=0, tiled=True
        ).reshape(1, tok_rows, width)

    if balance is None:
        row = lax.all_gather(tokens, "ctx", axis=0, tiled=True)
        router = jax.nn.softmax(
            jnp.dot(row, router_weight, preferred_element_type=jnp.float32), axis=-1
        )
        row_ids = lax.all_gather(expert_ids[0], "ctx", axis=0, tiled=True)
        hot = (row_ids[:, :, None] == jnp.arange(EXPERTS, dtype=jnp.int32)).astype(jnp.float32)
        at = jnp.arange(row.shape[0], dtype=jnp.int32)
        seg_at = jnp.sum((at[:, None] >= ends[None, :]).astype(jnp.int32), axis=1)
        seg_hot = (seg_at[:, None] == jnp.arange(NDOC, dtype=jnp.int32)).astype(jnp.float32)
        exact = lax.Precision.HIGHEST
        counts = jnp.dot(seg_hot.T, hot.sum(axis=1), precision=exact)
        mass = jnp.dot(seg_hot.T, router, precision=exact)
        per_doc = jnp.sum(counts * mass, axis=1) * scale[:, 0]
    else:
        per_doc = balance[:, 0]
    return context[None], expert_mix, per_doc.reshape(1, NDOC)


def solution(mesh):
    rows = P(("group", "exp"), "ctx", None)
    docs = P(("group", "exp"), None)
    return jax.shard_map(
        shards,
        mesh=mesh,
        in_specs=(rows, rows, docs, rows, P(), rows, P("exp", "ctx", None, None), P("exp", "ctx", None)),
        out_specs=(rows, rows, docs),
        check_vma=False,
    )
```

```python
import functools

import jax
import jax.numpy as jnp
from jax import lax
from jax.experimental import pallas as pl
from jax.experimental.pallas import tpu as pltpu
from jax.sharding import PartitionSpec as P

EXPERTS = 64
HEADS = 8
LATENT = 512
CAP = 16
NDOC = 8
BLOCK = 128
LANES = 128
EXPERT_ROWS = 256
EXTRA = 16
VMEM = 20 * 2**20
PEAK = 1.1e9

qk_scale = 192.0 ** (-0.5)
NT = (((1,), (1,)), ((), ()))
TN = (((0,), (0,)), ((), ()))


def call(kernel, micros, grid, in_specs, out_specs, out_shape, scratch, name):
    return pl.pallas_call(
        kernel,
        grid=grid,
        in_specs=in_specs,
        out_specs=out_specs,
        out_shape=out_shape,
        scratch_shapes=scratch,
        compiler_params=pltpu.CompilerParams(
            dimension_semantics=("arbitrary",) * len(grid), vmem_limit_bytes=VMEM
        ),
        cost_estimate=pl.CostEstimate(
            flops=int(micros * PEAK), bytes_accessed=0, transcendentals=0
        ),
        name=name,
    )


def dispatch_kernel(n_parts, n_row, top, base_ref, rw_ref, *refs):
    parts, refs = refs[:n_parts], refs[n_parts:]
    if n_row:
        seg_ref, scale_ref = refs[:2]
        refs = refs[2:]
    rows_ref, weight_ref, picks_ref = refs[:3]
    local = rows_ref.shape[0]
    width = rows_ref.shape[2]
    names = lax.broadcasted_iota(jnp.int32, (EXPERTS, BLOCK), 0).astype(jnp.float32)
    base = base_ref[0].astype(jnp.float32)
    before = (
        lax.broadcasted_iota(jnp.int32, (BLOCK, BLOCK), 0)
        < lax.broadcasted_iota(jnp.int32, (BLOCK, BLOCK), 1)
    ).astype(jnp.bfloat16)
    slot = lax.broadcasted_iota(jnp.int32, (local, CAP, BLOCK), 1).astype(jnp.float32)
    hots, probs = [], []
    for p in range(n_parts):
        x = parts[p][:BLOCK, :]
        ids = parts[p][BLOCK : BLOCK + EXTRA, :].astype(jnp.float32)[0:1] - base
        ids = jnp.where(ids < 0.0, ids + EXPERTS, ids)
        logits = lax.dot_general(rw_ref[...], x, NT, preferred_element_type=jnp.float32)
        expo = jnp.exp(logits - jnp.max(logits, axis=0, keepdims=True))
        prob = expo / jnp.sum(expo, axis=0, keepdims=True)
        hot = names == ids[:, :BLOCK]
        for k in range(1, top):
            hot = hot | (names == ids[:, k * BLOCK : (k + 1) * BLOCK])
        hot = hot.astype(jnp.float32)
        chosen = prob * hot
        gate = chosen[:local] / jnp.sum(chosen, axis=0, keepdims=True)
        own = hot[:local]
        rank = jnp.dot(own.astype(jnp.bfloat16), before, preferred_element_type=jnp.float32)
        key = jnp.where(own > 0.0, rank, -1.0)
        pick = (key[:, None, :] == slot).astype(jnp.float32)
        at = slice(p * CAP, (p + 1) * CAP)
        weight_ref[:, at, :] = jnp.broadcast_to(
            jnp.sum(pick * gate[:, None, :], axis=-1, keepdims=True), (local, CAP, LANES)
        )
        pick = pick.reshape(local * CAP, BLOCK).astype(jnp.bfloat16)
        picks_ref[p] = pick
        taken = jnp.dot(pick, x, preferred_element_type=jnp.float32)
        rows_ref[:, at, :] = taken.astype(jnp.bfloat16).reshape(local, CAP, width)
        hots.append(hot)
        probs.append(prob)
    if n_row:
        bal_ref = refs[3]
        for d in range(NDOC):
            counts = jnp.zeros((EXPERTS, BLOCK), jnp.float32)
            mass = jnp.zeros((EXPERTS, BLOCK), jnp.float32)
            for p in range(n_row):
                inside = seg_ref[p] == d
                counts = counts + jnp.where(inside, hots[p], 0.0)
                mass = mass + jnp.where(inside, probs[p], 0.0)
            both = jnp.sum(counts, axis=1, keepdims=True) * jnp.sum(mass, axis=1, keepdims=True)
            bal_ref[d : d + 1, :] = (
                jnp.broadcast_to(jnp.sum(both, axis=0, keepdims=True), (1, LANES))
                * scale_ref[d : d + 1, :]
            )


def whole(a):
    return pl.BlockSpec(a.shape, lambda *i: (0,) * a.ndim)


def dispatch(parts, top, base, rw, local, row=None):
    n_parts = len(parts)
    n, width = parts[0].shape[0] // (BLOCK + EXTRA), parts[0].shape[1]
    slots = n_parts * CAP
    in_specs = [
        pl.BlockSpec(memory_space=pltpu.SMEM),
        whole(rw),
    ] + [pl.BlockSpec((BLOCK + EXTRA, width), lambda i: (i, 0))] * n_parts
    out_specs = [
        pl.BlockSpec((local, slots, width), lambda i: (0, i, 0)),
        pl.BlockSpec((local, slots, LANES), lambda i: (0, i, 0)),
        pl.BlockSpec((n_parts, local * CAP, BLOCK), lambda i: (i, 0, 0)),
    ]
    out_shape = [
        jax.ShapeDtypeStruct((local, n * slots, width), jnp.bfloat16),
        jax.ShapeDtypeStruct((local, n * slots, LANES), jnp.float32),
        jax.ShapeDtypeStruct((n * n_parts, local * CAP, BLOCK), jnp.bfloat16),
    ]
    extra = ()
    if row is not None:
        extra = row
        in_specs += [whole(a) for a in row]
        out_specs.append(pl.BlockSpec((NDOC, LANES), lambda i: (0, 0)))
        out_shape.append(jax.ShapeDtypeStruct((NDOC, LANES), jnp.float32))
    return call(
        functools.partial(dispatch_kernel, n_parts, n_parts if row is not None else 0, top),
        3 * n,
        (n,),
        in_specs,
        out_specs,
        out_shape,
        [],
        "dispatch",
    )(base, rw, *parts, *extra)


def sort_kernel(gu_ref, out_ref, wide):
    group, _, hidden, width = out_ref.shape
    chunks = width // LANES
    for e in range(group):
        wide[e] = gu_ref[e].astype(jnp.float32)
        for z in range(2):
            for c in range(chunks):
                part = wide[e, pl.ds(2 * c + z, hidden, stride=2 * chunks), :]
                out_ref[e, z, :, c * LANES : (c + 1) * LANES] = part.astype(jnp.bfloat16)


def sort_rows(gate_up):
    local, hidden, _, width = gate_up.shape
    group = 2 if local % 2 == 0 else 1
    chunks = width // LANES
    gu = gate_up.reshape(local, hidden, 2, chunks, LANES).swapaxes(2, 3)
    gu = gu.reshape(local, hidden * 2 * chunks, LANES)
    return call(
        sort_kernel,
        8,
        (local // group,),
        [pl.BlockSpec((group,) + gu.shape[1:], lambda e: (e, 0, 0))],
        pl.BlockSpec((group, 2, hidden, width), lambda e: (e, 0, 0, 0)),
        jax.ShapeDtypeStruct((local, 2, hidden, width), jnp.bfloat16),
        [pltpu.VMEM((group,) + gu.shape[1:], jnp.float32)],
        "sort",
    )(gu)


def expert_kernel(n, *refs):
    rows, weights = refs[:n], refs[n : 2 * n]
    gu_ref, down_ref = refs[2 * n : 2 * n + 2]
    outs = refs[2 * n + 2 :]
    group = down_ref.shape[0]
    size = rows[0].shape[1]
    for e in range(group):
        held = jnp.concatenate([r[e] for r in rows], axis=0)
        g = lax.dot_general(held, gu_ref[e, 0], NT, preferred_element_type=jnp.float32)
        u = lax.dot_general(held, gu_ref[e, 1], NT, preferred_element_type=jnp.float32)
        inner = (g * lax.logistic(g) * u).astype(jnp.bfloat16)
        made = jnp.dot(inner, down_ref[e], preferred_element_type=jnp.float32)
        for i in range(n):
            w = weights[i][e]
            part = made[i * size : (i + 1) * size]
            for c in range(part.shape[1] // LANES):
                at = slice(c * LANES, (c + 1) * LANES)
                outs[i][e, :, at] = (part[:, at] * w).astype(jnp.bfloat16)


def experts(rows, weights, gu, down):
    n = len(rows)
    local, slots, width = rows[0].shape
    size = min(slots, EXPERT_ROWS)
    hidden = down.shape[1]
    group = 2 if local % 2 == 0 else 1
    rows_spec = pl.BlockSpec((group, size, width), lambda e, i: (e, i, 0))
    weight_spec = pl.BlockSpec((group, size, LANES), lambda e, i: (e, i, 0))
    return call(
        functools.partial(expert_kernel, n),
        6,
        (local // group, slots // size),
        [rows_spec] * n
        + [weight_spec] * n
        + [
            pl.BlockSpec((group, 2, hidden, width), lambda e, i: (e, 0, 0, 0)),
            pl.BlockSpec((group, hidden, width), lambda e, i: (e, 0, 0)),
        ],
        [rows_spec] * n,
        [jax.ShapeDtypeStruct(r.shape, jnp.bfloat16) for r in rows],
        [],
        "experts",
    )(*rows, *weights, gu, down)


def combine_kernel(groups, picks_ref, made_ref, *outs):
    local, _, width = made_ref.shape
    per = outs[0].shape[1] // BLOCK
    for p in range(picks_ref.shape[0]):
        held = made_ref[:, p * CAP : (p + 1) * CAP, :].reshape(local * CAP, width)
        mix = lax.dot_general(picks_ref[p], held, TN, preferred_element_type=jnp.float32)
        out, at = outs[p // per], p % per
        out[0, at * BLOCK : (at + 1) * BLOCK, :] = mix.astype(jnp.bfloat16)


def combine(picks, made, n_parts):
    n = picks.shape[0] // n_parts
    local, _, width = made.shape
    slots = n_parts * CAP
    half = n_parts // 2 * BLOCK
    out = pl.BlockSpec((1, half, width), lambda i: (i, 0, 0))
    return call(
        functools.partial(combine_kernel, 2),
        2 * n,
        (n,),
        [
            pl.BlockSpec((n_parts,) + picks.shape[1:], lambda i: (i, 0, 0)),
            pl.BlockSpec((local, slots, width), lambda i: (0, i, 0)),
        ],
        [out, out],
        [jax.ShapeDtypeStruct((n, half, width), jnp.bfloat16)] * 2,
        [],
        "combine",
    )(picks, made)


def attend_kernel(n, first_ref, last_ref, kpos_ref, q_ref, *refs):
    parts, (out_ref, even, odd) = refs[:n], refs[n:]
    rows, kdim = parts[0].shape
    wide = even.shape[1]
    half = wide - kdim

    @pl.when(pl.program_id(0) == 0)
    def _():
        pad = jnp.zeros((rows, half), jnp.bfloat16)
        for i in range(n):
            at = slice(i * rows, (i + 1) * rows)
            even[at, :] = jnp.concatenate([parts[i][...], pad], axis=1)
            odd[at, :] = jnp.concatenate([pad, parts[i][...]], axis=1)

    allowed = (kpos_ref[...] >= first_ref[...]) & (kpos_ref[...] <= last_ref[...])
    for i, keys in enumerate((even, odd)):
        at = i * (kdim - half)
        scores = lax.dot_general(
            q_ref[:, at : at + wide], keys[...], NT, preferred_element_type=jnp.float32
        )
        scores = jnp.where(allowed, scores * qk_scale, -1e30)
        expo = jnp.exp(scores - jnp.max(scores, axis=-1, keepdims=True))
        probs = (expo / jnp.sum(expo, axis=-1, keepdims=True)).astype(jnp.bfloat16)
        out_ref[:, i * LATENT : (i + 1) * LATENT] = jnp.dot(
            probs, even[:, :LATENT], preferred_element_type=jnp.float32
        ).astype(jnp.bfloat16)


def attend(queries, parts, first, last, kpos):
    n = len(parts)
    rows, kdim = parts[0].shape
    wide = -(-kdim // LANES) * LANES
    return call(
        functools.partial(attend_kernel, n),
        6,
        (HEADS // 2,),
        [whole(first), whole(last), whole(kpos)]
        + [pl.BlockSpec((rows, 2 * kdim), lambda h: (0, h))]
        + [whole(p) for p in parts],
        pl.BlockSpec((rows, 2 * LATENT), lambda h: (0, h)),
        jax.ShapeDtypeStruct((rows, HEADS * LATENT), jnp.bfloat16),
        [pltpu.VMEM((n * rows, wide), jnp.bfloat16)] * 2,
        "attention",
    )(first, last, kpos, queries, *parts)


def added(*terms):
    total = terms[0].astype(jnp.float32)
    for term in terms[1:]:
        total = total + term.astype(jnp.float32)
    return total.astype(jnp.bfloat16)


def shards(queries, latent_kv, doc_lengths, hidden_in, router_weight, expert_ids, gate_up, w_down):
    tok_rows, width = hidden_in.shape[1:]
    n_ctx, n_exp = lax.axis_size("ctx"), lax.axis_size("exp")
    ctx, exp = lax.axis_index("ctx"), lax.axis_index("exp")
    local = gate_up.shape[0]
    near = n_exp <= 4
    shifts = [0, 1, 3, 2][:n_exp] if near else [0]
    flips = (2, 1)
    tokens = hidden_in[0]

    def flip(a, bit):
        return lax.ppermute(a, "ctx", [(i, i ^ bit) for i in range(n_ctx)])

    def shift(a, d):
        return lax.ppermute(a, "exp", [(i, (i + d) % n_exp) for i in range(n_exp)])

    def along_exp(a):
        if near:
            return [a if d == 0 else shift(a, d) for d in shifts]
        return [lax.all_gather(a, "exp", axis=0, tiled=True)]

    masks = [0, 2, 1, 3]
    order = jnp.stack([ctx ^ m for m in masks])

    top = expert_ids.shape[2]
    picks = expert_ids[0].T.astype(jnp.bfloat16).reshape(1, top * tok_rows)
    picks = jnp.pad(picks, ((0, EXTRA - 1), (0, width - top * tok_rows)))
    packed = jnp.concatenate([tokens, picks], axis=0)

    near_parts = along_exp(packed)
    spread = [[a] for a in near_parts]
    spread = [held + [flip(a, 2) for a in held] for held in spread]
    spread = [held + [flip(a, 1) for a in held] for held in spread]
    kv = [latent_kv[0]]
    for bit in flips:
        kv = kv + [flip(a, bit) for a in kv]

    lengths = doc_lengths[0]
    ends = jnp.cumsum(lengths)
    row_pos = order[:, None] * tok_rows + jnp.arange(tok_rows, dtype=jnp.int32)[None, :]
    pos = row_pos[0]
    passed = pos[:, None] >= ends[None, :]
    first = jnp.max(jnp.where(passed, ends[None, :], 0), axis=1)
    context = attend(queries[0], kv, first[:, None], pos[:, None], row_pos.reshape(1, -1))

    seg = jnp.sum((row_pos[..., None] >= ends).astype(jnp.int32), axis=-1)
    sizes = lengths.astype(jnp.float32)
    scale = jnp.broadcast_to((EXPERTS / (top * sizes * sizes))[:, None], (NDOC, LANES))

    base = (exp * local).reshape(1).astype(jnp.int32)
    rw = jnp.roll(router_weight.T, -exp * local, axis=0)
    balance = None
    sent = []
    for i, held in enumerate(spread):
        row = (seg.reshape(-1, 1, BLOCK), scale) if near and i == 0 else None
        out = dispatch(held, top, base, rw, local, row)
        sent.append(out[:3])
        if row is not None:
            balance = out[3]

    gu = sort_rows(gate_up)
    groups = [[1, 0], [3, 2]] if len(shifts) == 4 else [range(len(shifts))]
    back = []
    for group in groups:
        made = experts([sent[i][0] for i in group], [sent[i][1] for i in group], gu, w_down)
        for i, part in zip(group, made):
            keep, give = combine(sent[i][2], part, n_ctx)
            got = flip(give, 1)
            far = added(keep[:, tok_rows:], got[:, tok_rows:])
            terms = [keep[:, :tok_rows], got[:, :tok_rows], flip(far, 2)]
            if i:
                back.append(shift(added(*terms), -shifts[i]))
            else:
                back = back + terms
    if near:
        expert_mix = added(*back)
    else:
        expert_mix = lax.psum_scatter(
            added(*back).reshape(-1, width), "exp", scatter_dimension=0, tiled=True
        ).reshape(1, tok_rows, width)

    if balance is None:
        row = lax.all_gather(tokens, "ctx", axis=0, tiled=True)
        router = jax.nn.softmax(
            jnp.dot(row, router_weight, preferred_element_type=jnp.float32), axis=-1
        )
        row_ids = lax.all_gather(expert_ids[0], "ctx", axis=0, tiled=True)
        hot = (row_ids[:, :, None] == jnp.arange(EXPERTS, dtype=jnp.int32)).astype(jnp.float32)
        at = jnp.arange(row.shape[0], dtype=jnp.int32)
        seg_at = jnp.sum((at[:, None] >= ends[None, :]).astype(jnp.int32), axis=1)
        seg_hot = (seg_at[:, None] == jnp.arange(NDOC, dtype=jnp.int32)).astype(jnp.float32)
        exact = lax.Precision.HIGHEST
        counts = jnp.dot(seg_hot.T, hot.sum(axis=1), precision=exact)
        mass = jnp.dot(seg_hot.T, router, precision=exact)
        per_doc = jnp.sum(counts * mass, axis=1) * scale[:, 0]
    else:
        per_doc = balance[:, 0]
    return context[None], expert_mix, per_doc.reshape(1, NDOC)


def solution(mesh):
    rows = P(("group", "exp"), "ctx", None)
    docs = P(("group", "exp"), None)
    return jax.shard_map(
        shards,
        mesh=mesh,
        in_specs=(rows, rows, docs, rows, P(), rows, P("exp", "ctx", None, None), P("exp", "ctx", None)),
        out_specs=(rows, rows, docs),
        check_vma=False,
    )
```

```python
import functools

import jax
import jax.numpy as jnp
from jax import lax
from jax.experimental import pallas as pl
from jax.experimental.pallas import tpu as pltpu
from jax.sharding import PartitionSpec as P

EXPERTS = 64
HEADS = 8
LATENT = 512
CAP = 16
NDOC = 8
BLOCK = 128
LANES = 128
EXPERT_ROWS = 256
EXTRA = 16
VMEM = 14 * 2**20
VMEM_EXPERTS = 40 * 2**20
VMEM_SORT = 56 * 2**20
PEAK = 1.1e9

qk_scale = 192.0 ** (-0.5)
NT = (((1,), (1,)), ((), ()))
TN = (((0,), (0,)), ((), ()))


def call(kernel, micros, grid, in_specs, out_specs, out_shape, scratch, name, limit=VMEM):
    return pl.pallas_call(
        kernel,
        grid=grid,
        in_specs=in_specs,
        out_specs=out_specs,
        out_shape=out_shape,
        scratch_shapes=scratch,
        compiler_params=pltpu.CompilerParams(
            dimension_semantics=("arbitrary",) * len(grid), vmem_limit_bytes=limit
        ),
        cost_estimate=pl.CostEstimate(
            flops=int(micros * PEAK), bytes_accessed=0, transcendentals=0
        ),
        name=name,
    )


def dispatch_kernel(n_parts, n_row, top, n_after, base_ref, rw_ref, *refs):
    parts, refs = refs[:n_parts], refs[n_parts + n_after :]
    if n_row:
        seg_ref, scale_ref = refs[:2]
        refs = refs[2:]
    rows_ref, weight_ref, picks_ref = refs[:3]
    local = rows_ref.shape[0]
    width = rows_ref.shape[2]
    names = lax.broadcasted_iota(jnp.int32, (EXPERTS, BLOCK), 0).astype(jnp.float32)
    base = base_ref[0].astype(jnp.float32)
    before = (
        lax.broadcasted_iota(jnp.int32, (BLOCK, BLOCK), 0)
        < lax.broadcasted_iota(jnp.int32, (BLOCK, BLOCK), 1)
    ).astype(jnp.bfloat16)
    slot = lax.broadcasted_iota(jnp.int32, (local, CAP, BLOCK), 1).astype(jnp.float32)
    hots, probs = [], []
    for p in range(n_parts):
        x = parts[p][:BLOCK, :]
        ids = parts[p][BLOCK : BLOCK + EXTRA, :].astype(jnp.float32)[0:1] - base
        ids = jnp.where(ids < 0.0, ids + EXPERTS, ids)
        logits = lax.dot_general(rw_ref[...], x, NT, preferred_element_type=jnp.float32)
        expo = jnp.exp(logits - jnp.max(logits, axis=0, keepdims=True))
        prob = expo / jnp.sum(expo, axis=0, keepdims=True)
        hot = names == ids[:, :BLOCK]
        for k in range(1, top):
            hot = hot | (names == ids[:, k * BLOCK : (k + 1) * BLOCK])
        hot = hot.astype(jnp.float32)
        chosen = prob * hot
        gate = chosen[:local] / jnp.sum(chosen, axis=0, keepdims=True)
        own = hot[:local]
        rank = jnp.dot(own.astype(jnp.bfloat16), before, preferred_element_type=jnp.float32)
        key = jnp.where(own > 0.0, rank, -1.0)
        pick = (key[:, None, :] == slot).astype(jnp.float32)
        at = slice(p * CAP, (p + 1) * CAP)
        weight_ref[:, at, :] = jnp.broadcast_to(
            jnp.sum(pick * gate[:, None, :], axis=-1, keepdims=True), (local, CAP, LANES)
        )
        pick = pick.reshape(local * CAP, BLOCK).astype(jnp.bfloat16)
        picks_ref[p] = pick
        taken = jnp.dot(pick, x, preferred_element_type=jnp.float32)
        rows_ref[:, at, :] = taken.astype(jnp.bfloat16).reshape(local, CAP, width)
        hots.append(hot)
        probs.append(prob)
    if n_row:
        bal_ref = refs[3]
        for d in range(NDOC):
            counts = jnp.zeros((EXPERTS, BLOCK), jnp.float32)
            mass = jnp.zeros((EXPERTS, BLOCK), jnp.float32)
            for p in range(n_row):
                inside = seg_ref[p] == d
                counts = counts + jnp.where(inside, hots[p], 0.0)
                mass = mass + jnp.where(inside, probs[p], 0.0)
            both = jnp.sum(counts, axis=1, keepdims=True) * jnp.sum(mass, axis=1, keepdims=True)
            bal_ref[d : d + 1, :] = (
                jnp.broadcast_to(jnp.sum(both, axis=0, keepdims=True), (1, LANES))
                * scale_ref[d : d + 1, :]
            )


IN_HBM = pl.BlockSpec(memory_space=pltpu.HBM)
ANYWHERE = pl.BlockSpec(memory_space=pl.ANY)


def whole(a):
    return pl.BlockSpec(a.shape, lambda *i: (0,) * a.ndim)


def dispatch(parts, top, base, rw, local, row=None, after=()):
    n_parts = len(parts)
    n, width = parts[0].shape[0] // (BLOCK + EXTRA), parts[0].shape[1]
    slots = n_parts * CAP
    in_specs = [
        pl.BlockSpec(memory_space=pltpu.SMEM),
        whole(rw),
    ] + [pl.BlockSpec((BLOCK + EXTRA, width), lambda i: (i, 0))] * n_parts
    in_specs += [ANYWHERE] * len(after)
    out_specs = [
        pl.BlockSpec((local, slots, width), lambda i: (0, i, 0)),
        pl.BlockSpec((local, slots, LANES), lambda i: (0, i, 0)),
        pl.BlockSpec((n_parts, local * CAP, BLOCK), lambda i: (i, 0, 0)),
    ]
    out_shape = [
        jax.ShapeDtypeStruct((local, n * slots, width), jnp.bfloat16),
        jax.ShapeDtypeStruct((local, n * slots, LANES), jnp.float32),
        jax.ShapeDtypeStruct((n * n_parts, local * CAP, BLOCK), jnp.bfloat16),
    ]
    extra = ()
    if row is not None:
        extra = row
        in_specs += [whole(a) for a in row]
        out_specs.append(pl.BlockSpec((NDOC, LANES), lambda i: (0, 0)))
        out_shape.append(jax.ShapeDtypeStruct((NDOC, LANES), jnp.float32))
    return call(
        functools.partial(dispatch_kernel, n_parts, n_parts if row is not None else 0, top, len(after)),
        3 * n,
        (n,),
        in_specs,
        out_specs,
        out_shape,
        [],
        "dispatch",
    )(base, rw, *parts, *after, *extra)


def fetch(sources, slots, sem, step, steps, first):
    group = slots[0].shape[1]

    def copies(at):
        slot = lax.rem(at, 2)
        return [
            pltpu.make_async_copy(
                source.at[pl.ds(at * group, group)], held.at[slot], sem.at[i, slot]
            )
            for i, (source, held) in enumerate(zip(sources, slots))
        ]

    @pl.when(first & (step == 0))
    def _():
        for copy in copies(step):
            copy.start()

    @pl.when(first & (step + 1 < steps))
    def _():
        for copy in copies(step + 1):
            copy.start()

    @pl.when(first)
    def _():
        for copy in copies(step):
            copy.wait()

    return lax.rem(step, 2)


def sort_kernel(gu_ref, out_ref, held, made, wide, in_sem, out_sem):
    step, steps = pl.program_id(0), pl.num_programs(0)
    _, group, _, hidden, width = made.shape
    chunks = width // LANES
    slot = fetch([gu_ref], [held], in_sem, step, steps, step >= 0)

    def leave(at):
        to = lax.rem(at, 2)
        return pltpu.make_async_copy(
            made.at[to], out_ref.at[pl.ds(at * group, group)], out_sem.at[to]
        )

    @pl.when(step >= 2)
    def _():
        leave(step - 2).wait()

    for e in range(group):
        wide[e] = held[slot, e].astype(jnp.float32)
        for z in range(2):
            for c in range(chunks):
                part = wide[e, pl.ds(2 * c + z, hidden, stride=2 * chunks), :]
                made[slot, e, z, :, c * LANES : (c + 1) * LANES] = part.astype(jnp.bfloat16)
    leave(step).start()

    @pl.when(step == steps - 1)
    def _():
        @pl.when(step >= 1)
        def _():
            leave(step - 1).wait()

        leave(step).wait()


def sort_rows(gate_up):
    local, hidden, _, width = gate_up.shape
    group = 2 if local % 2 == 0 else 1
    chunks = width // LANES
    gu = gate_up.reshape(local, hidden, 2, chunks, LANES).swapaxes(2, 3)
    gu = gu.reshape(local, hidden * 2 * chunks, LANES)
    return call(
        sort_kernel,
        8,
        (local // group,),
        [IN_HBM],
        IN_HBM,
        jax.ShapeDtypeStruct((local, 2, hidden, width), jnp.bfloat16),
        [
            pltpu.VMEM((2, group) + gu.shape[1:], jnp.bfloat16),
            pltpu.VMEM((2, group, 2, hidden, width), jnp.bfloat16),
            pltpu.VMEM((group,) + gu.shape[1:], jnp.float32),
            pltpu.SemaphoreType.DMA((1, 2)),
            pltpu.SemaphoreType.DMA((2,)),
        ],
        "sort",
        VMEM_SORT,
    )(gu)


def expert_kernel(n, *refs):
    rows, weights = refs[:n], refs[n : 2 * n]
    gu_ref, down_ref = refs[2 * n : 2 * n + 2]
    outs, (gu, down, sem) = refs[-3 - n : -3], refs[-3:]
    group = gu.shape[1]
    size = rows[0].shape[1]
    slot = fetch(
        [gu_ref, down_ref],
        [gu, down],
        sem,
        pl.program_id(0),
        pl.num_programs(0),
        pl.program_id(1) == 0,
    )
    for e in range(group):
        held = jnp.concatenate([r[e] for r in rows], axis=0)
        g = lax.dot_general(held, gu[slot, e, 0], NT, preferred_element_type=jnp.float32)
        u = lax.dot_general(held, gu[slot, e, 1], NT, preferred_element_type=jnp.float32)
        inner = (g * lax.logistic(g) * u).astype(jnp.bfloat16)
        made = jnp.dot(inner, down[slot, e], preferred_element_type=jnp.float32)
        for i in range(n):
            w = weights[i][e]
            part = made[i * size : (i + 1) * size]
            for c in range(part.shape[1] // LANES):
                at = slice(c * LANES, (c + 1) * LANES)
                outs[i][e, :, at] = (part[:, at] * w).astype(jnp.bfloat16)


def experts(rows, weights, gu, down, after=()):
    n = len(rows)
    local, slots, width = rows[0].shape
    size = min(slots, EXPERT_ROWS)
    hidden = down.shape[1]
    group = 2 if local % 2 == 0 else 1
    rows_spec = pl.BlockSpec((group, size, width), lambda e, i: (e, i, 0))
    weight_spec = pl.BlockSpec((group, size, LANES), lambda e, i: (e, i, 0))
    return call(
        functools.partial(expert_kernel, n),
        6,
        (local // group, slots // size),
        [rows_spec] * n + [weight_spec] * n + [IN_HBM, IN_HBM] + [ANYWHERE] * len(after),
        [rows_spec] * n,
        [jax.ShapeDtypeStruct(r.shape, jnp.bfloat16) for r in rows],
        [
            pltpu.VMEM((2, group, 2, hidden, width), jnp.bfloat16),
            pltpu.VMEM((2, group, hidden, width), jnp.bfloat16),
            pltpu.SemaphoreType.DMA((2, 2)),
        ],
        "experts",
        VMEM_EXPERTS,
    )(*rows, *weights, gu, down, *after)


def combine_kernel(groups, picks_ref, made_ref, *outs):
    local, _, width = made_ref.shape
    per = outs[0].shape[1] // BLOCK
    for p in range(picks_ref.shape[0]):
        held = made_ref[:, p * CAP : (p + 1) * CAP, :].reshape(local * CAP, width)
        mix = lax.dot_general(picks_ref[p], held, TN, preferred_element_type=jnp.float32)
        out, at = outs[p // per], p % per
        out[0, at * BLOCK : (at + 1) * BLOCK, :] = mix.astype(jnp.bfloat16)


def combine(picks, made, n_parts):
    n = picks.shape[0] // n_parts
    local, _, width = made.shape
    slots = n_parts * CAP
    half = n_parts // 2 * BLOCK
    out = pl.BlockSpec((1, half, width), lambda i: (i, 0, 0))
    return call(
        functools.partial(combine_kernel, 2),
        2 * n,
        (n,),
        [
            pl.BlockSpec((n_parts,) + picks.shape[1:], lambda i: (i, 0, 0)),
            pl.BlockSpec((local, slots, width), lambda i: (0, i, 0)),
        ],
        [out, out],
        [jax.ShapeDtypeStruct((n, half, width), jnp.bfloat16)] * 2,
        [],
        "combine",
    )(picks, made)


def attend_kernel(n, first_ref, last_ref, kpos_ref, q_ref, *refs):
    parts, (out_ref, even, odd) = refs[:n], refs[n:]
    rows, kdim = parts[0].shape
    wide = even.shape[1]
    half = wide - kdim

    @pl.when(pl.program_id(0) == 0)
    def _():
        pad = jnp.zeros((rows, half), jnp.bfloat16)
        for i in range(n):
            at = slice(i * rows, (i + 1) * rows)
            even[at, :] = jnp.concatenate([parts[i][...], pad], axis=1)
            odd[at, :] = jnp.concatenate([pad, parts[i][...]], axis=1)

    allowed = (kpos_ref[...] >= first_ref[...]) & (kpos_ref[...] <= last_ref[...])
    for i, keys in enumerate((even, odd)):
        at = i * (kdim - half)
        scores = lax.dot_general(
            q_ref[:, at : at + wide], keys[...], NT, preferred_element_type=jnp.float32
        )
        scores = jnp.where(allowed, scores * qk_scale, -1e30)
        expo = jnp.exp(scores - jnp.max(scores, axis=-1, keepdims=True))
        probs = (expo / jnp.sum(expo, axis=-1, keepdims=True)).astype(jnp.bfloat16)
        out_ref[:, i * LATENT : (i + 1) * LATENT] = jnp.dot(
            probs, even[:, :LATENT], preferred_element_type=jnp.float32
        ).astype(jnp.bfloat16)


def attend(queries, parts, first, last, kpos):
    n = len(parts)
    rows, kdim = parts[0].shape
    wide = -(-kdim // LANES) * LANES
    return call(
        functools.partial(attend_kernel, n),
        6,
        (HEADS // 2,),
        [whole(first), whole(last), whole(kpos)]
        + [pl.BlockSpec((rows, 2 * kdim), lambda h: (0, h))]
        + [whole(p) for p in parts],
        pl.BlockSpec((rows, 2 * LATENT), lambda h: (0, h)),
        jax.ShapeDtypeStruct((rows, HEADS * LATENT), jnp.bfloat16),
        [pltpu.VMEM((n * rows, wide), jnp.bfloat16)] * 2,
        "attention",
    )(first, last, kpos, queries, *parts)


def added(*terms):
    total = terms[0].astype(jnp.float32)
    for term in terms[1:]:
        total = total + term.astype(jnp.float32)
    return total.astype(jnp.bfloat16)


def shards(queries, latent_kv, doc_lengths, hidden_in, router_weight, expert_ids, gate_up, w_down):
    tok_rows, width = hidden_in.shape[1:]
    n_ctx, n_exp = lax.axis_size("ctx"), lax.axis_size("exp")
    ctx, exp = lax.axis_index("ctx"), lax.axis_index("exp")
    local = gate_up.shape[0]
    near = n_exp <= 4
    shifts = [0, 1, 3, 2][:n_exp] if near else [0]
    flips = (2, 1)
    tokens = hidden_in[0]

    def flip(a, bit):
        return lax.ppermute(a, "ctx", [(i, i ^ bit) for i in range(n_ctx)])

    def shift(a, d):
        return lax.ppermute(a, "exp", [(i, (i + d) % n_exp) for i in range(n_exp)])

    def along_exp(a):
        if near:
            return [a if d == 0 else shift(a, d) for d in shifts]
        return [lax.all_gather(a, "exp", axis=0, tiled=True)]

    masks = [0, 2, 1, 3]
    order = jnp.stack([ctx ^ m for m in masks])

    top = expert_ids.shape[2]
    picks = expert_ids[0].T.astype(jnp.bfloat16).reshape(1, top * tok_rows)
    picks = jnp.pad(picks, ((0, EXTRA - 1), (0, width - top * tok_rows)))
    packed = jnp.concatenate([tokens, picks], axis=0)

    near_parts = along_exp(packed)
    spread = [[a] for a in near_parts]
    spread = [held + [flip(a, 2) for a in held] for held in spread]
    spread = [held + [flip(a, 1) for a in held] for held in spread]
    kv = [latent_kv[0]]
    for bit in flips:
        kv = kv + [flip(a, bit) for a in kv]

    lengths = doc_lengths[0]
    ends = jnp.cumsum(lengths)
    row_pos = order[:, None] * tok_rows + jnp.arange(tok_rows, dtype=jnp.int32)[None, :]
    pos = row_pos[0]
    passed = pos[:, None] >= ends[None, :]
    first = jnp.max(jnp.where(passed, ends[None, :], 0), axis=1)
    context = attend(queries[0], kv, first[:, None], pos[:, None], row_pos.reshape(1, -1))

    seg = jnp.sum((row_pos[..., None] >= ends).astype(jnp.int32), axis=-1)
    sizes = lengths.astype(jnp.float32)
    scale = jnp.broadcast_to((EXPERTS / (top * sizes * sizes))[:, None], (NDOC, LANES))

    base = (exp * local).reshape(1).astype(jnp.int32)
    rw = jnp.roll(router_weight.T, -exp * local, axis=0)
    balance = None
    gu = sort_rows(gate_up)
    groups = [[1, 2], [3, 0]] if len(shifts) == 4 else [range(len(shifts))]
    back, before, begun = [], (), []
    for n, group in enumerate(groups):
        sent = []
        for i in group:
            row = (seg.reshape(-1, 1, BLOCK), scale) if near and i == 0 else None
            out = dispatch(spread[i], top, base, rw, local, row, before if i else ())
            sent.append(out[:3])
            if row is not None:
                balance = out[3]
        if n + 1 < len(groups):
            after = (near_parts[groups[n + 1][0]],)
        else:
            after = begun
        made = experts([a[0] for a in sent], [a[1] for a in sent], gu, w_down, after)
        before, begun = (made[0],), []
        for i, dispatched, part in zip(group, sent, made):
            keep, give = combine(dispatched[2], part, n_ctx)
            got = flip(give, 1)
            far = added(keep[:, tok_rows:], got[:, tok_rows:])
            begun.append(far)
            terms = [keep[:, :tok_rows], got[:, :tok_rows], flip(far, 2)]
            if i:
                back.append(shift(added(*terms), -shifts[i]))
            else:
                back = back + terms
    if near:
        expert_mix = added(*back)
    else:
        expert_mix = lax.psum_scatter(
            added(*back).reshape(-1, width), "exp", scatter_dimension=0, tiled=True
        ).reshape(1, tok_rows, width)

    if balance is None:
        row = lax.all_gather(tokens, "ctx", axis=0, tiled=True)
        router = jax.nn.softmax(
            jnp.dot(row, router_weight, preferred_element_type=jnp.float32), axis=-1
        )
        row_ids = lax.all_gather(expert_ids[0], "ctx", axis=0, tiled=True)
        hot = (row_ids[:, :, None] == jnp.arange(EXPERTS, dtype=jnp.int32)).astype(jnp.float32)
        at = jnp.arange(row.shape[0], dtype=jnp.int32)
        seg_at = jnp.sum((at[:, None] >= ends[None, :]).astype(jnp.int32), axis=1)
        seg_hot = (seg_at[:, None] == jnp.arange(NDOC, dtype=jnp.int32)).astype(jnp.float32)
        exact = lax.Precision.HIGHEST
        counts = jnp.dot(seg_hot.T, hot.sum(axis=1), precision=exact)
        mass = jnp.dot(seg_hot.T, router, precision=exact)
        per_doc = jnp.sum(counts * mass, axis=1) * scale[:, 0]
    else:
        per_doc = balance[:, 0]
    return context[None], expert_mix, per_doc.reshape(1, NDOC)


def solution(mesh):
    rows = P(("group", "exp"), "ctx", None)
    docs = P(("group", "exp"), None)
    return jax.shard_map(
        shards,
        mesh=mesh,
        in_specs=(rows, rows, docs, rows, P(), rows, P("exp", "ctx", None, None), P("exp", "ctx", None)),
        out_specs=(rows, rows, docs),
        check_vma=False,
    )
```

```python
import functools

import jax
import jax.numpy as jnp
from jax import lax
from jax.experimental import pallas as pl
from jax.experimental.pallas import tpu as pltpu
from jax.sharding import PartitionSpec as P

EXPERTS = 64
HEADS = 8
LATENT = 512
CAP = 16
NDOC = 8
BLOCK = 128
LANES = 128
EXPERT_ROWS = 256
EXTRA = 16
VMEM = 14 * 2**20
VMEM_EXPERTS = 36 * 2**20
VMEM_SORT = 52 * 2**20
PIECES = 4
DEPTH = 3
PEAK = 1.1e9

qk_scale = 192.0 ** (-0.5)
NT = (((1,), (1,)), ((), ()))
TN = (((0,), (0,)), ((), ()))


def call(kernel, micros, grid, in_specs, out_specs, out_shape, scratch, name, limit=VMEM, aliases={}):
    return pl.pallas_call(
        kernel,
        grid=grid,
        in_specs=in_specs,
        out_specs=out_specs,
        out_shape=out_shape,
        scratch_shapes=scratch,
        input_output_aliases=aliases,
        compiler_params=pltpu.CompilerParams(
            dimension_semantics=("arbitrary",) * len(grid), vmem_limit_bytes=limit
        ),
        cost_estimate=pl.CostEstimate(
            flops=int(micros * PEAK), bytes_accessed=0, transcendentals=0
        ),
        name=name,
    )


def dispatch_kernel(n_parts, n_row, top, n_after, base_ref, rw_ref, *refs):
    parts, refs = refs[:n_parts], refs[n_parts + n_after :]
    if n_row:
        seg_ref, scale_ref = refs[:2]
        refs = refs[2:]
    rows_ref, weight_ref, picks_ref = refs[:3]
    local = rows_ref.shape[0]
    width = rows_ref.shape[2]
    names = lax.broadcasted_iota(jnp.int32, (EXPERTS, BLOCK), 0).astype(jnp.float32)
    base = base_ref[0].astype(jnp.float32)
    before = (
        lax.broadcasted_iota(jnp.int32, (BLOCK, BLOCK), 0)
        < lax.broadcasted_iota(jnp.int32, (BLOCK, BLOCK), 1)
    ).astype(jnp.bfloat16)
    slot = lax.broadcasted_iota(jnp.int32, (local, CAP, BLOCK), 1).astype(jnp.float32)
    hots, probs = [], []
    for p in range(n_parts):
        x = parts[p][:BLOCK, :]
        ids = parts[p][BLOCK : BLOCK + EXTRA, :].astype(jnp.float32)[0:1] - base
        ids = jnp.where(ids < 0.0, ids + EXPERTS, ids)
        logits = lax.dot_general(rw_ref[...], x, NT, preferred_element_type=jnp.float32)
        expo = jnp.exp(logits - jnp.max(logits, axis=0, keepdims=True))
        prob = expo / jnp.sum(expo, axis=0, keepdims=True)
        hot = names == ids[:, :BLOCK]
        for k in range(1, top):
            hot = hot | (names == ids[:, k * BLOCK : (k + 1) * BLOCK])
        hot = hot.astype(jnp.float32)
        chosen = prob * hot
        gate = chosen[:local] / jnp.sum(chosen, axis=0, keepdims=True)
        own = hot[:local]
        rank = jnp.dot(own.astype(jnp.bfloat16), before, preferred_element_type=jnp.float32)
        key = jnp.where(own > 0.0, rank, -1.0)
        pick = (key[:, None, :] == slot).astype(jnp.float32)
        at = slice(p * CAP, (p + 1) * CAP)
        weight_ref[:, at, :] = jnp.broadcast_to(
            jnp.sum(pick * gate[:, None, :], axis=-1, keepdims=True), (local, CAP, LANES)
        )
        pick = pick.reshape(local * CAP, BLOCK).astype(jnp.bfloat16)
        picks_ref[p] = pick
        taken = jnp.dot(pick, x, preferred_element_type=jnp.float32)
        rows_ref[:, at, :] = taken.astype(jnp.bfloat16).reshape(local, CAP, width)
        hots.append(hot)
        probs.append(prob)
    if n_row:
        bal_ref = refs[3]
        for d in range(NDOC):
            counts = jnp.zeros((EXPERTS, BLOCK), jnp.float32)
            mass = jnp.zeros((EXPERTS, BLOCK), jnp.float32)
            for p in range(n_row):
                inside = seg_ref[p] == d
                counts = counts + jnp.where(inside, hots[p], 0.0)
                mass = mass + jnp.where(inside, probs[p], 0.0)
            both = jnp.sum(counts, axis=1, keepdims=True) * jnp.sum(mass, axis=1, keepdims=True)
            bal_ref[d : d + 1, :] = (
                jnp.broadcast_to(jnp.sum(both, axis=0, keepdims=True), (1, LANES))
                * scale_ref[d : d + 1, :]
            )


IN_HBM = pl.BlockSpec(memory_space=pltpu.HBM)
ANYWHERE = pl.BlockSpec(memory_space=pl.ANY)


def whole(a):
    return pl.BlockSpec(a.shape, lambda *i: (0,) * a.ndim)


def dispatch(parts, top, base, rw, local, row=None, after=()):
    n_parts = len(parts)
    n, width = parts[0].shape[0] // (BLOCK + EXTRA), rw.shape[1]
    slots = n_parts * CAP
    in_specs = [
        pl.BlockSpec(memory_space=pltpu.SMEM),
        whole(rw),
    ] + [pl.BlockSpec((BLOCK + EXTRA, width), lambda i: (i, 0))] * n_parts
    in_specs += [ANYWHERE] * len(after)
    out_specs = [
        pl.BlockSpec((local, slots, width), lambda i: (0, i, 0)),
        pl.BlockSpec((local, slots, LANES), lambda i: (0, i, 0)),
        pl.BlockSpec((n_parts, local * CAP, BLOCK), lambda i: (i, 0, 0)),
    ]
    out_shape = [
        jax.ShapeDtypeStruct((local, n * slots, width), jnp.bfloat16),
        jax.ShapeDtypeStruct((local, n * slots, LANES), jnp.float32),
        jax.ShapeDtypeStruct((n * n_parts, local * CAP, BLOCK), jnp.bfloat16),
    ]
    extra = ()
    if row is not None:
        extra = row
        in_specs += [whole(a) for a in row]
        out_specs.append(pl.BlockSpec((NDOC, LANES), lambda i: (0, 0)))
        out_shape.append(jax.ShapeDtypeStruct((NDOC, LANES), jnp.float32))
    return call(
        functools.partial(dispatch_kernel, n_parts, n_parts if row is not None else 0, top, len(after)),
        3 * n,
        (n,),
        in_specs,
        out_specs,
        out_shape,
        [],
        "dispatch",
    )(base, rw, *parts, *after, *extra)


def fetch(sources, slots, sem, step, steps, first, start=0):
    depth, group = slots[0].shape[:2]

    def copies(at):
        slot = lax.rem(at, depth)
        return [
            pltpu.make_async_copy(
                source.at[start + at * group + e], held.at[slot, e], sem.at[i, slot, e]
            )
            for i, (source, held) in enumerate(zip(sources, slots))
            for e in range(group)
        ]

    @pl.when(first & (step == 0))
    def _():
        for ahead in range(depth - 1):

            @pl.when(ahead < steps)
            def _():
                for copy in copies(step + ahead):
                    copy.start()

    @pl.when(first & (step + depth - 1 < steps))
    def _():
        for copy in copies(step + depth - 1):
            copy.start()

    @pl.when(first)
    def _():
        for copy in copies(step):
            copy.wait()

    return lax.rem(step, depth)


def sort_kernel(start, gu_ref, *refs):
    out_ref, held, made, wide, in_sem, out_sem = refs[-6:]
    step, steps = pl.program_id(0), pl.num_programs(0)
    _, group, _, hidden, width = made.shape
    chunks = width // LANES
    slot = fetch([gu_ref], [held], in_sem, step, steps, step >= 0, start)
    to = lax.rem(step, 2)

    def leave(at):
        to = lax.rem(at, 2)
        return pltpu.make_async_copy(
            made.at[to], out_ref.at[pl.ds(start + at * group, group)], out_sem.at[to]
        )

    @pl.when(step >= 2)
    def _():
        leave(step - 2).wait()

    for e in range(group):
        wide[e] = held[slot, e].astype(jnp.float32)
        for z in range(2):
            for c in range(chunks):
                part = wide[e, pl.ds(2 * c + z, hidden, stride=2 * chunks), :]
                made[to, e, z, :, c * LANES : (c + 1) * LANES] = part.astype(jnp.bfloat16)
    leave(step).start()

    @pl.when(step == steps - 1)
    def _():
        @pl.when(step >= 1)
        def _():
            leave(step - 1).wait()

        leave(step).wait()


def sort_rows(gate_up, behind):
    local, hidden, _, width = gate_up.shape
    pieces = PIECES if local % (2 * PIECES) == 0 else 1
    group = 2 if local % 2 == 0 else 1
    chunks = width // LANES
    gu = gate_up.reshape(local, hidden, 2, chunks, LANES).swapaxes(2, 3)
    gu = gu.reshape(local, hidden * 2 * chunks, LANES)
    done = ()
    for j in range(pieces):
        after = behind[j] if pieces > 1 else ()
        done = (
            call(
                functools.partial(sort_kernel, j * local // pieces),
                4,
                (local // pieces // group,),
                [IN_HBM] + [IN_HBM] * len(done) + [ANYWHERE] * len(after),
                IN_HBM,
                jax.ShapeDtypeStruct((local, 2, hidden, width), jnp.bfloat16),
                [
                    pltpu.VMEM((2, group) + gu.shape[1:], jnp.bfloat16),
                    pltpu.VMEM((2, group, 2, hidden, width), jnp.bfloat16),
                    pltpu.VMEM((group,) + gu.shape[1:], jnp.float32),
                    pltpu.SemaphoreType.DMA((1, 2, group)),
                    pltpu.SemaphoreType.DMA((2,)),
                ],
                "sort",
                VMEM_SORT,
                {1: 0} if done else {},
            )(gu, *done, *after),
        )
    return done[0]


def expert_kernel(n, *refs):
    rows, weights = refs[:n], refs[n : 2 * n]
    gu_ref, down_ref = refs[2 * n : 2 * n + 2]
    outs, (gu, down, sem) = refs[-3 - n : -3], refs[-3:]
    group = gu.shape[1]
    size = rows[0].shape[1]
    slot = fetch(
        [gu_ref, down_ref],
        [gu, down],
        sem,
        pl.program_id(0),
        pl.num_programs(0),
        pl.program_id(1) == 0,
    )
    for e in range(group):
        held = jnp.concatenate([r[e] for r in rows], axis=0)
        g = lax.dot_general(held, gu[slot, e, 0], NT, preferred_element_type=jnp.float32)
        u = lax.dot_general(held, gu[slot, e, 1], NT, preferred_element_type=jnp.float32)
        inner = (g * lax.logistic(g) * u).astype(jnp.bfloat16)
        made = jnp.dot(inner, down[slot, e], preferred_element_type=jnp.float32)
        for i in range(n):
            w = weights[i][e]
            part = made[i * size : (i + 1) * size]
            for c in range(part.shape[1] // LANES):
                at = slice(c * LANES, (c + 1) * LANES)
                outs[i][e, :, at] = (part[:, at] * w).astype(jnp.bfloat16)


def experts(rows, weights, gu, down, after=()):
    n = len(rows)
    local, slots, width = rows[0].shape
    size = min(slots, EXPERT_ROWS)
    hidden = down.shape[1]
    group = 2 if local % 2 == 0 else 1
    rows_spec = pl.BlockSpec((group, size, width), lambda e, i: (e, i, 0))
    weight_spec = pl.BlockSpec((group, size, LANES), lambda e, i: (e, i, 0))
    return call(
        functools.partial(expert_kernel, n),
        6,
        (local // group, slots // size),
        [rows_spec] * n + [weight_spec] * n + [IN_HBM, IN_HBM] + [ANYWHERE] * len(after),
        [rows_spec] * n,
        [jax.ShapeDtypeStruct(r.shape, jnp.bfloat16) for r in rows],
        [
            pltpu.VMEM((DEPTH, group, 2, hidden, width), jnp.bfloat16),
            pltpu.VMEM((DEPTH, group, hidden, width), jnp.bfloat16),
            pltpu.SemaphoreType.DMA((2, DEPTH, group)),
        ],
        "experts",
        VMEM_EXPERTS,
    )(*rows, *weights, gu, down, *after)


def combine_kernel(n, *refs):
    picks, made, outs = refs[:n], refs[n : 2 * n], refs[-2:]
    local, _, width = made[0].shape
    parts = picks[0].shape[0]
    half = parts // 2
    for i in range(n):
        for p in range(parts):
            held = made[i][:, p * CAP : (p + 1) * CAP, :].reshape(local * CAP, width)
            mix = lax.dot_general(picks[i][p], held, TN, preferred_element_type=jnp.float32)
            at = ((p % half) * n + i) * BLOCK
            outs[p // half][0, at : at + BLOCK, :] = mix.astype(jnp.bfloat16)


def combine(picks, made, n_parts, after=()):
    n = len(picks)
    steps = picks[0].shape[0] // n_parts
    local, _, width = made[0].shape
    half = n_parts // 2 * n * BLOCK
    out = pl.BlockSpec((1, half, width), lambda i: (i, 0, 0))
    return call(
        functools.partial(combine_kernel, n),
        2 * steps,
        (steps,),
        [pl.BlockSpec((n_parts,) + picks[0].shape[1:], lambda i: (i, 0, 0))] * n
        + [pl.BlockSpec((local, n_parts * CAP, width), lambda i: (0, i, 0))] * n
        + [ANYWHERE] * len(after),
        [out, out],
        [jax.ShapeDtypeStruct((steps, half, width), jnp.bfloat16)] * 2,
        [],
        "combine",
    )(*picks, *made, *after)


def attend_kernel(n, kdim, first_ref, last_ref, kpos_ref, q_ref, *refs):
    parts, (out_ref, even, odd) = refs[:n], refs[n:]
    rows = q_ref.shape[0]
    start = max(parts[0].shape[1] - even.shape[1], 0)
    wide = even.shape[1]
    half = wide - kdim

    @pl.when(pl.program_id(0) == 0)
    def _():
        pad = jnp.zeros((rows, half), jnp.bfloat16)
        for i in range(n):
            at = slice(i * rows, (i + 1) * rows)
            keys = parts[i][:rows, start : start + kdim]
            even[at, :] = jnp.concatenate([keys, pad], axis=1)
            odd[at, :] = jnp.concatenate([pad, keys], axis=1)

    allowed = (kpos_ref[...] >= first_ref[...]) & (kpos_ref[...] <= last_ref[...])
    for i, keys in enumerate((even, odd)):
        at = i * (kdim - half)
        scores = lax.dot_general(
            q_ref[:, at : at + wide], keys[...], NT, preferred_element_type=jnp.float32
        )
        scores = jnp.where(allowed, scores * qk_scale, -1e30)
        expo = jnp.exp(scores - jnp.max(scores, axis=-1, keepdims=True))
        probs = (expo / jnp.sum(expo, axis=-1, keepdims=True)).astype(jnp.bfloat16)
        out_ref[:, i * LATENT : (i + 1) * LATENT] = jnp.dot(
            probs, even[:, :LATENT], preferred_element_type=jnp.float32
        ).astype(jnp.bfloat16)


def attend(queries, parts, first, last, kpos):
    n = len(parts)
    rows, kdim = queries.shape[0], queries.shape[1] // HEADS
    wide = -(-kdim // LANES) * LANES
    return call(
        functools.partial(attend_kernel, n, kdim),
        6,
        (HEADS // 2,),
        [whole(first), whole(last), whole(kpos)]
        + [pl.BlockSpec((rows, 2 * kdim), lambda h: (0, h))]
        + [whole(p) for p in parts],
        pl.BlockSpec((rows, 2 * LATENT), lambda h: (0, h)),
        jax.ShapeDtypeStruct((rows, HEADS * LATENT), jnp.bfloat16),
        [pltpu.VMEM((n * rows, wide), jnp.bfloat16)] * 2,
        "attention",
    )(first, last, kpos, queries, *parts)


def added(*terms):
    total = terms[0].astype(jnp.float32)
    for term in terms[1:]:
        total = total + term.astype(jnp.float32)
    return total.astype(jnp.bfloat16)


def shards(queries, latent_kv, doc_lengths, hidden_in, router_weight, expert_ids, gate_up, w_down):
    tok_rows, width = hidden_in.shape[1:]
    n_ctx, n_exp = lax.axis_size("ctx"), lax.axis_size("exp")
    ctx, exp = lax.axis_index("ctx"), lax.axis_index("exp")
    local = gate_up.shape[0]
    near = n_exp <= 4
    shifts = [0, 1, 3, 2][:n_exp] if near else [0]
    flips = (2, 1)
    tokens = hidden_in[0]

    def flip(a, bit):
        return lax.ppermute(a, "ctx", [(i, i ^ bit) for i in range(n_ctx)])

    def shift(a, d):
        return lax.ppermute(a, "exp", [(i, (i + d) % n_exp) for i in range(n_exp)])

    def along_exp(a):
        if near:
            return [a if d == 0 else shift(a, d) for d in shifts]
        return [lax.all_gather(a, "exp", axis=0, tiled=True)]

    masks = [0, 2, 1, 3]
    order = jnp.stack([ctx ^ m for m in masks])

    top = expert_ids.shape[2]
    picks = expert_ids[0].T.astype(jnp.bfloat16).reshape(1, top * tok_rows)
    picks = jnp.pad(picks, ((0, EXTRA - 1), (0, width - top * tok_rows)))
    packed = jnp.concatenate([tokens, picks], axis=0)

    near_parts = along_exp(packed)
    arrived = list(near_parts)
    if near:
        kdim = latent_kv.shape[2]
        keys = jnp.pad(latent_kv[0], ((0, EXTRA), (0, -kdim % LANES)))
        near_parts[0] = jnp.concatenate([packed, keys], axis=1)
    spread = [[a] for a in near_parts]
    spread = [held + [flip(a, 2) for a in held] for held in spread]
    behind = [(), (), (), ()]
    if len(shifts) == 4:
        behind = [(), (arrived[1],), (arrived[2],), (spread[0][1],)]
    spread = [held + [flip(a, 1) for a in held] for held in spread]
    if near:
        kv = spread[0]
    else:
        kv = [latent_kv[0]]
        for bit in flips:
            kv = kv + [flip(a, bit) for a in kv]

    lengths = doc_lengths[0]
    ends = jnp.cumsum(lengths)
    row_pos = order[:, None] * tok_rows + jnp.arange(tok_rows, dtype=jnp.int32)[None, :]
    pos = row_pos[0]
    passed = pos[:, None] >= ends[None, :]
    first = jnp.max(jnp.where(passed, ends[None, :], 0), axis=1)
    context = attend(queries[0], kv, first[:, None], pos[:, None], row_pos.reshape(1, -1))

    seg = jnp.sum((row_pos[..., None] >= ends).astype(jnp.int32), axis=-1)
    sizes = lengths.astype(jnp.float32)
    scale = jnp.broadcast_to((EXPERTS / (top * sizes * sizes))[:, None], (NDOC, LANES))

    base = (exp * local).reshape(1).astype(jnp.int32)
    rw = jnp.roll(router_weight.T, -exp * local, axis=0)
    balance = None
    gu = sort_rows(gate_up, behind)
    groups = [[1, 2], [3, 0]] if len(shifts) == 4 else [range(len(shifts))]
    back, before, begun, far = [], (), [], []
    for n, group in enumerate(groups):
        sent = []
        for i in group:
            row = (seg.reshape(-1, 1, BLOCK), scale) if near and i == 0 else None
            out = dispatch(spread[i], top, base, rw, local, row, before if i else ())
            sent.append(out[:3])
            if row is not None:
                balance = out[3]
        if n + 1 < len(groups):
            after = (arrived[groups[n + 1][0]],)
        else:
            after = begun
        made = experts([a[0] for a in sent], [a[1] for a in sent], gu, w_down, after)
        before = (made[0],)
        keep, give = combine([a[2] for a in sent], made, n_ctx, tuple(far))
        got = flip(give, 1)
        size = len(group) * tok_rows
        last = n + 1 == len(groups)
        cuts = [slice(j * tok_rows, (j + 1) * tok_rows) for j in range(len(group))]
        crossing = cuts if last else [slice(0, size)]
        far = [added(keep[:, size + c.start : size + c.stop], got[:, size + c.start : size + c.stop]) for c in crossing]
        begun = far
        far = [flip(a, 2) for a in far]
        for j, i in enumerate(group):
            crossed = far[j] if last else far[0][:, cuts[j]]
            terms = [keep[:, cuts[j]], got[:, cuts[j]], crossed]
            if i:
                back.append(shift(added(*terms), -shifts[i]))
            else:
                back = back + terms
    if near:
        expert_mix = added(*back)
    else:
        expert_mix = lax.psum_scatter(
            added(*back).reshape(-1, width), "exp", scatter_dimension=0, tiled=True
        ).reshape(1, tok_rows, width)

    if balance is None:
        row = lax.all_gather(tokens, "ctx", axis=0, tiled=True)
        router = jax.nn.softmax(
            jnp.dot(row, router_weight, preferred_element_type=jnp.float32), axis=-1
        )
        row_ids = lax.all_gather(expert_ids[0], "ctx", axis=0, tiled=True)
        hot = (row_ids[:, :, None] == jnp.arange(EXPERTS, dtype=jnp.int32)).astype(jnp.float32)
        at = jnp.arange(row.shape[0], dtype=jnp.int32)
        seg_at = jnp.sum((at[:, None] >= ends[None, :]).astype(jnp.int32), axis=1)
        seg_hot = (seg_at[:, None] == jnp.arange(NDOC, dtype=jnp.int32)).astype(jnp.float32)
        exact = lax.Precision.HIGHEST
        counts = jnp.dot(seg_hot.T, hot.sum(axis=1), precision=exact)
        mass = jnp.dot(seg_hot.T, router, precision=exact)
        per_doc = jnp.sum(counts * mass, axis=1) * scale[:, 0]
    else:
        per_doc = balance[:, 0]
    return context[None], expert_mix, per_doc.reshape(1, NDOC)


def solution(mesh):
    rows = P(("group", "exp"), "ctx", None)
    docs = P(("group", "exp"), None)
    return jax.shard_map(
        shards,
        mesh=mesh,
        in_specs=(rows, rows, docs, rows, P(), rows, P("exp", "ctx", None, None), P("exp", "ctx", None)),
        out_specs=(rows, rows, docs),
        check_vma=False,
    )
```

```python
import functools

import jax
import jax.numpy as jnp
from jax import lax
from jax.experimental import pallas as pl
from jax.experimental.pallas import tpu as pltpu
from jax.sharding import PartitionSpec as P

EXPERTS = 64
HEADS = 8
LATENT = 512
CAP = 16
NDOC = 8
BLOCK = 128
LANES = 128
EXPERT_ROWS = 256
EXTRA = 16
VMEM = 14 * 2**20
VMEM_EXPERTS = 36 * 2**20
VMEM_SORT = 52 * 2**20
PIECES = 4
DEPTH = 3
PEAK = 1.1e9

qk_scale = 192.0 ** (-0.5)
NT = (((1,), (1,)), ((), ()))
TN = (((0,), (0,)), ((), ()))


def call(kernel, micros, grid, in_specs, out_specs, out_shape, scratch, name, limit=VMEM, aliases={}):
    return pl.pallas_call(
        kernel,
        grid=grid,
        in_specs=in_specs,
        out_specs=out_specs,
        out_shape=out_shape,
        scratch_shapes=scratch,
        input_output_aliases=aliases,
        compiler_params=pltpu.CompilerParams(
            dimension_semantics=("arbitrary",) * len(grid), vmem_limit_bytes=limit
        ),
        cost_estimate=pl.CostEstimate(
            flops=int(micros * PEAK), bytes_accessed=0, transcendentals=0
        ),
        name=name,
    )


def dispatch_kernel(n_parts, n_row, top, n_after, base_ref, rw_ref, *refs):
    parts, refs = refs[:n_parts], refs[n_parts + n_after :]
    if n_row:
        seg_ref, scale_ref = refs[:2]
        refs = refs[2:]
    rows_ref, weight_ref, picks_ref = refs[:3]
    local = rows_ref.shape[0]
    width = rows_ref.shape[2]
    names = lax.broadcasted_iota(jnp.int32, (EXPERTS, BLOCK), 0).astype(jnp.float32)
    base = base_ref[0].astype(jnp.float32)
    before = (
        lax.broadcasted_iota(jnp.int32, (BLOCK, BLOCK), 0)
        < lax.broadcasted_iota(jnp.int32, (BLOCK, BLOCK), 1)
    ).astype(jnp.bfloat16)
    slot = lax.broadcasted_iota(jnp.int32, (local, CAP, BLOCK), 1).astype(jnp.float32)
    hots, probs = [], []
    for p in range(n_parts):
        x = parts[p][:BLOCK, :]
        ids = parts[p][BLOCK : BLOCK + EXTRA, :].astype(jnp.float32)[0:1] - base
        ids = jnp.where(ids < 0.0, ids + EXPERTS, ids)
        logits = lax.dot_general(rw_ref[...], x, NT, preferred_element_type=jnp.float32)
        expo = jnp.exp(logits - jnp.max(logits, axis=0, keepdims=True))
        prob = expo / jnp.sum(expo, axis=0, keepdims=True)
        hot = names == ids[:, :BLOCK]
        for k in range(1, top):
            hot = hot | (names == ids[:, k * BLOCK : (k + 1) * BLOCK])
        hot = hot.astype(jnp.float32)
        chosen = prob * hot
        gate = chosen[:local] / jnp.sum(chosen, axis=0, keepdims=True)
        own = hot[:local]
        rank = jnp.dot(own.astype(jnp.bfloat16), before, preferred_element_type=jnp.float32)
        key = jnp.where(own > 0.0, rank, -1.0)
        pick = (key[:, None, :] == slot).astype(jnp.float32)
        at = slice(p * CAP, (p + 1) * CAP)
        weight_ref[:, at, :] = jnp.broadcast_to(
            jnp.sum(pick * gate[:, None, :], axis=-1, keepdims=True), (local, CAP, LANES)
        )
        pick = pick.reshape(local * CAP, BLOCK).astype(jnp.bfloat16)
        picks_ref[p] = pick
        taken = jnp.dot(pick, x, preferred_element_type=jnp.float32)
        rows_ref[:, at, :] = taken.astype(jnp.bfloat16).reshape(local, CAP, width)
        hots.append(hot)
        probs.append(prob)
    if n_row:
        bal_ref = refs[3]
        for d in range(NDOC):
            counts = jnp.zeros((EXPERTS, BLOCK), jnp.float32)
            mass = jnp.zeros((EXPERTS, BLOCK), jnp.float32)
            for p in range(n_row):
                inside = seg_ref[p] == d
                counts = counts + jnp.where(inside, hots[p], 0.0)
                mass = mass + jnp.where(inside, probs[p], 0.0)
            both = jnp.sum(counts, axis=1, keepdims=True) * jnp.sum(mass, axis=1, keepdims=True)
            bal_ref[d : d + 1, :] = (
                jnp.broadcast_to(jnp.sum(both, axis=0, keepdims=True), (1, LANES))
                * scale_ref[d : d + 1, :]
            )


IN_HBM = pl.BlockSpec(memory_space=pltpu.HBM)
ANYWHERE = pl.BlockSpec(memory_space=pl.ANY)


def whole(a):
    return pl.BlockSpec(a.shape, lambda *i: (0,) * a.ndim)


def dispatch(parts, top, base, rw, local, row=None, after=()):
    n_parts = len(parts)
    n, width = parts[0].shape[0] // (BLOCK + EXTRA), rw.shape[1]
    slots = n_parts * CAP
    in_specs = [
        pl.BlockSpec(memory_space=pltpu.SMEM),
        whole(rw),
    ] + [pl.BlockSpec((BLOCK + EXTRA, width), lambda i: (i, 0))] * n_parts
    in_specs += [ANYWHERE] * len(after)
    out_specs = [
        pl.BlockSpec((local, slots, width), lambda i: (0, i, 0)),
        pl.BlockSpec((local, slots, LANES), lambda i: (0, i, 0)),
        pl.BlockSpec((n_parts, local * CAP, BLOCK), lambda i: (i, 0, 0)),
    ]
    out_shape = [
        jax.ShapeDtypeStruct((local, n * slots, width), jnp.bfloat16),
        jax.ShapeDtypeStruct((local, n * slots, LANES), jnp.float32),
        jax.ShapeDtypeStruct((n * n_parts, local * CAP, BLOCK), jnp.bfloat16),
    ]
    extra = ()
    if row is not None:
        extra = row
        in_specs += [whole(a) for a in row]
        out_specs.append(pl.BlockSpec((NDOC, LANES), lambda i: (0, 0)))
        out_shape.append(jax.ShapeDtypeStruct((NDOC, LANES), jnp.float32))
    return call(
        functools.partial(dispatch_kernel, n_parts, n_parts if row is not None else 0, top, len(after)),
        3 * n,
        (n,),
        in_specs,
        out_specs,
        out_shape,
        [],
        "dispatch",
    )(base, rw, *parts, *after, *extra)


def fetch(sources, slots, sem, step, steps, first, start=0):
    depth, group = slots[0].shape[:2]

    def copies(at):
        slot = lax.rem(at, depth)
        return [
            pltpu.make_async_copy(
                source.at[start + at * group + e], held.at[slot, e], sem.at[i, slot, e]
            )
            for i, (source, held) in enumerate(zip(sources, slots))
            for e in range(group)
        ]

    @pl.when(first & (step == 0))
    def _():
        for ahead in range(depth - 1):

            @pl.when(ahead < steps)
            def _():
                for copy in copies(step + ahead):
                    copy.start()

    @pl.when(first & (step + depth - 1 < steps))
    def _():
        for copy in copies(step + depth - 1):
            copy.start()

    @pl.when(first)
    def _():
        for copy in copies(step):
            copy.wait()

    return lax.rem(step, depth)


def sort_kernel(start, gu_ref, *refs):
    out_ref, held, made, wide, in_sem, out_sem = refs[-6:]
    step, steps = pl.program_id(0), pl.num_programs(0)
    _, group, _, hidden, width = made.shape
    chunks = width // LANES
    slot = fetch([gu_ref], [held], in_sem, step, steps, step >= 0, start)
    to = lax.rem(step, 2)

    def leave(at):
        to = lax.rem(at, 2)
        return pltpu.make_async_copy(
            made.at[to], out_ref.at[pl.ds(start + at * group, group)], out_sem.at[to]
        )

    @pl.when(step >= 2)
    def _():
        leave(step - 2).wait()

    for e in range(group):
        wide[e] = held[slot, e].astype(jnp.float32)
        for z in range(2):
            for c in range(chunks):
                part = wide[e, pl.ds(2 * c + z, hidden, stride=2 * chunks), :]
                made[to, e, z, :, c * LANES : (c + 1) * LANES] = part.astype(jnp.bfloat16)
    leave(step).start()

    @pl.when(step == steps - 1)
    def _():
        @pl.when(step >= 1)
        def _():
            leave(step - 1).wait()

        leave(step).wait()


def sort_rows(gate_up, behind):
    local, hidden, _, width = gate_up.shape
    pieces = PIECES if local % (2 * PIECES) == 0 else 1
    group = 2 if local % 2 == 0 else 1
    chunks = width // LANES
    gu = gate_up.reshape(local, hidden, 2, chunks, LANES).swapaxes(2, 3)
    gu = gu.reshape(local, hidden * 2 * chunks, LANES)
    done = ()
    for j in range(pieces):
        after = behind[j] if pieces > 1 else ()
        done = (
            call(
                functools.partial(sort_kernel, j * local // pieces),
                4,
                (local // pieces // group,),
                [IN_HBM] + [IN_HBM] * len(done) + [ANYWHERE] * len(after),
                IN_HBM,
                jax.ShapeDtypeStruct((local, 2, hidden, width), jnp.bfloat16),
                [
                    pltpu.VMEM((2, group) + gu.shape[1:], jnp.bfloat16),
                    pltpu.VMEM((2, group, 2, hidden, width), jnp.bfloat16),
                    pltpu.VMEM((group,) + gu.shape[1:], jnp.float32),
                    pltpu.SemaphoreType.DMA((1, 2, group)),
                    pltpu.SemaphoreType.DMA((2,)),
                ],
                "sort",
                VMEM_SORT,
                {1: 0} if done else {},
            )(gu, *done, *after),
        )
    return done[0]


def expert_kernel(n, *refs):
    rows, weights = refs[:n], refs[n : 2 * n]
    gu_ref, down_ref = refs[2 * n : 2 * n + 2]
    outs, (gu, down, sem) = refs[-3 - n : -3], refs[-3:]
    group = gu.shape[1]
    size = rows[0].shape[1]
    slot = fetch(
        [gu_ref, down_ref],
        [gu, down],
        sem,
        pl.program_id(0),
        pl.num_programs(0),
        pl.program_id(1) == 0,
    )
    for e in range(group):
        held = jnp.concatenate([r[e] for r in rows], axis=0)
        g = lax.dot_general(held, gu[slot, e, 0], NT, preferred_element_type=jnp.float32)
        u = lax.dot_general(held, gu[slot, e, 1], NT, preferred_element_type=jnp.float32)
        inner = (g * lax.logistic(g) * u).astype(jnp.bfloat16)
        made = jnp.dot(inner, down[slot, e], preferred_element_type=jnp.float32)
        for i in range(n):
            w = weights[i][e]
            part = made[i * size : (i + 1) * size]
            for c in range(part.shape[1] // LANES):
                at = slice(c * LANES, (c + 1) * LANES)
                outs[i][e, :, at] = (part[:, at] * w).astype(jnp.bfloat16)


def experts(rows, weights, gu, down, after=()):
    n = len(rows)
    local, slots, width = rows[0].shape
    size = min(slots, EXPERT_ROWS)
    hidden = down.shape[1]
    group = 2 if local % 2 == 0 else 1
    rows_spec = pl.BlockSpec((group, size, width), lambda e, i: (e, i, 0))
    weight_spec = pl.BlockSpec((group, size, LANES), lambda e, i: (e, i, 0))
    return call(
        functools.partial(expert_kernel, n),
        6,
        (local // group, slots // size),
        [rows_spec] * n + [weight_spec] * n + [IN_HBM, IN_HBM] + [ANYWHERE] * len(after),
        [rows_spec] * n,
        [jax.ShapeDtypeStruct(r.shape, jnp.bfloat16) for r in rows],
        [
            pltpu.VMEM((DEPTH, group, 2, hidden, width), jnp.bfloat16),
            pltpu.VMEM((DEPTH, group, hidden, width), jnp.bfloat16),
            pltpu.SemaphoreType.DMA((2, DEPTH, group)),
        ],
        "experts",
        VMEM_EXPERTS,
    )(*rows, *weights, gu, down, *after)


def combine_kernel(n, *refs):
    picks, made, outs = refs[:n], refs[n : 2 * n], refs[-2:]
    local, _, width = made[0].shape
    parts = picks[0].shape[0]
    half = parts // 2
    for i in range(n):
        for p in range(parts):
            held = made[i][:, p * CAP : (p + 1) * CAP, :].reshape(local * CAP, width)
            mix = lax.dot_general(picks[i][p], held, TN, preferred_element_type=jnp.float32)
            at = ((p % half) * n + i) * BLOCK
            outs[p // half][0, at : at + BLOCK, :] = mix.astype(jnp.bfloat16)


def combine(picks, made, n_parts, after=()):
    n = len(picks)
    steps = picks[0].shape[0] // n_parts
    local, _, width = made[0].shape
    half = n_parts // 2 * n * BLOCK
    out = pl.BlockSpec((1, half, width), lambda i: (i, 0, 0))
    return call(
        functools.partial(combine_kernel, n),
        2 * steps,
        (steps,),
        [pl.BlockSpec((n_parts,) + picks[0].shape[1:], lambda i: (i, 0, 0))] * n
        + [pl.BlockSpec((local, n_parts * CAP, width), lambda i: (0, i, 0))] * n
        + [ANYWHERE] * len(after),
        [out, out],
        [jax.ShapeDtypeStruct((steps, half, width), jnp.bfloat16)] * 2,
        [],
        "combine",
    )(*picks, *made, *after)


def attend_kernel(n, kdim, first_ref, last_ref, kpos_ref, q_ref, *refs):
    parts, (out_ref, even, odd) = refs[:n], refs[n:]
    rows = q_ref.shape[0]
    start = max(parts[0].shape[1] - even.shape[1], 0)
    wide = even.shape[1]
    half = wide - kdim

    @pl.when(pl.program_id(0) == 0)
    def _():
        pad = jnp.zeros((rows, half), jnp.bfloat16)
        for i in range(n):
            at = slice(i * rows, (i + 1) * rows)
            keys = parts[i][:rows, start : start + kdim]
            even[at, :] = jnp.concatenate([keys, pad], axis=1)
            odd[at, :] = jnp.concatenate([pad, keys], axis=1)

    allowed = (kpos_ref[...] >= first_ref[...]) & (kpos_ref[...] <= last_ref[...])
    for i, keys in enumerate((even, odd)):
        at = i * (kdim - half)
        scores = lax.dot_general(
            q_ref[:, at : at + wide], keys[...], NT, preferred_element_type=jnp.float32
        )
        scores = jnp.where(allowed, scores * qk_scale, -1e30)
        expo = jnp.exp(scores - jnp.max(scores, axis=-1, keepdims=True))
        probs = (expo / jnp.sum(expo, axis=-1, keepdims=True)).astype(jnp.bfloat16)
        out_ref[:, i * LATENT : (i + 1) * LATENT] = jnp.dot(
            probs, even[:, :LATENT], preferred_element_type=jnp.float32
        ).astype(jnp.bfloat16)


def attend(queries, parts, first, last, kpos):
    n = len(parts)
    rows, kdim = queries.shape[0], queries.shape[1] // HEADS
    wide = -(-kdim // LANES) * LANES
    return call(
        functools.partial(attend_kernel, n, kdim),
        6,
        (HEADS // 2,),
        [whole(first), whole(last), whole(kpos)]
        + [pl.BlockSpec((rows, 2 * kdim), lambda h: (0, h))]
        + [whole(p) for p in parts],
        pl.BlockSpec((rows, 2 * LATENT), lambda h: (0, h)),
        jax.ShapeDtypeStruct((rows, HEADS * LATENT), jnp.bfloat16),
        [pltpu.VMEM((n * rows, wide), jnp.bfloat16)] * 2,
        "attention",
    )(first, last, kpos, queries, *parts)


def added(*terms):
    total = terms[0].astype(jnp.float32)
    for term in terms[1:]:
        total = total + term.astype(jnp.float32)
    return total.astype(jnp.bfloat16)


def shards(queries, latent_kv, doc_lengths, hidden_in, router_weight, expert_ids, gate_up, w_down):
    tok_rows, width = hidden_in.shape[1:]
    n_ctx, n_exp = lax.axis_size("ctx"), lax.axis_size("exp")
    ctx, exp = lax.axis_index("ctx"), lax.axis_index("exp")
    local = gate_up.shape[0]
    near = n_exp == 4
    shifts = [0, 1, 3, 2] if near else [0]
    flips = (2, 1)
    tokens = hidden_in[0]

    def flip(a, bit):
        return lax.ppermute(a, "ctx", [(i, i ^ bit) for i in range(n_ctx)])

    def shift(a, d):
        return lax.ppermute(a, "exp", [(i, i ^ d) for i in range(n_exp)])

    def along_exp(a):
        if near:
            beside, across = shift(a, 1), shift(a, 3)
            return [a, beside, across, shift(across, 1)]
        return [lax.all_gather(a, "exp", axis=0, tiled=True)]

    masks = [0, 2, 1, 3]
    order = jnp.stack([ctx ^ m for m in masks])

    top = expert_ids.shape[2]
    picks = expert_ids[0].T.astype(jnp.bfloat16).reshape(1, top * tok_rows)
    picks = jnp.pad(picks, ((0, EXTRA - 1), (0, width - top * tok_rows)))
    packed = jnp.concatenate([tokens, picks], axis=0)

    near_parts = along_exp(packed)
    arrived = list(near_parts)
    if near:
        kdim = latent_kv.shape[2]
        keys = jnp.pad(latent_kv[0], ((0, EXTRA), (0, -kdim % LANES)))
        near_parts[0] = jnp.concatenate([packed, keys], axis=1)
    spread = [[a] for a in near_parts]
    spread = [held + [flip(a, 2) for a in held] for held in spread]
    behind = [(), (), (), ()]
    if len(shifts) == 4:
        behind = [(), (arrived[1],), (arrived[2],), (arrived[3],)]
    spread = [held + [flip(a, 1) for a in held] for held in spread]
    if near:
        kv = spread[0]
    else:
        kv = [latent_kv[0]]
        for bit in flips:
            kv = kv + [flip(a, bit) for a in kv]

    lengths = doc_lengths[0]
    ends = jnp.cumsum(lengths)
    row_pos = order[:, None] * tok_rows + jnp.arange(tok_rows, dtype=jnp.int32)[None, :]
    pos = row_pos[0]
    passed = pos[:, None] >= ends[None, :]
    first = jnp.max(jnp.where(passed, ends[None, :], 0), axis=1)
    context = attend(queries[0], kv, first[:, None], pos[:, None], row_pos.reshape(1, -1))

    seg = jnp.sum((row_pos[..., None] >= ends).astype(jnp.int32), axis=-1)
    sizes = lengths.astype(jnp.float32)
    scale = jnp.broadcast_to((EXPERTS / (top * sizes * sizes))[:, None], (NDOC, LANES))

    base = (exp * local).reshape(1).astype(jnp.int32)
    rw = jnp.roll(router_weight.T, -exp * local, axis=0)
    balance = None
    gu = sort_rows(gate_up, behind)
    groups = [[1, 2], [3, 0]] if len(shifts) == 4 else [range(len(shifts))]
    back, before, begun, far = [], (), [], []
    late = (spread[3][1],) if near else ()
    for n, group in enumerate(groups):
        sent = []
        for i in group:
            row = (seg.reshape(-1, 1, BLOCK), scale) if near and i == 0 else None
            out = dispatch(spread[i], top, base, rw, local, row, before if i else ())
            sent.append(out[:3])
            if row is not None:
                balance = out[3]
        if n + 1 < len(groups):
            after = (arrived[groups[n + 1][0]],)
        else:
            after = begun
        made = experts([a[0] for a in sent], [a[1] for a in sent], gu, w_down, after)
        before = (made[0],)
        keep, give = combine([a[2] for a in sent], made, n_ctx, tuple(far) if n else late)
        got = flip(give, 1)
        size = len(group) * tok_rows
        last = n + 1 == len(groups)
        cuts = [slice(j * tok_rows, (j + 1) * tok_rows) for j in range(len(group))]
        crossing = cuts if last else [slice(0, size)]
        far = [added(keep[:, size + c.start : size + c.stop], got[:, size + c.start : size + c.stop]) for c in crossing]
        begun = far
        far = [flip(a, 2) for a in far]
        for j, i in enumerate(group):
            crossed = far[j] if last else far[0][:, cuts[j]]
            terms = [keep[:, cuts[j]], got[:, cuts[j]], crossed]
            if i:
                back.append(shift(added(*terms), shifts[i]))
            else:
                back = back + terms
    if near:
        expert_mix = added(*back)
    else:
        expert_mix = lax.psum_scatter(
            added(*back).reshape(-1, width), "exp", scatter_dimension=0, tiled=True
        ).reshape(1, tok_rows, width)

    if balance is None:
        row = lax.all_gather(tokens, "ctx", axis=0, tiled=True)
        router = jax.nn.softmax(
            jnp.dot(row, router_weight, preferred_element_type=jnp.float32), axis=-1
        )
        row_ids = lax.all_gather(expert_ids[0], "ctx", axis=0, tiled=True)
        hot = (row_ids[:, :, None] == jnp.arange(EXPERTS, dtype=jnp.int32)).astype(jnp.float32)
        at = jnp.arange(row.shape[0], dtype=jnp.int32)
        seg_at = jnp.sum((at[:, None] >= ends[None, :]).astype(jnp.int32), axis=1)
        seg_hot = (seg_at[:, None] == jnp.arange(NDOC, dtype=jnp.int32)).astype(jnp.float32)
        exact = lax.Precision.HIGHEST
        counts = jnp.dot(seg_hot.T, hot.sum(axis=1), precision=exact)
        mass = jnp.dot(seg_hot.T, router, precision=exact)
        per_doc = jnp.sum(counts * mass, axis=1) * scale[:, 0]
    else:
        per_doc = balance[:, 0]
    return context[None], expert_mix, per_doc.reshape(1, NDOC)


def solution(mesh):
    rows = P(("group", "exp"), "ctx", None)
    docs = P(("group", "exp"), None)
    return jax.shard_map(
        shards,
        mesh=mesh,
        in_specs=(rows, rows, docs, rows, P(), rows, P("exp", "ctx", None, None), P("exp", "ctx", None)),
        out_specs=(rows, rows, docs),
        check_vma=False,
    )
```

```python
import functools

import jax
import jax.numpy as jnp
from jax import lax
from jax.experimental import pallas as pl
from jax.experimental.pallas import tpu as pltpu
from jax.sharding import PartitionSpec as P

EXPERTS = 64
HEADS = 8
LATENT = 512
CAP = 16
NDOC = 8
BLOCK = 128
LANES = 128
EXPERT_ROWS = 256
EXTRA = 16
VMEM = 14 * 2**20
VMEM_EXPERTS = 24 * 2**20
VMEM_SORT = 52 * 2**20
PIECES = 4
DEPTH = 3
PEAK = 1.1e9

qk_scale = 192.0 ** (-0.5)
NT = (((1,), (1,)), ((), ()))
TN = (((0,), (0,)), ((), ()))


def call(kernel, micros, grid, in_specs, out_specs, out_shape, scratch, name, limit=VMEM, aliases={}):
    return pl.pallas_call(
        kernel,
        grid=grid,
        in_specs=in_specs,
        out_specs=out_specs,
        out_shape=out_shape,
        scratch_shapes=scratch,
        input_output_aliases=aliases,
        compiler_params=pltpu.CompilerParams(
            dimension_semantics=("arbitrary",) * len(grid), vmem_limit_bytes=limit
        ),
        cost_estimate=pl.CostEstimate(
            flops=int(micros * PEAK), bytes_accessed=0, transcendentals=0
        ),
        name=name,
    )


def dispatch_kernel(n_parts, n_row, top, n_after, base_ref, rw_ref, *refs):
    parts, refs = refs[:n_parts], refs[n_parts + n_after :]
    if n_row:
        seg_ref, scale_ref = refs[:2]
        refs = refs[2:]
    rows_ref, weight_ref, picks_ref = refs[:3]
    local = rows_ref.shape[0]
    width = rows_ref.shape[2]
    names = lax.broadcasted_iota(jnp.int32, (EXPERTS, BLOCK), 0).astype(jnp.float32)
    base = base_ref[0].astype(jnp.float32)
    before = (
        lax.broadcasted_iota(jnp.int32, (BLOCK, BLOCK), 0)
        < lax.broadcasted_iota(jnp.int32, (BLOCK, BLOCK), 1)
    ).astype(jnp.bfloat16)
    slot = lax.broadcasted_iota(jnp.int32, (local, CAP, BLOCK), 1).astype(jnp.float32)
    hots, probs = [], []
    for p in range(n_parts):
        x = parts[p][:BLOCK, :]
        ids = parts[p][BLOCK : BLOCK + EXTRA, :].astype(jnp.float32)[0:1] - base
        ids = jnp.where(ids < 0.0, ids + EXPERTS, ids)
        logits = lax.dot_general(rw_ref[...], x, NT, preferred_element_type=jnp.float32)
        expo = jnp.exp(logits - jnp.max(logits, axis=0, keepdims=True))
        prob = expo / jnp.sum(expo, axis=0, keepdims=True)
        hot = names == ids[:, :BLOCK]
        for k in range(1, top):
            hot = hot | (names == ids[:, k * BLOCK : (k + 1) * BLOCK])
        hot = hot.astype(jnp.float32)
        chosen = prob * hot
        gate = chosen[:local] / jnp.sum(chosen, axis=0, keepdims=True)
        own = hot[:local]
        rank = jnp.dot(own.astype(jnp.bfloat16), before, preferred_element_type=jnp.float32)
        key = jnp.where(own > 0.0, rank, -1.0)
        pick = (key[:, None, :] == slot).astype(jnp.float32)
        at = slice(p * CAP, (p + 1) * CAP)
        weight_ref[:, at, :] = jnp.broadcast_to(
            jnp.sum(pick * gate[:, None, :], axis=-1, keepdims=True), (local, CAP, LANES)
        )
        pick = pick.reshape(local * CAP, BLOCK).astype(jnp.bfloat16)
        picks_ref[p] = pick
        taken = jnp.dot(pick, x, preferred_element_type=jnp.float32)
        rows_ref[:, at, :] = taken.astype(jnp.bfloat16).reshape(local, CAP, width)
        hots.append(hot)
        probs.append(prob)
    if n_row:
        bal_ref = refs[3]
        for d in range(NDOC):
            counts = jnp.zeros((EXPERTS, BLOCK), jnp.float32)
            mass = jnp.zeros((EXPERTS, BLOCK), jnp.float32)
            for p in range(n_row):
                inside = seg_ref[p] == d
                counts = counts + jnp.where(inside, hots[p], 0.0)
                mass = mass + jnp.where(inside, probs[p], 0.0)
            both = jnp.sum(counts, axis=1, keepdims=True) * jnp.sum(mass, axis=1, keepdims=True)
            bal_ref[d : d + 1, :] = (
                jnp.broadcast_to(jnp.sum(both, axis=0, keepdims=True), (1, LANES))
                * scale_ref[d : d + 1, :]
            )


IN_HBM = pl.BlockSpec(memory_space=pltpu.HBM)
ANYWHERE = pl.BlockSpec(memory_space=pl.ANY)


def whole(a):
    return pl.BlockSpec(a.shape, lambda *i: (0,) * a.ndim)


def dispatch(parts, n, top, base, rw, local, row=None, after=()):
    n_parts = len(parts)
    width = rw.shape[1]
    slots = n_parts * CAP
    in_specs = [
        pl.BlockSpec(memory_space=pltpu.SMEM),
        whole(rw),
    ] + [
        pl.BlockSpec((BLOCK + EXTRA, width), lambda i, k=k: (k + i, 0)) for _, k in parts
    ]
    in_specs += [ANYWHERE] * len(after)
    out_specs = [
        pl.BlockSpec((local, slots, width), lambda i: (0, i, 0)),
        pl.BlockSpec((local, slots, LANES), lambda i: (0, i, 0)),
        pl.BlockSpec((n_parts, local * CAP, BLOCK), lambda i: (i, 0, 0)),
    ]
    out_shape = [
        jax.ShapeDtypeStruct((local, n * slots, width), jnp.bfloat16),
        jax.ShapeDtypeStruct((local, n * slots, LANES), jnp.float32),
        jax.ShapeDtypeStruct((n * n_parts, local * CAP, BLOCK), jnp.bfloat16),
    ]
    extra = ()
    if row is not None:
        extra = row
        in_specs += [whole(a) for a in row]
        out_specs.append(pl.BlockSpec((NDOC, LANES), lambda i: (0, 0)))
        out_shape.append(jax.ShapeDtypeStruct((NDOC, LANES), jnp.float32))
    return call(
        functools.partial(dispatch_kernel, n_parts, n_parts if row is not None else 0, top, len(after)),
        3 * n,
        (n,),
        in_specs,
        out_specs,
        out_shape,
        [],
        "dispatch",
    )(base, rw, *[a for a, _ in parts], *after, *extra)


def fetch(sources, slots, sem, step, steps, first, start=0):
    depth, group = slots[0].shape[:2]

    def copies(at):
        slot = lax.rem(at, depth)
        return [
            pltpu.make_async_copy(
                source.at[start + at * group + e], held.at[slot, e], sem.at[i, slot, e]
            )
            for i, (source, held) in enumerate(zip(sources, slots))
            for e in range(group)
        ]

    @pl.when(first & (step == 0))
    def _():
        for ahead in range(depth - 1):

            @pl.when(ahead < steps)
            def _():
                for copy in copies(step + ahead):
                    copy.start()

    @pl.when(first & (step + depth - 1 < steps))
    def _():
        for copy in copies(step + depth - 1):
            copy.start()

    @pl.when(first)
    def _():
        for copy in copies(step):
            copy.wait()

    return lax.rem(step, depth)


def sort_kernel(start, gu_ref, *refs):
    out_ref, held, made, wide, in_sem, out_sem = refs[-6:]
    step, steps = pl.program_id(0), pl.num_programs(0)
    _, group, _, hidden, width = made.shape
    chunks = width // LANES
    slot = fetch([gu_ref], [held], in_sem, step, steps, step >= 0, start)
    to = lax.rem(step, 2)

    def leave(at):
        to = lax.rem(at, 2)
        return pltpu.make_async_copy(
            made.at[to], out_ref.at[pl.ds(start + at * group, group)], out_sem.at[to]
        )

    @pl.when(step >= 2)
    def _():
        leave(step - 2).wait()

    for e in range(group):
        wide[e] = held[slot, e].astype(jnp.float32)
        for z in range(2):
            for c in range(chunks):
                part = wide[e, pl.ds(2 * c + z, hidden, stride=2 * chunks), :]
                made[to, e, z, :, c * LANES : (c + 1) * LANES] = part.astype(jnp.bfloat16)
    leave(step).start()

    @pl.when(step == steps - 1)
    def _():
        @pl.when(step >= 1)
        def _():
            leave(step - 1).wait()

        leave(step).wait()


def sort_rows(gate_up, behind):
    local, hidden, _, width = gate_up.shape
    pieces = PIECES if local % (2 * PIECES) == 0 else 1
    group = 2 if local % 2 == 0 else 1
    chunks = width // LANES
    gu = gate_up.reshape(local, hidden, 2, chunks, LANES).swapaxes(2, 3)
    gu = gu.reshape(local, hidden * 2 * chunks, LANES)
    done = ()
    for j in range(pieces):
        after = behind[j] if pieces > 1 else ()
        done = (
            call(
                functools.partial(sort_kernel, j * local // pieces),
                4,
                (local // pieces // group,),
                [IN_HBM] + [IN_HBM] * len(done) + [ANYWHERE] * len(after),
                IN_HBM,
                jax.ShapeDtypeStruct((local, 2, hidden, width), jnp.bfloat16),
                [
                    pltpu.VMEM((2, group) + gu.shape[1:], jnp.bfloat16),
                    pltpu.VMEM((2, group, 2, hidden, width), jnp.bfloat16),
                    pltpu.VMEM((group,) + gu.shape[1:], jnp.float32),
                    pltpu.SemaphoreType.DMA((1, 2, group)),
                    pltpu.SemaphoreType.DMA((2,)),
                ],
                "sort",
                VMEM_SORT,
                {1: 0} if done else {},
            )(gu, *done, *after),
        )
    return done[0]


def expert_kernel(n, *refs):
    rows, weights = refs[:n], refs[n : 2 * n]
    gu_ref, down_ref = refs[2 * n : 2 * n + 2]
    outs, (gu, down, sem) = refs[-3 - n : -3], refs[-3:]
    group = gu.shape[1]
    size = rows[0].shape[1]
    slot = fetch(
        [gu_ref, down_ref],
        [gu, down],
        sem,
        pl.program_id(0),
        pl.num_programs(0),
        pl.program_id(1) == 0,
    )
    for e in range(group):
        held = jnp.concatenate([r[e] for r in rows], axis=0)
        g = lax.dot_general(held, gu[slot, e, 0], NT, preferred_element_type=jnp.float32)
        u = lax.dot_general(held, gu[slot, e, 1], NT, preferred_element_type=jnp.float32)
        inner = (g * lax.logistic(g) * u).astype(jnp.bfloat16)
        made = jnp.dot(inner, down[slot, e], preferred_element_type=jnp.float32)
        for i in range(n):
            w = weights[i][e]
            part = made[i * size : (i + 1) * size]
            for c in range(part.shape[1] // LANES):
                at = slice(c * LANES, (c + 1) * LANES)
                outs[i][e, :, at] = (part[:, at] * w).astype(jnp.bfloat16)


def experts(rows, weights, gu, down, after=()):
    n = len(rows)
    local, slots, width = rows[0].shape
    size = min(slots, EXPERT_ROWS)
    hidden = down.shape[1]
    group = 2 if local % 2 == 0 else 1
    rows_spec = pl.BlockSpec((group, size, width), lambda e, i: (e, i, 0))
    weight_spec = pl.BlockSpec((group, size, LANES), lambda e, i: (e, i, 0))
    return call(
        functools.partial(expert_kernel, n),
        6,
        (local // group, slots // size),
        [rows_spec] * n + [weight_spec] * n + [IN_HBM, IN_HBM] + [ANYWHERE] * len(after),
        [rows_spec] * n,
        [jax.ShapeDtypeStruct(r.shape, jnp.bfloat16) for r in rows],
        [
            pltpu.VMEM((DEPTH, group, 2, hidden, width), jnp.bfloat16),
            pltpu.VMEM((DEPTH, group, hidden, width), jnp.bfloat16),
            pltpu.SemaphoreType.DMA((2, DEPTH, group)),
        ],
        "experts",
        VMEM_EXPERTS,
    )(*rows, *weights, gu, down, *after)


def combine_kernel(n, *refs):
    picks, made, outs = refs[:n], refs[n : 2 * n], refs[-2:]
    local, _, width = made[0].shape
    parts = picks[0].shape[0]
    half = parts // 2
    for i in range(n):
        for p in range(parts):
            held = made[i][:, p * CAP : (p + 1) * CAP, :].reshape(local * CAP, width)
            mix = lax.dot_general(picks[i][p], held, TN, preferred_element_type=jnp.float32)
            at = ((p % half) * n + i) * BLOCK
            outs[p // half][0, at : at + BLOCK, :] = mix.astype(jnp.bfloat16)


def combine(picks, made, n_parts, after=()):
    n = len(picks)
    steps = picks[0].shape[0] // n_parts
    local, _, width = made[0].shape
    half = n_parts // 2 * n * BLOCK
    out = pl.BlockSpec((1, half, width), lambda i: (i, 0, 0))
    return call(
        functools.partial(combine_kernel, n),
        2 * steps,
        (steps,),
        [pl.BlockSpec((n_parts,) + picks[0].shape[1:], lambda i: (i, 0, 0))] * n
        + [pl.BlockSpec((local, n_parts * CAP, width), lambda i: (0, i, 0))] * n
        + [ANYWHERE] * len(after),
        [out, out],
        [jax.ShapeDtypeStruct((steps, half, width), jnp.bfloat16)] * 2,
        [],
        "combine",
    )(*picks, *made, *after)


def attend_kernel(starts, kdim, first_ref, last_ref, kpos_ref, q_ref, *refs):
    n = len(starts)
    parts, (out_ref, even, odd) = refs[:n], refs[n:]
    rows = q_ref.shape[0]
    start = max(parts[0].shape[1] - even.shape[1], 0)
    wide = even.shape[1]
    half = wide - kdim

    @pl.when(pl.program_id(0) == 0)
    def _():
        pad = jnp.zeros((rows, half), jnp.bfloat16)
        for i in range(n):
            at = slice(i * rows, (i + 1) * rows)
            keys = parts[i][starts[i] : starts[i] + rows, start : start + kdim]
            even[at, :] = jnp.concatenate([keys, pad], axis=1)
            odd[at, :] = jnp.concatenate([pad, keys], axis=1)

    allowed = (kpos_ref[...] >= first_ref[...]) & (kpos_ref[...] <= last_ref[...])
    for i, keys in enumerate((even, odd)):
        at = i * (kdim - half)
        scores = lax.dot_general(
            q_ref[:, at : at + wide], keys[...], NT, preferred_element_type=jnp.float32
        )
        scores = jnp.where(allowed, scores * qk_scale, -1e30)
        expo = jnp.exp(scores - jnp.max(scores, axis=-1, keepdims=True))
        probs = (expo / jnp.sum(expo, axis=-1, keepdims=True)).astype(jnp.bfloat16)
        out_ref[:, i * LATENT : (i + 1) * LATENT] = jnp.dot(
            probs, even[:, :LATENT], preferred_element_type=jnp.float32
        ).astype(jnp.bfloat16)


def attend(queries, parts, first, last, kpos):
    n = len(parts)
    rows, kdim = queries.shape[0], queries.shape[1] // HEADS
    wide = -(-kdim // LANES) * LANES
    return call(
        functools.partial(attend_kernel, [at for _, at in parts], kdim),
        6,
        (HEADS // 2,),
        [whole(first), whole(last), whole(kpos)]
        + [pl.BlockSpec((rows, 2 * kdim), lambda h: (0, h))]
        + [whole(p) for p, _ in parts],
        pl.BlockSpec((rows, 2 * LATENT), lambda h: (0, h)),
        jax.ShapeDtypeStruct((rows, HEADS * LATENT), jnp.bfloat16),
        [pltpu.VMEM((n * rows, wide), jnp.bfloat16)] * 2,
        "attention",
    )(first, last, kpos, queries, *[p for p, _ in parts])


def added(*terms):
    total = terms[0].astype(jnp.float32)
    for term in terms[1:]:
        total = total + term.astype(jnp.float32)
    return total.astype(jnp.bfloat16)


def shards(queries, latent_kv, doc_lengths, hidden_in, router_weight, expert_ids, gate_up, w_down):
    tok_rows, width = hidden_in.shape[1:]
    n_ctx, n_exp = lax.axis_size("ctx"), lax.axis_size("exp")
    ctx, exp = lax.axis_index("ctx"), lax.axis_index("exp")
    local = gate_up.shape[0]
    near = n_exp == 4
    shifts = [0, 1, 3, 2] if near else [0]
    flips = (2, 1)
    tokens = hidden_in[0]

    def flip(a, bit):
        return lax.ppermute(a, "ctx", [(i, i ^ bit) for i in range(n_ctx)])

    def shift(a, d):
        return lax.ppermute(a, "exp", [(i, i ^ d) for i in range(n_exp)])

    def along_exp(a):
        if near:
            beside, across = shift(a, 1), shift(a, 3)
            return [a, beside, across, shift(across, 1)]
        return [lax.all_gather(a, "exp", axis=0, tiled=True)]

    masks = [0, 2, 1, 3]
    order = jnp.stack([ctx ^ m for m in masks])

    top = expert_ids.shape[2]
    picks = expert_ids[0].T.astype(jnp.bfloat16).reshape(1, top * tok_rows)
    picks = jnp.pad(picks, ((0, EXTRA - 1), (0, width - top * tok_rows)))
    packed = jnp.concatenate([tokens, picks], axis=0)

    near_parts = along_exp(packed)
    arrived = list(near_parts)
    if near:
        kdim = latent_kv.shape[2]
        keys = jnp.pad(latent_kv[0], ((0, EXTRA), (0, -kdim % LANES)))
        near_parts[0] = jnp.concatenate([packed, keys], axis=1)
    crossed = [flip(a, 2) for a in near_parts]
    if near:
        blocks = 1
        pairs = [jnp.concatenate([a, b], axis=0) for a, b in zip(near_parts, crossed)]
        flipped = [flip(a, 1) for a in pairs]
        spread = [[(a, 0), (a, 1), (b, 0), (b, 1)] for a, b in zip(pairs, flipped)]
        kv = [(a, k * (BLOCK + EXTRA)) for a, k in spread[0]]
    else:
        blocks = near_parts[0].shape[0] // (BLOCK + EXTRA)
        spread = [[(near_parts[0], 0), (crossed[0], 0)]]
        spread[0] = spread[0] + [(flip(a, 1), 0) for a, _ in spread[0]]
        kv = [latent_kv[0]]
        for bit in flips:
            kv = kv + [flip(a, bit) for a in kv]
        kv = [(a, 0) for a in kv]
    behind = [()] * PIECES
    if near:
        behind = [(), (arrived[1],), (arrived[2], crossed[0]), (arrived[3],)]

    lengths = doc_lengths[0]
    ends = jnp.cumsum(lengths)
    row_pos = order[:, None] * tok_rows + jnp.arange(tok_rows, dtype=jnp.int32)[None, :]
    pos = row_pos[0]
    passed = pos[:, None] >= ends[None, :]
    first = jnp.max(jnp.where(passed, ends[None, :], 0), axis=1)
    context = attend(queries[0], kv, first[:, None], pos[:, None], row_pos.reshape(1, -1))

    seg = jnp.sum((row_pos[..., None] >= ends).astype(jnp.int32), axis=-1)
    sizes = lengths.astype(jnp.float32)
    scale = jnp.broadcast_to((EXPERTS / (top * sizes * sizes))[:, None], (NDOC, LANES))

    base = (exp * local).reshape(1).astype(jnp.int32)
    rw = jnp.roll(router_weight.T, -exp * local, axis=0)
    balance = None
    gu = sort_rows(gate_up, behind)
    sent = []
    for i in range(len(shifts)):
        row = (seg.reshape(-1, 1, BLOCK), scale) if near and i == 0 else None
        out = dispatch(spread[i], blocks, top, base, rw, local, row)
        sent.append(out[:3])
        if row is not None:
            balance = out[3]
    made = experts([a[0] for a in sent], [a[1] for a in sent], gu, w_down)
    back = []
    for i in reversed(range(len(shifts))):
        keep, give = combine([sent[i][2]], [made[i]], n_ctx)
        got = flip(give, 1)
        far = added(keep[:, tok_rows:], got[:, tok_rows:])
        terms = [keep[:, :tok_rows], got[:, :tok_rows], flip(far, 2)]
        if i:
            back.append(shift(added(*terms), shifts[i]))
        else:
            back = back + terms
    if near:
        expert_mix = added(*back)
    else:
        expert_mix = lax.psum_scatter(
            added(*back).reshape(-1, width), "exp", scatter_dimension=0, tiled=True
        ).reshape(1, tok_rows, width)

    if balance is None:
        row = lax.all_gather(tokens, "ctx", axis=0, tiled=True)
        router = jax.nn.softmax(
            jnp.dot(row, router_weight, preferred_element_type=jnp.float32), axis=-1
        )
        row_ids = lax.all_gather(expert_ids[0], "ctx", axis=0, tiled=True)
        hot = (row_ids[:, :, None] == jnp.arange(EXPERTS, dtype=jnp.int32)).astype(jnp.float32)
        at = jnp.arange(row.shape[0], dtype=jnp.int32)
        seg_at = jnp.sum((at[:, None] >= ends[None, :]).astype(jnp.int32), axis=1)
        seg_hot = (seg_at[:, None] == jnp.arange(NDOC, dtype=jnp.int32)).astype(jnp.float32)
        exact = lax.Precision.HIGHEST
        counts = jnp.dot(seg_hot.T, hot.sum(axis=1), precision=exact)
        mass = jnp.dot(seg_hot.T, router, precision=exact)
        per_doc = jnp.sum(counts * mass, axis=1) * scale[:, 0]
    else:
        per_doc = balance[:, 0]
    return context[None], expert_mix, per_doc.reshape(1, NDOC)


def solution(mesh):
    rows = P(("group", "exp"), "ctx", None)
    docs = P(("group", "exp"), None)
    return jax.shard_map(
        shards,
        mesh=mesh,
        in_specs=(rows, rows, docs, rows, P(), rows, P("exp", "ctx", None, None), P("exp", "ctx", None)),
        out_specs=(rows, rows, docs),
        check_vma=False,
    )
```

```python
import functools

import jax
import jax.numpy as jnp
from jax import lax
from jax.experimental import pallas as pl
from jax.experimental.pallas import tpu as pltpu
from jax.sharding import PartitionSpec as P

EXPERTS = 64
HEADS = 8
LATENT = 512
CAP = 16
NDOC = 8
BLOCK = 128
LANES = 128
EXPERT_ROWS = 256
EXTRA = 16
VMEM = 14 * 2**20
VMEM_EXPERTS = 20 * 2**20
VMEM_SORT = 52 * 2**20
PIECES = 2
DEPTH = 3
PEAK = 1.1e9

qk_scale = 192.0 ** (-0.5)
NT = (((1,), (1,)), ((), ()))
TN = (((0,), (0,)), ((), ()))


def call(kernel, micros, grid, in_specs, out_specs, out_shape, scratch, name, limit=VMEM, aliases={}):
    return pl.pallas_call(
        kernel,
        grid=grid,
        in_specs=in_specs,
        out_specs=out_specs,
        out_shape=out_shape,
        scratch_shapes=scratch,
        input_output_aliases=aliases,
        compiler_params=pltpu.CompilerParams(
            dimension_semantics=("arbitrary",) * len(grid), vmem_limit_bytes=limit
        ),
        cost_estimate=pl.CostEstimate(
            flops=int(micros * PEAK), bytes_accessed=0, transcendentals=0
        ),
        name=name,
    )


def dispatch_kernel(n_parts, n_row, top, n_carried, base_ref, rw_ref, *refs):
    parts, carried, refs = refs[:n_parts], refs[n_parts : n_parts + n_carried], refs[n_parts + n_carried :]
    if n_row:
        seg_ref, scale_ref = refs[:2]
        refs = refs[2:]
    rows_ref, weight_ref, picks_ref = refs[:3]
    local = rows_ref.shape[0]
    width = rows_ref.shape[2]
    names = lax.broadcasted_iota(jnp.int32, (EXPERTS, BLOCK), 0).astype(jnp.float32)
    base = base_ref[0].astype(jnp.float32)
    before = (
        lax.broadcasted_iota(jnp.int32, (BLOCK, BLOCK), 0)
        < lax.broadcasted_iota(jnp.int32, (BLOCK, BLOCK), 1)
    ).astype(jnp.bfloat16)
    slot = lax.broadcasted_iota(jnp.int32, (local, CAP, BLOCK), 1).astype(jnp.float32)
    hots, probs = [], []
    for p in range(n_parts):
        x = parts[p][:BLOCK, :]
        ids = parts[p][BLOCK : BLOCK + EXTRA, :].astype(jnp.float32)[0:1] - base
        ids = jnp.where(ids < 0.0, ids + EXPERTS, ids)
        logits = lax.dot_general(rw_ref[...], x, NT, preferred_element_type=jnp.float32)
        expo = jnp.exp(logits - jnp.max(logits, axis=0, keepdims=True))
        prob = expo / jnp.sum(expo, axis=0, keepdims=True)
        hot = names == ids[:, :BLOCK]
        for k in range(1, top):
            hot = hot | (names == ids[:, k * BLOCK : (k + 1) * BLOCK])
        hot = hot.astype(jnp.float32)
        chosen = prob * hot
        gate = chosen[:local] / jnp.sum(chosen, axis=0, keepdims=True)
        own = hot[:local]
        rank = jnp.dot(own.astype(jnp.bfloat16), before, preferred_element_type=jnp.float32)
        key = jnp.where(own > 0.0, rank, -1.0)
        pick = (key[:, None, :] == slot).astype(jnp.float32)
        at = slice(p * CAP, (p + 1) * CAP)
        weight_ref[:, at, :] = jnp.broadcast_to(
            jnp.sum(pick * gate[:, None, :], axis=-1, keepdims=True), (local, CAP, LANES)
        )
        pick = pick.reshape(local * CAP, BLOCK).astype(jnp.bfloat16)
        picks_ref[p] = pick
        taken = jnp.dot(pick, x, preferred_element_type=jnp.float32)
        rows_ref[:, at, :] = taken.astype(jnp.bfloat16).reshape(local, CAP, width)
        hots.append(hot)
        probs.append(prob)
    for source, target in zip(carried, refs[len(refs) - n_carried :]):
        target[...] = source[...]
    if n_row:
        bal_ref = refs[3]
        for d in range(NDOC):
            counts = jnp.zeros((EXPERTS, BLOCK), jnp.float32)
            mass = jnp.zeros((EXPERTS, BLOCK), jnp.float32)
            for p in range(n_row):
                inside = seg_ref[p] == d
                counts = counts + jnp.where(inside, hots[p], 0.0)
                mass = mass + jnp.where(inside, probs[p], 0.0)
            both = jnp.sum(counts, axis=1, keepdims=True) * jnp.sum(mass, axis=1, keepdims=True)
            bal_ref[d : d + 1, :] = (
                jnp.broadcast_to(jnp.sum(both, axis=0, keepdims=True), (1, LANES))
                * scale_ref[d : d + 1, :]
            )


IN_HBM = pl.BlockSpec(memory_space=pltpu.HBM)
ANYWHERE = pl.BlockSpec(memory_space=pl.ANY)


def whole(a):
    return pl.BlockSpec(a.shape, lambda *i: (0,) * a.ndim)


def dispatch(parts, n, top, base, rw, local, row=None, carried=()):
    n_parts = len(parts)
    width = rw.shape[1]
    slots = n_parts * CAP
    in_specs = [
        pl.BlockSpec(memory_space=pltpu.SMEM),
        whole(rw),
    ] + [
        pl.BlockSpec((BLOCK + EXTRA, width), lambda i, k=k: (k + i, 0)) for _, k in parts
    ]
    in_specs += [whole(a) for a in carried]
    out_specs = [
        pl.BlockSpec((local, slots, width), lambda i: (0, i, 0)),
        pl.BlockSpec((local, slots, LANES), lambda i: (0, i, 0)),
        pl.BlockSpec((n_parts, local * CAP, BLOCK), lambda i: (i, 0, 0)),
    ]
    out_shape = [
        jax.ShapeDtypeStruct((local, n * slots, width), jnp.bfloat16),
        jax.ShapeDtypeStruct((local, n * slots, LANES), jnp.float32),
        jax.ShapeDtypeStruct((n * n_parts, local * CAP, BLOCK), jnp.bfloat16),
    ]
    extra = ()
    if row is not None:
        extra = row
        in_specs += [whole(a) for a in row]
        out_specs.append(pl.BlockSpec((NDOC, LANES), lambda i: (0, 0)))
        out_shape.append(jax.ShapeDtypeStruct((NDOC, LANES), jnp.float32))
    out_specs += [whole(a) for a in carried]
    out_shape += [jax.ShapeDtypeStruct(a.shape, a.dtype) for a in carried]
    return call(
        functools.partial(dispatch_kernel, n_parts, n_parts if row is not None else 0, top, len(carried)),
        3 * n,
        (n,),
        in_specs,
        out_specs,
        out_shape,
        [],
        "dispatch",
    )(base, rw, *[a for a, _ in parts], *carried, *extra)


def fetch(sources, slots, sem, step, steps, first, start=0):
    depth, group = slots[0].shape[:2]

    def copies(at):
        slot = lax.rem(at, depth)
        return [
            pltpu.make_async_copy(
                source.at[start + at * group + e], held.at[slot, e], sem.at[i, slot, e]
            )
            for i, (source, held) in enumerate(zip(sources, slots))
            for e in range(group)
        ]

    @pl.when(first & (step == 0))
    def _():
        for ahead in range(depth - 1):

            @pl.when(ahead < steps)
            def _():
                for copy in copies(step + ahead):
                    copy.start()

    @pl.when(first & (step + depth - 1 < steps))
    def _():
        for copy in copies(step + depth - 1):
            copy.start()

    @pl.when(first)
    def _():
        for copy in copies(step):
            copy.wait()

    return lax.rem(step, depth)


def sort_kernel(start, gu_ref, *refs):
    out_ref, token_ref, held, made, wide, in_sem, out_sem = refs[-7:]
    token_ref[...] = jnp.zeros_like(token_ref)
    step, steps = pl.program_id(0), pl.num_programs(0)
    _, group, _, hidden, width = made.shape
    chunks = width // LANES
    slot = fetch([gu_ref], [held], in_sem, step, steps, step >= 0, start)
    to = lax.rem(step, 2)

    def leave(at):
        to = lax.rem(at, 2)
        return pltpu.make_async_copy(
            made.at[to], out_ref.at[pl.ds(start + at * group, group)], out_sem.at[to]
        )

    @pl.when(step >= 2)
    def _():
        leave(step - 2).wait()

    for e in range(group):
        wide[e] = held[slot, e].astype(jnp.float32)
        for z in range(2):
            for c in range(chunks):
                part = wide[e, pl.ds(2 * c + z, hidden, stride=2 * chunks), :]
                made[to, e, z, :, c * LANES : (c + 1) * LANES] = part.astype(jnp.bfloat16)
    leave(step).start()

    @pl.when(step == steps - 1)
    def _():
        @pl.when(step >= 1)
        def _():
            leave(step - 1).wait()

        leave(step).wait()


def sort_rows(gate_up, behind):
    local, hidden, _, width = gate_up.shape
    pieces = PIECES if local % (2 * PIECES) == 0 else 1
    group = 1
    chunks = width // LANES
    gu = gate_up.reshape(local, hidden, 2, chunks, LANES).swapaxes(2, 3)
    gu = gu.reshape(local, hidden * 2 * chunks, LANES)
    done = ()
    for j in range(pieces):
        after = behind[j] if pieces > 1 else ()
        *done, token = (
            call(
                functools.partial(sort_kernel, j * local // pieces),
                8 // pieces,
                (local // pieces // group,),
                [IN_HBM] + [IN_HBM] * len(done) + [ANYWHERE] * len(after),
                [IN_HBM, pl.BlockSpec((8, LANES), lambda e: (0, 0))],
                [
                    jax.ShapeDtypeStruct((local, 2, hidden, width), jnp.bfloat16),
                    jax.ShapeDtypeStruct((8, LANES), jnp.float32),
                ],
                [
                    pltpu.VMEM((2, group) + gu.shape[1:], jnp.bfloat16),
                    pltpu.VMEM((2, group, 2, hidden, width), jnp.bfloat16),
                    pltpu.VMEM((group,) + gu.shape[1:], jnp.float32),
                    pltpu.SemaphoreType.DMA((1, 2, group)),
                    pltpu.SemaphoreType.DMA((2,)),
                ],
                "sort",
                VMEM_SORT,
                {1: 0} if done else {},
            )(gu, *done, *after)
        )
    return done[0], token


def stack_kernel(a_ref, b_ref, *refs):
    rows = a_ref.shape[0]
    refs[-1][:rows, :] = a_ref[...]
    refs[-1][rows:, :] = b_ref[...]


def stack(a, b, before):
    rows, width = a.shape
    return call(
        stack_kernel,
        1,
        (1,),
        [whole(a), whole(b)] + [ANYWHERE] * len(before),
        pl.BlockSpec((2 * rows, width), lambda i: (0, 0)),
        jax.ShapeDtypeStruct((2 * rows, width), a.dtype),
        [],
        "stack",
    )(a, b, *before)


def expert_kernel(n, *refs):
    rows, weights = refs[:n], refs[n : 2 * n]
    gu_ref, down_ref = refs[2 * n : 2 * n + 2]
    outs, (gu, down, sem) = refs[-3 - n : -3], refs[-3:]
    group = gu.shape[1]
    size = rows[0].shape[1]
    slot = fetch(
        [gu_ref, down_ref],
        [gu, down],
        sem,
        pl.program_id(0),
        pl.num_programs(0),
        pl.program_id(1) == 0,
    )
    for e in range(group):
        held = jnp.concatenate([r[e] for r in rows], axis=0)
        _, hidden, width = gu.shape[2:]
        both = gu[slot, e].reshape(2 * hidden, width)
        both = lax.dot_general(both, held, NT, preferred_element_type=jnp.float32)
        g, u = both[:hidden], both[hidden:]
        inner = (g * lax.logistic(g) * u).astype(jnp.bfloat16)
        made = lax.dot_general(inner, down[slot, e], TN, preferred_element_type=jnp.float32)
        for i in range(n):
            w = weights[i][e]
            part = made[i * size : (i + 1) * size]
            for c in range(part.shape[1] // LANES):
                at = slice(c * LANES, (c + 1) * LANES)
                outs[i][e, :, at] = (part[:, at] * w).astype(jnp.bfloat16)


def experts(rows, weights, gu, down, after=()):
    n = len(rows)
    local, slots, width = rows[0].shape
    size = min(slots, EXPERT_ROWS)
    hidden = down.shape[1]
    group = 2 if local % 2 == 0 else 1
    rows_spec = pl.BlockSpec((group, size, width), lambda e, i: (e, i, 0))
    weight_spec = pl.BlockSpec((group, size, LANES), lambda e, i: (e, i, 0))
    return call(
        functools.partial(expert_kernel, n),
        6,
        (local // group, slots // size),
        [rows_spec] * n + [weight_spec] * n + [IN_HBM, IN_HBM] + [ANYWHERE] * len(after),
        [rows_spec] * n,
        [jax.ShapeDtypeStruct(r.shape, jnp.bfloat16) for r in rows],
        [
            pltpu.VMEM((DEPTH, group, 2, hidden, width), jnp.bfloat16),
            pltpu.VMEM((DEPTH, group, hidden, width), jnp.bfloat16),
            pltpu.SemaphoreType.DMA((2, DEPTH, group)),
        ],
        "experts",
        VMEM_EXPERTS,
    )(*rows, *weights, gu, down, *after)


def combine_kernel(n, *refs):
    picks, made, outs = refs[:n], refs[n : 2 * n], refs[-2:]
    local, _, width = made[0].shape
    parts = picks[0].shape[0]
    half = parts // 2
    for i in range(n):
        for p in range(parts):
            held = made[i][:, p * CAP : (p + 1) * CAP, :].reshape(local * CAP, width)
            mix = lax.dot_general(picks[i][p], held, TN, preferred_element_type=jnp.float32)
            at = ((p % half) * n + i) * BLOCK
            outs[p // half][0, at : at + BLOCK, :] = mix.astype(jnp.bfloat16)


def combine(picks, made, n_parts, after=()):
    n = len(picks)
    steps = picks[0].shape[0] // n_parts
    local, _, width = made[0].shape
    half = n_parts // 2 * n * BLOCK
    out = pl.BlockSpec((1, half, width), lambda i: (i, 0, 0))
    return call(
        functools.partial(combine_kernel, n),
        2 * steps,
        (steps,),
        [pl.BlockSpec((n_parts,) + picks[0].shape[1:], lambda i: (i, 0, 0))] * n
        + [pl.BlockSpec((local, n_parts * CAP, width), lambda i: (0, i, 0))] * n
        + [ANYWHERE] * len(after),
        [out, out],
        [jax.ShapeDtypeStruct((steps, half, width), jnp.bfloat16)] * 2,
        [],
        "combine",
    )(*picks, *made, *after)


def attend_kernel(starts, kdim, first_ref, last_ref, kpos_ref, q_ref, *refs):
    n = len(starts)
    parts, (out_ref, even, odd) = refs[:n], refs[n:]
    rows = q_ref.shape[0]
    start = max(parts[0].shape[1] - even.shape[1], 0)
    wide = even.shape[1]
    half = wide - kdim

    @pl.when(pl.program_id(0) == 0)
    def _():
        pad = jnp.zeros((rows, half), jnp.bfloat16)
        for i in range(n):
            at = slice(i * rows, (i + 1) * rows)
            keys = parts[i][starts[i] : starts[i] + rows, start : start + kdim]
            even[at, :] = jnp.concatenate([keys, pad], axis=1)
            odd[at, :] = jnp.concatenate([pad, keys], axis=1)

    allowed = (kpos_ref[...] >= first_ref[...]) & (kpos_ref[...] <= last_ref[...])
    for i, keys in enumerate((even, odd)):
        at = i * (kdim - half)
        scores = lax.dot_general(
            q_ref[:, at : at + wide], keys[...], NT, preferred_element_type=jnp.float32
        )
        scores = jnp.where(allowed, scores * qk_scale, -1e30)
        expo = jnp.exp(scores - jnp.max(scores, axis=-1, keepdims=True))
        probs = (expo / jnp.sum(expo, axis=-1, keepdims=True)).astype(jnp.bfloat16)
        out_ref[:, i * LATENT : (i + 1) * LATENT] = jnp.dot(
            probs, even[:, :LATENT], preferred_element_type=jnp.float32
        ).astype(jnp.bfloat16)


def attend(queries, parts, first, last, kpos):
    n = len(parts)
    rows, kdim = queries.shape[0], queries.shape[1] // HEADS
    wide = -(-kdim // LANES) * LANES
    return call(
        functools.partial(attend_kernel, [at for _, at in parts], kdim),
        6,
        (HEADS // 2,),
        [whole(first), whole(last), whole(kpos)]
        + [pl.BlockSpec((rows, 2 * kdim), lambda h: (0, h))]
        + [whole(p) for p, _ in parts],
        pl.BlockSpec((rows, 2 * LATENT), lambda h: (0, h)),
        jax.ShapeDtypeStruct((rows, HEADS * LATENT), jnp.bfloat16),
        [pltpu.VMEM((n * rows, wide), jnp.bfloat16)] * 2,
        "attention",
    )(first, last, kpos, queries, *[p for p, _ in parts])


def added(*terms):
    total = terms[0].astype(jnp.float32)
    for term in terms[1:]:
        total = total + term.astype(jnp.float32)
    return total.astype(jnp.bfloat16)


def shards(queries, latent_kv, doc_lengths, hidden_in, router_weight, expert_ids, gate_up, w_down):
    tok_rows, width = hidden_in.shape[1:]
    n_ctx, n_exp = lax.axis_size("ctx"), lax.axis_size("exp")
    ctx, exp = lax.axis_index("ctx"), lax.axis_index("exp")
    local = gate_up.shape[0]
    near = n_exp == 4
    shifts = [0, 1, 3, 2] if near else [0]
    tokens = hidden_in[0]

    def flip(a, bit):
        return lax.ppermute(a, "ctx", [(i, i ^ bit) for i in range(n_ctx)])

    def shift(a, d):
        return lax.ppermute(a, "exp", [(i, i ^ d) for i in range(n_exp)])

    def along_exp(a):
        if near:
            beside, across = shift(a, 1), shift(a, 3)
            return [a, beside, across, shift(across, 1)]
        return [lax.all_gather(a, "exp", axis=0, tiled=True)]

    masks = [0, 2, 1, 3]
    order = jnp.stack([ctx ^ m for m in masks])

    top = expert_ids.shape[2]
    picks = expert_ids[0].T.astype(jnp.bfloat16).reshape(1, top * tok_rows)
    picks = jnp.pad(picks, ((0, EXTRA - 1), (0, width - top * tok_rows)))
    packed = jnp.concatenate([tokens, picks], axis=0)

    near_parts = along_exp(packed)
    arrived = list(near_parts)
    crossed = [flip(a, 2) for a in near_parts]
    if near:
        blocks = 1
        pairs = [jnp.concatenate([a, b], axis=0) for a, b in zip(near_parts[:-1], crossed[:-1])]
        flipped = [flip(a, 1) for a in pairs]
        spread = [[(a, 0), (a, 1), (b, 0), (b, 1)] for a, b in zip(pairs, flipped)]
    else:
        blocks = near_parts[0].shape[0] // (BLOCK + EXTRA)
        spread = [[(near_parts[0], 0), (crossed[0], 0)]]
        spread[0] = spread[0] + [(flip(a, 1), 0) for a, _ in spread[0]]

    lengths = doc_lengths[0]
    ends = jnp.cumsum(lengths)
    row_pos = order[:, None] * tok_rows + jnp.arange(tok_rows, dtype=jnp.int32)[None, :]
    pos = row_pos[0]
    passed = pos[:, None] >= ends[None, :]
    first = jnp.max(jnp.where(passed, ends[None, :], 0), axis=1)
    seg = jnp.sum((row_pos[..., None] >= ends).astype(jnp.int32), axis=-1)
    sizes = lengths.astype(jnp.float32)
    scale = jnp.broadcast_to((EXPERTS / (top * sizes * sizes))[:, None], (NDOC, LANES))

    base = (exp * local).reshape(1).astype(jnp.int32)
    rw = jnp.roll(router_weight.T, -exp * local, axis=0)
    balance = None
    gu, token = sort_rows(gate_up, [(), (arrived[2],)] if near else [(), ()])
    sent, keys = [], latent_kv[0]
    for i in range(len(shifts)):
        if near and i + 1 == len(shifts):
            before = [token] + [a[0] for a in sent]
            pair = stack(near_parts[i], crossed[i], before)
            flipped = flip(pair, 1)
            spread.append([(pair, 0), (pair, 1), (flipped, 0), (flipped, 1)])
        row = (seg.reshape(-1, 1, BLOCK), scale) if near and i == 0 else None
        carried = (keys,) if i + 1 == len(shifts) else ()
        out = dispatch(spread[i], blocks, top, base, rw, local, row, carried)
        sent.append(out[:3])
        if row is not None:
            balance = out[3]
        if carried:
            keys = out[-1]
    keys = jnp.concatenate([keys, flip(keys, 2)], axis=0)
    keys = [keys, flip(keys, 1)]
    made = experts([a[0] for a in sent], [a[1] for a in sent], gu, w_down)
    back = []
    for i in reversed(range(len(shifts))):
        keep, give = combine([sent[i][2]], [made[i]], n_ctx, () if i else (keys[1],))
        got = flip(give, 1)
        far = added(keep[:, tok_rows:], got[:, tok_rows:])
        terms = [keep[:, :tok_rows], got[:, :tok_rows], flip(far, 2)]
        if i:
            back.append(shift(added(*terms), shifts[i]))
        else:
            back = back + terms
    kv = [(a, k * tok_rows) for a in keys for k in range(2)]
    context = attend(queries[0], kv, first[:, None], pos[:, None], row_pos.reshape(1, -1))
    if near:
        expert_mix = added(*back)
    else:
        expert_mix = lax.psum_scatter(
            added(*back).reshape(-1, width), "exp", scatter_dimension=0, tiled=True
        ).reshape(1, tok_rows, width)

    if balance is None:
        row = lax.all_gather(tokens, "ctx", axis=0, tiled=True)
        router = jax.nn.softmax(
            jnp.dot(row, router_weight, preferred_element_type=jnp.float32), axis=-1
        )
        row_ids = lax.all_gather(expert_ids[0], "ctx", axis=0, tiled=True)
        hot = (row_ids[:, :, None] == jnp.arange(EXPERTS, dtype=jnp.int32)).astype(jnp.float32)
        at = jnp.arange(row.shape[0], dtype=jnp.int32)
        seg_at = jnp.sum((at[:, None] >= ends[None, :]).astype(jnp.int32), axis=1)
        seg_hot = (seg_at[:, None] == jnp.arange(NDOC, dtype=jnp.int32)).astype(jnp.float32)
        exact = lax.Precision.HIGHEST
        counts = jnp.dot(seg_hot.T, hot.sum(axis=1), precision=exact)
        mass = jnp.dot(seg_hot.T, router, precision=exact)
        per_doc = jnp.sum(counts * mass, axis=1) * scale[:, 0]
    else:
        per_doc = balance[:, 0]
    return context[None], expert_mix, per_doc.reshape(1, NDOC)


def solution(mesh):
    rows = P(("group", "exp"), "ctx", None)
    docs = P(("group", "exp"), None)
    return jax.shard_map(
        shards,
        mesh=mesh,
        in_specs=(rows, rows, docs, rows, P(), rows, P("exp", "ctx", None, None), P("exp", "ctx", None)),
        out_specs=(rows, rows, docs),
        check_vma=False,
    )
```

```python
import functools

import jax
import jax.numpy as jnp
from jax import lax
from jax.experimental import pallas as pl
from jax.experimental.pallas import tpu as pltpu
from jax.sharding import PartitionSpec as P

EXPERTS = 64
HEADS = 8
LATENT = 512
CAP = 16
NDOC = 8
BLOCK = 128
LANES = 128
EXPERT_ROWS = 256
EXTRA = 16
VMEM = 14 * 2**20
VMEM_EXPERTS = 20 * 2**20
PEAK = 1.1e9

qk_scale = 192.0 ** (-0.5)
NT = (((1,), (1,)), ((), ()))
TN = (((0,), (0,)), ((), ()))


def call(kernel, micros, grid, in_specs, out_specs, out_shape, scratch, name, limit=VMEM):
    return pl.pallas_call(
        kernel,
        grid=grid,
        in_specs=in_specs,
        out_specs=out_specs,
        out_shape=out_shape,
        scratch_shapes=scratch,
        compiler_params=pltpu.CompilerParams(
            dimension_semantics=("arbitrary",) * len(grid), vmem_limit_bytes=limit
        ),
        cost_estimate=pl.CostEstimate(
            flops=int(micros * PEAK), bytes_accessed=0, transcendentals=0
        ),
        name=name,
    )


def dispatch_kernel(n_parts, n_row, top, n_carried, base_ref, rw_ref, *refs):
    parts, carried, refs = refs[:n_parts], refs[n_parts : n_parts + n_carried], refs[n_parts + n_carried :]
    if n_row:
        seg_ref, scale_ref = refs[:2]
        refs = refs[2:]
    rows_ref, weight_ref, picks_ref = refs[:3]
    local = rows_ref.shape[0]
    width = rows_ref.shape[2]
    names = lax.broadcasted_iota(jnp.int32, (EXPERTS, BLOCK), 0).astype(jnp.float32)
    base = base_ref[0].astype(jnp.float32)
    before = (
        lax.broadcasted_iota(jnp.int32, (BLOCK, BLOCK), 0)
        < lax.broadcasted_iota(jnp.int32, (BLOCK, BLOCK), 1)
    ).astype(jnp.bfloat16)
    slot = lax.broadcasted_iota(jnp.int32, (local, CAP, BLOCK), 1).astype(jnp.float32)
    hots, probs = [], []
    for p in range(n_parts):
        x = parts[p][:BLOCK, :]
        ids = parts[p][BLOCK : BLOCK + EXTRA, :].astype(jnp.float32)[0:1] - base
        ids = jnp.where(ids < 0.0, ids + EXPERTS, ids)
        logits = lax.dot_general(rw_ref[...], x, NT, preferred_element_type=jnp.float32)
        expo = jnp.exp(logits - jnp.max(logits, axis=0, keepdims=True))
        prob = expo / jnp.sum(expo, axis=0, keepdims=True)
        hot = names == ids[:, :BLOCK]
        for k in range(1, top):
            hot = hot | (names == ids[:, k * BLOCK : (k + 1) * BLOCK])
        hot = hot.astype(jnp.float32)
        chosen = prob * hot
        gate = chosen[:local] / jnp.sum(chosen, axis=0, keepdims=True)
        own = hot[:local]
        rank = jnp.dot(own.astype(jnp.bfloat16), before, preferred_element_type=jnp.float32)
        key = jnp.where(own > 0.0, rank, -1.0)
        pick = (key[:, None, :] == slot).astype(jnp.float32)
        at = slice(p * CAP, (p + 1) * CAP)
        weight_ref[:, at, :] = jnp.broadcast_to(
            jnp.sum(pick * gate[:, None, :], axis=-1, keepdims=True), (local, CAP, LANES)
        )
        pick = pick.reshape(local * CAP, BLOCK).astype(jnp.bfloat16)
        picks_ref[p] = pick
        taken = jnp.dot(pick, x, preferred_element_type=jnp.float32)
        rows_ref[:, at, :] = taken.astype(jnp.bfloat16).reshape(local, CAP, width)
        hots.append(hot)
        probs.append(prob)
    for source, target in zip(carried, refs[len(refs) - n_carried :]):
        target[...] = source[...]
    if n_row:
        bal_ref = refs[3]
        for d in range(NDOC):
            counts = jnp.zeros((EXPERTS, BLOCK), jnp.float32)
            mass = jnp.zeros((EXPERTS, BLOCK), jnp.float32)
            for p in range(n_row):
                inside = seg_ref[p] == d
                counts = counts + jnp.where(inside, hots[p], 0.0)
                mass = mass + jnp.where(inside, probs[p], 0.0)
            both = jnp.sum(counts, axis=1, keepdims=True) * jnp.sum(mass, axis=1, keepdims=True)
            bal_ref[d : d + 1, :] = (
                jnp.broadcast_to(jnp.sum(both, axis=0, keepdims=True), (1, LANES))
                * scale_ref[d : d + 1, :]
            )


ANYWHERE = pl.BlockSpec(memory_space=pl.ANY)


def whole(a):
    return pl.BlockSpec(a.shape, lambda *i: (0,) * a.ndim)


def dispatch(parts, n, top, base, rw, local, row=None, carried=()):
    n_parts = len(parts)
    width = rw.shape[1]
    slots = n_parts * CAP
    in_specs = [
        pl.BlockSpec(memory_space=pltpu.SMEM),
        whole(rw),
    ] + [
        pl.BlockSpec((BLOCK + EXTRA, width), lambda i, k=k: (k + i, 0)) for _, k in parts
    ]
    in_specs += [whole(a) for a in carried]
    out_specs = [
        pl.BlockSpec((local, slots, width), lambda i: (0, i, 0)),
        pl.BlockSpec((local, slots, LANES), lambda i: (0, i, 0)),
        pl.BlockSpec((n_parts, local * CAP, BLOCK), lambda i: (i, 0, 0)),
    ]
    out_shape = [
        jax.ShapeDtypeStruct((local, n * slots, width), jnp.bfloat16),
        jax.ShapeDtypeStruct((local, n * slots, LANES), jnp.float32),
        jax.ShapeDtypeStruct((n * n_parts, local * CAP, BLOCK), jnp.bfloat16),
    ]
    extra = ()
    if row is not None:
        extra = row
        in_specs += [whole(a) for a in row]
        out_specs.append(pl.BlockSpec((NDOC, LANES), lambda i: (0, 0)))
        out_shape.append(jax.ShapeDtypeStruct((NDOC, LANES), jnp.float32))
    out_specs += [whole(a) for a in carried]
    out_shape += [jax.ShapeDtypeStruct(a.shape, a.dtype) for a in carried]
    return call(
        functools.partial(dispatch_kernel, n_parts, n_parts if row is not None else 0, top, len(carried)),
        3 * n,
        (n,),
        in_specs,
        out_specs,
        out_shape,
        [],
        "dispatch",
    )(base, rw, *[a for a, _ in parts], *carried, *extra)


def stack_kernel(a_ref, b_ref, *refs):
    rows = a_ref.shape[0]
    refs[-1][:rows, :] = a_ref[...]
    refs[-1][rows:, :] = b_ref[...]


def stack(a, b, before):
    rows, width = a.shape
    return call(
        stack_kernel,
        1,
        (1,),
        [whole(a), whole(b)] + [ANYWHERE] * len(before),
        pl.BlockSpec((2 * rows, width), lambda i: (0, 0)),
        jax.ShapeDtypeStruct((2 * rows, width), a.dtype),
        [],
        "stack",
    )(a, b, *before)


def expert_kernel(n, *refs):
    rows, weights = refs[:n], refs[n : 2 * n]
    gu_ref, down_ref = refs[2 * n : 2 * n + 2]
    outs, wide = refs[2 * n + 2 : 3 * n + 2], refs[3 * n + 2]
    group, hidden, width = down_ref.shape
    size = rows[0].shape[1]
    chunks = width // LANES
    for e in range(group):
        wide[e] = gu_ref[e].astype(jnp.float32)
        held = jnp.concatenate([r[e] for r in rows], axis=0)
        both = []
        for z in range(2):
            matrix = jnp.concatenate(
                [
                    wide[e, pl.ds(2 * c + z, hidden, stride=2 * chunks), :].astype(jnp.bfloat16)
                    for c in range(chunks)
                ],
                axis=1,
            )
            both.append(lax.dot_general(held, matrix, NT, preferred_element_type=jnp.float32))
        g, u = both
        inner = (g * lax.logistic(g) * u).astype(jnp.bfloat16)
        made = jnp.dot(inner, down_ref[e], preferred_element_type=jnp.float32)
        for i in range(n):
            w = weights[i][e]
            part = made[i * size : (i + 1) * size]
            for c in range(chunks):
                at = slice(c * LANES, (c + 1) * LANES)
                outs[i][e, :, at] = (part[:, at] * w).astype(jnp.bfloat16)


def experts(rows, weights, gate_up, down):
    n = len(rows)
    local, slots, width = rows[0].shape
    size = min(slots, EXPERT_ROWS)
    hidden = down.shape[1]
    group = 2 if local % 2 == 0 else 1
    chunks = width // LANES
    gu = gate_up.reshape(local, hidden, 2, chunks, LANES).swapaxes(2, 3)
    gu = gu.reshape(local, hidden * 2 * chunks, LANES)
    rows_spec = pl.BlockSpec((group, size, width), lambda e, i: (e, i, 0))
    weight_spec = pl.BlockSpec((group, size, LANES), lambda e, i: (e, i, 0))
    return call(
        functools.partial(expert_kernel, n),
        12,
        (local // group, slots // size),
        [rows_spec] * n
        + [weight_spec] * n
        + [
            pl.BlockSpec((group,) + gu.shape[1:], lambda e, i: (e, 0, 0)),
            pl.BlockSpec((group, hidden, width), lambda e, i: (e, 0, 0)),
        ],
        [rows_spec] * n,
        [jax.ShapeDtypeStruct(r.shape, jnp.bfloat16) for r in rows],
        [pltpu.VMEM((group,) + gu.shape[1:], jnp.float32)],
        "experts",
        VMEM_EXPERTS,
    )(*rows, *weights, gu, down)


def combine_kernel(n, *refs):
    picks, made, outs = refs[:n], refs[n : 2 * n], refs[-2:]
    local, _, width = made[0].shape
    parts = picks[0].shape[0]
    half = parts // 2
    for i in range(n):
        for p in range(parts):
            held = made[i][:, p * CAP : (p + 1) * CAP, :].reshape(local * CAP, width)
            mix = lax.dot_general(picks[i][p], held, TN, preferred_element_type=jnp.float32)
            at = ((p % half) * n + i) * BLOCK
            outs[p // half][0, at : at + BLOCK, :] = mix.astype(jnp.bfloat16)


def combine(picks, made, n_parts, after=()):
    n = len(picks)
    steps = picks[0].shape[0] // n_parts
    local, _, width = made[0].shape
    half = n_parts // 2 * n * BLOCK
    out = pl.BlockSpec((1, half, width), lambda i: (i, 0, 0))
    return call(
        functools.partial(combine_kernel, n),
        2 * steps,
        (steps,),
        [pl.BlockSpec((n_parts,) + picks[0].shape[1:], lambda i: (i, 0, 0))] * n
        + [pl.BlockSpec((local, n_parts * CAP, width), lambda i: (0, i, 0))] * n
        + [ANYWHERE] * len(after),
        [out, out],
        [jax.ShapeDtypeStruct((steps, half, width), jnp.bfloat16)] * 2,
        [],
        "combine",
    )(*picks, *made, *after)


def attend_kernel(starts, kdim, first_ref, last_ref, kpos_ref, q_ref, *refs):
    n = len(starts)
    parts, (out_ref, even, odd) = refs[:n], refs[n:]
    rows = q_ref.shape[0]
    start = max(parts[0].shape[1] - even.shape[1], 0)
    wide = even.shape[1]
    half = wide - kdim

    @pl.when(pl.program_id(0) == 0)
    def _():
        pad = jnp.zeros((rows, half), jnp.bfloat16)
        for i in range(n):
            at = slice(i * rows, (i + 1) * rows)
            keys = parts[i][starts[i] : starts[i] + rows, start : start + kdim]
            even[at, :] = jnp.concatenate([keys, pad], axis=1)
            odd[at, :] = jnp.concatenate([pad, keys], axis=1)

    allowed = (kpos_ref[...] >= first_ref[...]) & (kpos_ref[...] <= last_ref[...])
    for i, keys in enumerate((even, odd)):
        at = i * (kdim - half)
        scores = lax.dot_general(
            q_ref[:, at : at + wide], keys[...], NT, preferred_element_type=jnp.float32
        )
        scores = jnp.where(allowed, scores * qk_scale, -1e30)
        expo = jnp.exp(scores - jnp.max(scores, axis=-1, keepdims=True))
        probs = (expo / jnp.sum(expo, axis=-1, keepdims=True)).astype(jnp.bfloat16)
        out_ref[:, i * LATENT : (i + 1) * LATENT] = jnp.dot(
            probs, even[:, :LATENT], preferred_element_type=jnp.float32
        ).astype(jnp.bfloat16)


def attend(queries, parts, first, last, kpos):
    n = len(parts)
    rows, kdim = queries.shape[0], queries.shape[1] // HEADS
    wide = -(-kdim // LANES) * LANES
    return call(
        functools.partial(attend_kernel, [at for _, at in parts], kdim),
        6,
        (HEADS // 2,),
        [whole(first), whole(last), whole(kpos)]
        + [pl.BlockSpec((rows, 2 * kdim), lambda h: (0, h))]
        + [whole(p) for p, _ in parts],
        pl.BlockSpec((rows, 2 * LATENT), lambda h: (0, h)),
        jax.ShapeDtypeStruct((rows, HEADS * LATENT), jnp.bfloat16),
        [pltpu.VMEM((n * rows, wide), jnp.bfloat16)] * 2,
        "attention",
    )(first, last, kpos, queries, *[p for p, _ in parts])


def added(*terms):
    total = terms[0].astype(jnp.float32)
    for term in terms[1:]:
        total = total + term.astype(jnp.float32)
    return total.astype(jnp.bfloat16)


def shards(queries, latent_kv, doc_lengths, hidden_in, router_weight, expert_ids, gate_up, w_down):
    tok_rows, width = hidden_in.shape[1:]
    n_ctx, n_exp = lax.axis_size("ctx"), lax.axis_size("exp")
    ctx, exp = lax.axis_index("ctx"), lax.axis_index("exp")
    local = gate_up.shape[0]
    near = n_exp == 4
    shifts = [0, 1, 3, 2] if near else [0]
    tokens = hidden_in[0]

    def flip(a, bit):
        return lax.ppermute(a, "ctx", [(i, i ^ bit) for i in range(n_ctx)])

    def shift(a, d):
        return lax.ppermute(a, "exp", [(i, i ^ d) for i in range(n_exp)])

    def along_exp(a):
        if near:
            beside, across = shift(a, 1), shift(a, 3)
            return [a, beside, across, shift(across, 1)]
        return [lax.all_gather(a, "exp", axis=0, tiled=True)]

    masks = [0, 2, 1, 3]
    order = jnp.stack([ctx ^ m for m in masks])

    top = expert_ids.shape[2]
    picks = expert_ids[0].T.astype(jnp.bfloat16).reshape(1, top * tok_rows)
    picks = jnp.pad(picks, ((0, EXTRA - 1), (0, width - top * tok_rows)))
    packed = jnp.concatenate([tokens, picks], axis=0)

    near_parts = along_exp(packed)
    crossed = [flip(a, 2) for a in near_parts]
    if near:
        blocks = 1
        pairs = [jnp.concatenate([a, b], axis=0) for a, b in zip(near_parts[:-1], crossed[:-1])]
        flipped = [flip(a, 1) for a in pairs]
        spread = [[(a, 0), (a, 1), (b, 0), (b, 1)] for a, b in zip(pairs, flipped)]
    else:
        blocks = near_parts[0].shape[0] // (BLOCK + EXTRA)
        spread = [[(near_parts[0], 0), (crossed[0], 0)]]
        spread[0] = spread[0] + [(flip(a, 1), 0) for a, _ in spread[0]]

    lengths = doc_lengths[0]
    ends = jnp.cumsum(lengths)
    row_pos = order[:, None] * tok_rows + jnp.arange(tok_rows, dtype=jnp.int32)[None, :]
    pos = row_pos[0]
    passed = pos[:, None] >= ends[None, :]
    first = jnp.max(jnp.where(passed, ends[None, :], 0), axis=1)
    seg = jnp.sum((row_pos[..., None] >= ends).astype(jnp.int32), axis=-1)
    sizes = lengths.astype(jnp.float32)
    scale = jnp.broadcast_to((EXPERTS / (top * sizes * sizes))[:, None], (NDOC, LANES))

    base = (exp * local).reshape(1).astype(jnp.int32)
    rw = jnp.roll(router_weight.T, -exp * local, axis=0)
    balance = None
    sent, keys = [], latent_kv[0]
    for i in range(len(shifts)):
        if near and i + 1 == len(shifts):
            before = [a[0] for a in sent]
            pair = stack(near_parts[i], crossed[i], before)
            flipped = flip(pair, 1)
            spread.append([(pair, 0), (pair, 1), (flipped, 0), (flipped, 1)])
        row = (seg.reshape(-1, 1, BLOCK), scale) if near and i == 0 else None
        carried = (keys,) if i + 1 == len(shifts) else ()
        out = dispatch(spread[i], blocks, top, base, rw, local, row, carried)
        sent.append(out[:3])
        if row is not None:
            balance = out[3]
        if carried:
            keys = out[-1]
    keys = jnp.concatenate([keys, flip(keys, 2)], axis=0)
    keys = [keys, flip(keys, 1)]
    made = experts([a[0] for a in sent], [a[1] for a in sent], gate_up, w_down)
    back = []
    for i in reversed(range(len(shifts))):
        keep, give = combine([sent[i][2]], [made[i]], n_ctx, () if i else (keys[1],))
        got = flip(give, 1)
        far = added(keep[:, tok_rows:], got[:, tok_rows:])
        terms = [keep[:, :tok_rows], got[:, :tok_rows], flip(far, 2)]
        if i:
            back.append(shift(added(*terms), shifts[i]))
        else:
            back = back + terms
    kv = [(a, k * tok_rows) for a in keys for k in range(2)]
    context = attend(queries[0], kv, first[:, None], pos[:, None], row_pos.reshape(1, -1))
    if near:
        expert_mix = added(*back)
    else:
        expert_mix = lax.psum_scatter(
            added(*back).reshape(-1, width), "exp", scatter_dimension=0, tiled=True
        ).reshape(1, tok_rows, width)

    if balance is None:
        row = lax.all_gather(tokens, "ctx", axis=0, tiled=True)
        router = jax.nn.softmax(
            jnp.dot(row, router_weight, preferred_element_type=jnp.float32), axis=-1
        )
        row_ids = lax.all_gather(expert_ids[0], "ctx", axis=0, tiled=True)
        hot = (row_ids[:, :, None] == jnp.arange(EXPERTS, dtype=jnp.int32)).astype(jnp.float32)
        at = jnp.arange(row.shape[0], dtype=jnp.int32)
        seg_at = jnp.sum((at[:, None] >= ends[None, :]).astype(jnp.int32), axis=1)
        seg_hot = (seg_at[:, None] == jnp.arange(NDOC, dtype=jnp.int32)).astype(jnp.float32)
        exact = lax.Precision.HIGHEST
        counts = jnp.dot(seg_hot.T, hot.sum(axis=1), precision=exact)
        mass = jnp.dot(seg_hot.T, router, precision=exact)
        per_doc = jnp.sum(counts * mass, axis=1) * scale[:, 0]
    else:
        per_doc = balance[:, 0]
    return context[None], expert_mix, per_doc.reshape(1, NDOC)


def solution(mesh):
    rows = P(("group", "exp"), "ctx", None)
    docs = P(("group", "exp"), None)
    return jax.shard_map(
        shards,
        mesh=mesh,
        in_specs=(rows, rows, docs, rows, P(), rows, P("exp", "ctx", None, None), P("exp", "ctx", None)),
        out_specs=(rows, rows, docs),
        check_vma=False,
    )
```

```python
import functools

import jax
import jax.numpy as jnp
from jax import lax
from jax.experimental import pallas as pl
from jax.experimental.pallas import tpu as pltpu
from jax.sharding import PartitionSpec as P

EXPERTS = 64
HEADS = 8
LATENT = 512
CAP = 16
NDOC = 8
BLOCK = 128
LANES = 128
EXPERT_ROWS = 256
EXTRA = 16
VMEM = 14 * 2**20
VMEM_EXPERTS = 24 * 2**20
VMEM_SORT = 52 * 2**20
PIECES = 4
DEPTH = 3
PEAK = 1.1e9

qk_scale = 192.0 ** (-0.5)
NT = (((1,), (1,)), ((), ()))
TN = (((0,), (0,)), ((), ()))


def call(kernel, micros, grid, in_specs, out_specs, out_shape, scratch, name, limit=VMEM, aliases={}):
    return pl.pallas_call(
        kernel,
        grid=grid,
        in_specs=in_specs,
        out_specs=out_specs,
        out_shape=out_shape,
        scratch_shapes=scratch,
        input_output_aliases=aliases,
        compiler_params=pltpu.CompilerParams(
            dimension_semantics=("arbitrary",) * len(grid), vmem_limit_bytes=limit
        ),
        cost_estimate=pl.CostEstimate(
            flops=int(micros * PEAK), bytes_accessed=0, transcendentals=0
        ),
        name=name,
    )


def dispatch_kernel(n_parts, n_row, top, n_after, base_ref, rw_ref, *refs):
    parts, refs = refs[:n_parts], refs[n_parts + n_after :]
    if n_row:
        seg_ref, scale_ref = refs[:2]
        refs = refs[2:]
    rows_ref, weight_ref, picks_ref = refs[:3]
    local = rows_ref.shape[0]
    width = rows_ref.shape[2]
    names = lax.broadcasted_iota(jnp.int32, (EXPERTS, BLOCK), 0).astype(jnp.float32)
    base = base_ref[0].astype(jnp.float32)
    before = (
        lax.broadcasted_iota(jnp.int32, (BLOCK, BLOCK), 0)
        < lax.broadcasted_iota(jnp.int32, (BLOCK, BLOCK), 1)
    ).astype(jnp.bfloat16)
    slot = lax.broadcasted_iota(jnp.int32, (local, CAP, BLOCK), 1).astype(jnp.float32)
    hots, probs = [], []
    for p in range(n_parts):
        x = parts[p][:BLOCK, :]
        ids = parts[p][BLOCK : BLOCK + EXTRA, :].astype(jnp.float32)[0:1] - base
        ids = jnp.where(ids < 0.0, ids + EXPERTS, ids)
        logits = lax.dot_general(rw_ref[...], x, NT, preferred_element_type=jnp.float32)
        expo = jnp.exp(logits - jnp.max(logits, axis=0, keepdims=True))
        prob = expo / jnp.sum(expo, axis=0, keepdims=True)
        hot = names == ids[:, :BLOCK]
        for k in range(1, top):
            hot = hot | (names == ids[:, k * BLOCK : (k + 1) * BLOCK])
        hot = hot.astype(jnp.float32)
        chosen = prob * hot
        gate = chosen[:local] / jnp.sum(chosen, axis=0, keepdims=True)
        own = hot[:local]
        rank = jnp.dot(own.astype(jnp.bfloat16), before, preferred_element_type=jnp.float32)
        key = jnp.where(own > 0.0, rank, -1.0)
        pick = (key[:, None, :] == slot).astype(jnp.float32)
        at = slice(p * CAP, (p + 1) * CAP)
        weight_ref[:, at, :] = jnp.broadcast_to(
            jnp.sum(pick * gate[:, None, :], axis=-1, keepdims=True), (local, CAP, LANES)
        )
        pick = pick.reshape(local * CAP, BLOCK).astype(jnp.bfloat16)
        picks_ref[p] = pick
        taken = jnp.dot(pick, x, preferred_element_type=jnp.float32)
        rows_ref[:, at, :] = taken.astype(jnp.bfloat16).reshape(local, CAP, width)
        hots.append(hot)
        probs.append(prob)
    if n_row:
        bal_ref = refs[3]
        for d in range(NDOC):
            counts = jnp.zeros((EXPERTS, BLOCK), jnp.float32)
            mass = jnp.zeros((EXPERTS, BLOCK), jnp.float32)
            for p in range(n_row):
                inside = seg_ref[p] == d
                counts = counts + jnp.where(inside, hots[p], 0.0)
                mass = mass + jnp.where(inside, probs[p], 0.0)
            both = jnp.sum(counts, axis=1, keepdims=True) * jnp.sum(mass, axis=1, keepdims=True)
            bal_ref[d : d + 1, :] = (
                jnp.broadcast_to(jnp.sum(both, axis=0, keepdims=True), (1, LANES))
                * scale_ref[d : d + 1, :]
            )


IN_HBM = pl.BlockSpec(memory_space=pltpu.HBM)
ANYWHERE = pl.BlockSpec(memory_space=pl.ANY)


def whole(a):
    return pl.BlockSpec(a.shape, lambda *i: (0,) * a.ndim)


def dispatch(parts, n, top, base, rw, local, row=None, after=()):
    n_parts = len(parts)
    width = rw.shape[1]
    slots = n_parts * CAP
    in_specs = [
        pl.BlockSpec(memory_space=pltpu.SMEM),
        whole(rw),
    ] + [
        pl.BlockSpec((BLOCK + EXTRA, width), lambda i, k=k: (k + i, 0)) for _, k in parts
    ]
    in_specs += [ANYWHERE] * len(after)
    out_specs = [
        pl.BlockSpec((local, slots, width), lambda i: (0, i, 0)),
        pl.BlockSpec((local, slots, LANES), lambda i: (0, i, 0)),
        pl.BlockSpec((n_parts, local * CAP, BLOCK), lambda i: (i, 0, 0)),
    ]
    out_shape = [
        jax.ShapeDtypeStruct((local, n * slots, width), jnp.bfloat16),
        jax.ShapeDtypeStruct((local, n * slots, LANES), jnp.float32),
        jax.ShapeDtypeStruct((n * n_parts, local * CAP, BLOCK), jnp.bfloat16),
    ]
    extra = ()
    if row is not None:
        extra = row
        in_specs += [whole(a) for a in row]
        out_specs.append(pl.BlockSpec((NDOC, LANES), lambda i: (0, 0)))
        out_shape.append(jax.ShapeDtypeStruct((NDOC, LANES), jnp.float32))
    return call(
        functools.partial(dispatch_kernel, n_parts, n_parts if row is not None else 0, top, len(after)),
        3 * n,
        (n,),
        in_specs,
        out_specs,
        out_shape,
        [],
        "dispatch",
    )(base, rw, *[a for a, _ in parts], *after, *extra)


def fetch(sources, slots, sem, step, steps, first, start=0):
    depth, group = slots[0].shape[:2]

    def copies(at):
        slot = lax.rem(at, depth)
        return [
            pltpu.make_async_copy(
                source.at[start + at * group + e], held.at[slot, e], sem.at[i, slot, e]
            )
            for i, (source, held) in enumerate(zip(sources, slots))
            for e in range(group)
        ]

    @pl.when(first & (step == 0))
    def _():
        for ahead in range(depth - 1):

            @pl.when(ahead < steps)
            def _():
                for copy in copies(step + ahead):
                    copy.start()

    @pl.when(first & (step + depth - 1 < steps))
    def _():
        for copy in copies(step + depth - 1):
            copy.start()

    @pl.when(first)
    def _():
        for copy in copies(step):
            copy.wait()

    return lax.rem(step, depth)


def sort_kernel(start, gu_ref, *refs):
    out_ref, held, made, wide, in_sem, out_sem = refs[-6:]
    step, steps = pl.program_id(0), pl.num_programs(0)
    _, group, _, hidden, width = made.shape
    chunks = width // LANES
    slot = fetch([gu_ref], [held], in_sem, step, steps, step >= 0, start)
    to = lax.rem(step, 2)

    def leave(at):
        to = lax.rem(at, 2)
        return pltpu.make_async_copy(
            made.at[to], out_ref.at[pl.ds(start + at * group, group)], out_sem.at[to]
        )

    @pl.when(step >= 2)
    def _():
        leave(step - 2).wait()

    for e in range(group):
        wide[e] = held[slot, e].astype(jnp.float32)
        for z in range(2):
            for c in range(chunks):
                part = wide[e, pl.ds(2 * c + z, hidden, stride=2 * chunks), :]
                made[to, e, z, :, c * LANES : (c + 1) * LANES] = part.astype(jnp.bfloat16)
    leave(step).start()

    @pl.when(step == steps - 1)
    def _():
        @pl.when(step >= 1)
        def _():
            leave(step - 1).wait()

        leave(step).wait()


def sort_rows(gate_up, behind):
    local, hidden, _, width = gate_up.shape
    pieces = PIECES if local % (2 * PIECES) == 0 else 1
    group = 2 if local % 2 == 0 else 1
    chunks = width // LANES
    gu = gate_up.reshape(local, hidden, 2, chunks, LANES).swapaxes(2, 3)
    gu = gu.reshape(local, hidden * 2 * chunks, LANES)
    done = ()
    for j in range(pieces):
        after = behind[j] if pieces > 1 else ()
        done = (
            call(
                functools.partial(sort_kernel, j * local // pieces),
                4,
                (local // pieces // group,),
                [IN_HBM] + [IN_HBM] * len(done) + [ANYWHERE] * len(after),
                IN_HBM,
                jax.ShapeDtypeStruct((local, 2, hidden, width), jnp.bfloat16),
                [
                    pltpu.VMEM((2, group) + gu.shape[1:], jnp.bfloat16),
                    pltpu.VMEM((2, group, 2, hidden, width), jnp.bfloat16),
                    pltpu.VMEM((group,) + gu.shape[1:], jnp.float32),
                    pltpu.SemaphoreType.DMA((1, 2, group)),
                    pltpu.SemaphoreType.DMA((2,)),
                ],
                "sort",
                VMEM_SORT,
                {1: 0} if done else {},
            )(gu, *done, *after),
        )
    return done[0]


def expert_kernel(n, *refs):
    rows, weights = refs[:n], refs[n : 2 * n]
    gu_ref, down_ref = refs[2 * n : 2 * n + 2]
    outs, (gu, down, sem) = refs[-3 - n : -3], refs[-3:]
    group = gu.shape[1]
    size = rows[0].shape[1]
    slot = fetch(
        [gu_ref, down_ref],
        [gu, down],
        sem,
        pl.program_id(0),
        pl.num_programs(0),
        pl.program_id(1) == 0,
    )
    for e in range(group):
        held = jnp.concatenate([r[e] for r in rows], axis=0)
        g = lax.dot_general(held, gu[slot, e, 0], NT, preferred_element_type=jnp.float32)
        u = lax.dot_general(held, gu[slot, e, 1], NT, preferred_element_type=jnp.float32)
        inner = (g * lax.logistic(g) * u).astype(jnp.bfloat16)
        made = jnp.dot(inner, down[slot, e], preferred_element_type=jnp.float32)
        for i in range(n):
            w = weights[i][e]
            part = made[i * size : (i + 1) * size]
            for c in range(part.shape[1] // LANES):
                at = slice(c * LANES, (c + 1) * LANES)
                outs[i][e, :, at] = (part[:, at] * w).astype(jnp.bfloat16)


def experts(rows, weights, gu, down, after=()):
    n = len(rows)
    local, slots, width = rows[0].shape
    size = min(slots, EXPERT_ROWS)
    hidden = down.shape[1]
    group = 2 if local % 2 == 0 else 1
    rows_spec = pl.BlockSpec((group, size, width), lambda e, i: (e, i, 0))
    weight_spec = pl.BlockSpec((group, size, LANES), lambda e, i: (e, i, 0))
    return call(
        functools.partial(expert_kernel, n),
        6,
        (local // group, slots // size),
        [rows_spec] * n + [weight_spec] * n + [IN_HBM, IN_HBM] + [ANYWHERE] * len(after),
        [rows_spec] * n,
        [jax.ShapeDtypeStruct(r.shape, jnp.bfloat16) for r in rows],
        [
            pltpu.VMEM((DEPTH, group, 2, hidden, width), jnp.bfloat16),
            pltpu.VMEM((DEPTH, group, hidden, width), jnp.bfloat16),
            pltpu.SemaphoreType.DMA((2, DEPTH, group)),
        ],
        "experts",
        VMEM_EXPERTS,
    )(*rows, *weights, gu, down, *after)


def combine_kernel(n, *refs):
    picks, made, outs = refs[:n], refs[n : 2 * n], refs[-2:]
    local, _, width = made[0].shape
    parts = picks[0].shape[0]
    half = parts // 2
    for i in range(n):
        for p in range(parts):
            held = made[i][:, p * CAP : (p + 1) * CAP, :].reshape(local * CAP, width)
            mix = lax.dot_general(picks[i][p], held, TN, preferred_element_type=jnp.float32)
            at = ((p % half) * n + i) * BLOCK
            outs[p // half][0, at : at + BLOCK, :] = mix.astype(jnp.bfloat16)


def combine(picks, made, n_parts, after=()):
    n = len(picks)
    steps = picks[0].shape[0] // n_parts
    local, _, width = made[0].shape
    half = n_parts // 2 * n * BLOCK
    out = pl.BlockSpec((1, half, width), lambda i: (i, 0, 0))
    return call(
        functools.partial(combine_kernel, n),
        2 * steps,
        (steps,),
        [pl.BlockSpec((n_parts,) + picks[0].shape[1:], lambda i: (i, 0, 0))] * n
        + [pl.BlockSpec((local, n_parts * CAP, width), lambda i: (0, i, 0))] * n
        + [ANYWHERE] * len(after),
        [out, out],
        [jax.ShapeDtypeStruct((steps, half, width), jnp.bfloat16)] * 2,
        [],
        "combine",
    )(*picks, *made, *after)


def attend_kernel(starts, kdim, first_ref, last_ref, kpos_ref, q_ref, *refs):
    n = len(starts)
    parts, (out_ref, even, odd) = refs[:n], refs[n:]
    rows = q_ref.shape[0]
    start = max(parts[0].shape[1] - even.shape[1], 0)
    wide = even.shape[1]
    half = wide - kdim

    @pl.when(pl.program_id(0) == 0)
    def _():
        pad = jnp.zeros((rows, half), jnp.bfloat16)
        for i in range(n):
            at = slice(i * rows, (i + 1) * rows)
            keys = parts[i][starts[i] : starts[i] + rows, start : start + kdim]
            even[at, :] = jnp.concatenate([keys, pad], axis=1)
            odd[at, :] = jnp.concatenate([pad, keys], axis=1)

    allowed = (kpos_ref[...] >= first_ref[...]) & (kpos_ref[...] <= last_ref[...])
    for i, keys in enumerate((even, odd)):
        at = i * (kdim - half)
        scores = lax.dot_general(
            q_ref[:, at : at + wide], keys[...], NT, preferred_element_type=jnp.float32
        )
        scores = jnp.where(allowed, scores * qk_scale, -1e30)
        expo = jnp.exp(scores - jnp.max(scores, axis=-1, keepdims=True))
        probs = (expo / jnp.sum(expo, axis=-1, keepdims=True)).astype(jnp.bfloat16)
        out_ref[:, i * LATENT : (i + 1) * LATENT] = jnp.dot(
            probs, even[:, :LATENT], preferred_element_type=jnp.float32
        ).astype(jnp.bfloat16)


def attend(queries, parts, first, last, kpos):
    n = len(parts)
    rows, kdim = queries.shape[0], queries.shape[1] // HEADS
    wide = -(-kdim // LANES) * LANES
    return call(
        functools.partial(attend_kernel, [at for _, at in parts], kdim),
        6,
        (HEADS // 2,),
        [whole(first), whole(last), whole(kpos)]
        + [pl.BlockSpec((rows, 2 * kdim), lambda h: (0, h))]
        + [whole(p) for p, _ in parts],
        pl.BlockSpec((rows, 2 * LATENT), lambda h: (0, h)),
        jax.ShapeDtypeStruct((rows, HEADS * LATENT), jnp.bfloat16),
        [pltpu.VMEM((n * rows, wide), jnp.bfloat16)] * 2,
        "attention",
    )(first, last, kpos, queries, *[p for p, _ in parts])


def added(*terms):
    total = terms[0].astype(jnp.float32)
    for term in terms[1:]:
        total = total + term.astype(jnp.float32)
    return total.astype(jnp.bfloat16)


def shards(queries, latent_kv, doc_lengths, hidden_in, router_weight, expert_ids, gate_up, w_down):
    tok_rows, width = hidden_in.shape[1:]
    n_ctx, n_exp = lax.axis_size("ctx"), lax.axis_size("exp")
    ctx, exp = lax.axis_index("ctx"), lax.axis_index("exp")
    local = gate_up.shape[0]
    near = n_exp == 4
    shifts = [0, 1, 3, 2] if near else [0]
    tokens = hidden_in[0]

    def flip(a, bit):
        return lax.ppermute(a, "ctx", [(i, i ^ bit) for i in range(n_ctx)])

    def shift(a, d):
        return lax.ppermute(a, "exp", [(i, i ^ d) for i in range(n_exp)])

    def along_exp(a):
        if near:
            beside, across = shift(a, 1), shift(a, 3)
            return [a, beside, across, shift(across, 1)]
        return [lax.all_gather(a, "exp", axis=0, tiled=True)]

    masks = [0, 2, 1, 3]
    order = jnp.stack([ctx ^ m for m in masks])

    top = expert_ids.shape[2]
    picks = expert_ids[0].T.astype(jnp.bfloat16).reshape(1, top * tok_rows)
    picks = jnp.pad(picks, ((0, EXTRA - 1), (0, width - top * tok_rows)))
    packed = jnp.concatenate([tokens, picks], axis=0)

    keys = latent_kv[0]
    keys = jnp.concatenate([keys, flip(keys, 2)], axis=0)
    near_parts = along_exp(packed)
    arrived = near_parts
    crossed = [flip(a, 2) for a in near_parts[:3]]
    if near:
        crossed.append(shift(crossed[2], 1))
    kv = [(a, k * tok_rows) for a in (keys, flip(keys, 1)) for k in range(2)]
    if near:
        blocks = 1
        pairs = [jnp.concatenate([a, b], axis=0) for a, b in zip(near_parts, crossed)]
        flipped = [flip(a, 1) for a in pairs]
        spread = [[(a, 0), (a, 1), (b, 0), (b, 1)] for a, b in zip(pairs, flipped)]
    else:
        blocks = near_parts[0].shape[0] // (BLOCK + EXTRA)
        spread = [[(near_parts[0], 0), (crossed[0], 0)]]
        spread[0] = spread[0] + [(flip(a, 1), 0) for a, _ in spread[0]]
    behind = [()] * PIECES
    if near:
        behind = [(), (arrived[1],), (arrived[2],), (crossed[2],)]

    lengths = doc_lengths[0]
    ends = jnp.cumsum(lengths)
    row_pos = order[:, None] * tok_rows + jnp.arange(tok_rows, dtype=jnp.int32)[None, :]
    pos = row_pos[0]
    passed = pos[:, None] >= ends[None, :]
    first = jnp.max(jnp.where(passed, ends[None, :], 0), axis=1)
    context = attend(queries[0], kv, first[:, None], pos[:, None], row_pos.reshape(1, -1))

    seg = jnp.sum((row_pos[..., None] >= ends).astype(jnp.int32), axis=-1)
    sizes = lengths.astype(jnp.float32)
    scale = jnp.broadcast_to((EXPERTS / (top * sizes * sizes))[:, None], (NDOC, LANES))

    base = (exp * local).reshape(1).astype(jnp.int32)
    rw = jnp.roll(router_weight.T, -exp * local, axis=0)
    balance = None
    gu = sort_rows(gate_up, behind)
    sent = []
    for i in range(len(shifts)):
        row = (seg.reshape(-1, 1, BLOCK), scale) if near and i == 0 else None
        out = dispatch(spread[i], blocks, top, base, rw, local, row)
        sent.append(out[:3])
        if row is not None:
            balance = out[3]
    made = experts([a[0] for a in sent], [a[1] for a in sent], gu, w_down)
    back = []
    for i in reversed(range(len(shifts))):
        keep, give = combine([sent[i][2]], [made[i]], n_ctx)
        got = flip(give, 1)
        far = added(keep[:, tok_rows:], got[:, tok_rows:])
        terms = [keep[:, :tok_rows], got[:, :tok_rows], flip(far, 2)]
        if shifts[i] == 2:
            joining = [shift(added(*terms), 1)]
        elif i:
            back.append(shift(added(*terms, *(joining if shifts[i] == 3 else [])), shifts[i]))
        else:
            back = back + terms
    if near:
        expert_mix = added(*back)
    else:
        expert_mix = lax.psum_scatter(
            added(*back).reshape(-1, width), "exp", scatter_dimension=0, tiled=True
        ).reshape(1, tok_rows, width)

    if balance is None:
        row = lax.all_gather(tokens, "ctx", axis=0, tiled=True)
        router = jax.nn.softmax(
            jnp.dot(row, router_weight, preferred_element_type=jnp.float32), axis=-1
        )
        row_ids = lax.all_gather(expert_ids[0], "ctx", axis=0, tiled=True)
        hot = (row_ids[:, :, None] == jnp.arange(EXPERTS, dtype=jnp.int32)).astype(jnp.float32)
        at = jnp.arange(row.shape[0], dtype=jnp.int32)
        seg_at = jnp.sum((at[:, None] >= ends[None, :]).astype(jnp.int32), axis=1)
        seg_hot = (seg_at[:, None] == jnp.arange(NDOC, dtype=jnp.int32)).astype(jnp.float32)
        exact = lax.Precision.HIGHEST
        counts = jnp.dot(seg_hot.T, hot.sum(axis=1), precision=exact)
        mass = jnp.dot(seg_hot.T, router, precision=exact)
        per_doc = jnp.sum(counts * mass, axis=1) * scale[:, 0]
    else:
        per_doc = balance[:, 0]
    return context[None], expert_mix, per_doc.reshape(1, NDOC)


def solution(mesh):
    rows = P(("group", "exp"), "ctx", None)
    docs = P(("group", "exp"), None)
    return jax.shard_map(
        shards,
        mesh=mesh,
        in_specs=(rows, rows, docs, rows, P(), rows, P("exp", "ctx", None, None), P("exp", "ctx", None)),
        out_specs=(rows, rows, docs),
        check_vma=False,
    )
```

```python
import functools

import jax
import jax.numpy as jnp
from jax import lax
from jax.experimental import pallas as pl
from jax.experimental.pallas import tpu as pltpu
from jax.sharding import PartitionSpec as P

EXPERTS = 64
HEADS = 8
LATENT = 512
CAP = 16
NDOC = 8
BLOCK = 128
LANES = 128
EXPERT_ROWS = 256
EXTRA = 16
VMEM = 14 * 2**20
VMEM_EXPERTS = 24 * 2**20
VMEM_SORT = 52 * 2**20
PIECES = 2
DEPTH = 3
PEAK = 1.1e9

qk_scale = 192.0 ** (-0.5)
NT = (((1,), (1,)), ((), ()))
TN = (((0,), (0,)), ((), ()))


def call(kernel, micros, grid, in_specs, out_specs, out_shape, scratch, name, limit=VMEM, aliases={}):
    return pl.pallas_call(
        kernel,
        grid=grid,
        in_specs=in_specs,
        out_specs=out_specs,
        out_shape=out_shape,
        scratch_shapes=scratch,
        input_output_aliases=aliases,
        compiler_params=pltpu.CompilerParams(
            dimension_semantics=("arbitrary",) * len(grid), vmem_limit_bytes=limit
        ),
        cost_estimate=pl.CostEstimate(
            flops=int(micros * PEAK), bytes_accessed=0, transcendentals=0
        ),
        name=name,
    )


def dispatch_kernel(n_parts, n_row, top, n_after, base_ref, rw_ref, *refs):
    parts, refs = refs[:n_parts], refs[n_parts + n_after :]
    if n_row:
        seg_ref, scale_ref = refs[:2]
        refs = refs[2:]
    rows_ref, weight_ref, picks_ref = refs[:3]
    local = rows_ref.shape[0]
    width = rows_ref.shape[2]
    names = lax.broadcasted_iota(jnp.int32, (EXPERTS, BLOCK), 0).astype(jnp.float32)
    base = base_ref[0].astype(jnp.float32)
    before = (
        lax.broadcasted_iota(jnp.int32, (BLOCK, BLOCK), 0)
        < lax.broadcasted_iota(jnp.int32, (BLOCK, BLOCK), 1)
    ).astype(jnp.bfloat16)
    slot = lax.broadcasted_iota(jnp.int32, (local, CAP, BLOCK), 1).astype(jnp.float32)
    hots, probs = [], []
    for p in range(n_parts):
        x = parts[p][:BLOCK, :]
        ids = parts[p][BLOCK : BLOCK + EXTRA, :].astype(jnp.float32)[0:1] - base
        ids = jnp.where(ids < 0.0, ids + EXPERTS, ids)
        logits = lax.dot_general(rw_ref[...], x, NT, preferred_element_type=jnp.float32)
        expo = jnp.exp(logits - jnp.max(logits, axis=0, keepdims=True))
        prob = expo / jnp.sum(expo, axis=0, keepdims=True)
        hot = names == ids[:, :BLOCK]
        for k in range(1, top):
            hot = hot | (names == ids[:, k * BLOCK : (k + 1) * BLOCK])
        hot = hot.astype(jnp.float32)
        chosen = prob * hot
        gate = chosen[:local] / jnp.sum(chosen, axis=0, keepdims=True)
        own = hot[:local]
        rank = jnp.dot(own.astype(jnp.bfloat16), before, preferred_element_type=jnp.float32)
        key = jnp.where(own > 0.0, rank, -1.0)
        pick = (key[:, None, :] == slot).astype(jnp.float32)
        at = slice(p * CAP, (p + 1) * CAP)
        weight_ref[:, at, :] = jnp.broadcast_to(
            jnp.sum(pick * gate[:, None, :], axis=-1, keepdims=True), (local, CAP, LANES)
        )
        pick = pick.reshape(local * CAP, BLOCK).astype(jnp.bfloat16)
        picks_ref[p] = pick
        taken = jnp.dot(pick, x, preferred_element_type=jnp.float32)
        rows_ref[:, at, :] = taken.astype(jnp.bfloat16).reshape(local, CAP, width)
        hots.append(hot)
        probs.append(prob)
    if n_row:
        bal_ref = refs[3]
        for d in range(NDOC):
            counts = jnp.zeros((EXPERTS, BLOCK), jnp.float32)
            mass = jnp.zeros((EXPERTS, BLOCK), jnp.float32)
            for p in range(n_row):
                inside = seg_ref[p] == d
                counts = counts + jnp.where(inside, hots[p], 0.0)
                mass = mass + jnp.where(inside, probs[p], 0.0)
            both = jnp.sum(counts, axis=1, keepdims=True) * jnp.sum(mass, axis=1, keepdims=True)
            bal_ref[d : d + 1, :] = (
                jnp.broadcast_to(jnp.sum(both, axis=0, keepdims=True), (1, LANES))
                * scale_ref[d : d + 1, :]
            )


IN_HBM = pl.BlockSpec(memory_space=pltpu.HBM)
ANYWHERE = pl.BlockSpec(memory_space=pl.ANY)


def whole(a):
    return pl.BlockSpec(a.shape, lambda *i: (0,) * a.ndim)


def dispatch(parts, n, top, base, rw, local, row=None, after=()):
    n_parts = len(parts)
    width = rw.shape[1]
    slots = n_parts * CAP
    in_specs = [
        pl.BlockSpec(memory_space=pltpu.SMEM),
        whole(rw),
    ] + [
        pl.BlockSpec((BLOCK + EXTRA, width), lambda i, k=k: (k + i, 0)) for _, k in parts
    ]
    in_specs += [ANYWHERE] * len(after)
    out_specs = [
        pl.BlockSpec((local, slots, width), lambda i: (0, i, 0)),
        pl.BlockSpec((local, slots, LANES), lambda i: (0, i, 0)),
        pl.BlockSpec((n_parts, local * CAP, BLOCK), lambda i: (i, 0, 0)),
    ]
    out_shape = [
        jax.ShapeDtypeStruct((local, n * slots, width), jnp.bfloat16),
        jax.ShapeDtypeStruct((local, n * slots, LANES), jnp.float32),
        jax.ShapeDtypeStruct((n * n_parts, local * CAP, BLOCK), jnp.bfloat16),
    ]
    extra = ()
    if row is not None:
        extra = row
        in_specs += [whole(a) for a in row]
        out_specs.append(pl.BlockSpec((NDOC, LANES), lambda i: (0, 0)))
        out_shape.append(jax.ShapeDtypeStruct((NDOC, LANES), jnp.float32))
    return call(
        functools.partial(dispatch_kernel, n_parts, n_parts if row is not None else 0, top, len(after)),
        3 * n,
        (n,),
        in_specs,
        out_specs,
        out_shape,
        [],
        "dispatch",
    )(base, rw, *[a for a, _ in parts], *after, *extra)


def fetch(sources, slots, sem, step, steps, first, start=0):
    depth, group = slots[0].shape[:2]

    def copies(at):
        slot = lax.rem(at, depth)
        return [
            pltpu.make_async_copy(
                source.at[start + at * group + e], held.at[slot, e], sem.at[i, slot, e]
            )
            for i, (source, held) in enumerate(zip(sources, slots))
            for e in range(group)
        ]

    @pl.when(first & (step == 0))
    def _():
        for ahead in range(depth - 1):

            @pl.when(ahead < steps)
            def _():
                for copy in copies(step + ahead):
                    copy.start()

    @pl.when(first & (step + depth - 1 < steps))
    def _():
        for copy in copies(step + depth - 1):
            copy.start()

    @pl.when(first)
    def _():
        for copy in copies(step):
            copy.wait()

    return lax.rem(step, depth)


def sort_kernel(start, gu_ref, *refs):
    out_ref, token_ref, held, made, wide, in_sem, out_sem = refs[-7:]
    token_ref[...] = jnp.zeros_like(token_ref)
    step, steps = pl.program_id(0), pl.num_programs(0)
    _, group, _, hidden, width = made.shape
    chunks = width // LANES
    slot = fetch([gu_ref], [held], in_sem, step, steps, step >= 0, start)
    to = lax.rem(step, 2)

    def leave(at):
        to = lax.rem(at, 2)
        return pltpu.make_async_copy(
            made.at[to], out_ref.at[pl.ds(start + at * group, group)], out_sem.at[to]
        )

    @pl.when(step >= 2)
    def _():
        leave(step - 2).wait()

    for e in range(group):
        wide[e] = held[slot, e].astype(jnp.float32)
        for z in range(2):
            for c in range(chunks):
                part = wide[e, pl.ds(2 * c + z, hidden, stride=2 * chunks), :]
                made[to, e, z, :, c * LANES : (c + 1) * LANES] = part.astype(jnp.bfloat16)
    leave(step).start()

    @pl.when(step == steps - 1)
    def _():
        @pl.when(step >= 1)
        def _():
            leave(step - 1).wait()

        leave(step).wait()


def sort_rows(gate_up, behind):
    local, hidden, _, width = gate_up.shape
    pieces = PIECES if local % (2 * PIECES) == 0 else 1
    group = 2 if local % 2 == 0 else 1
    chunks = width // LANES
    gu = gate_up.reshape(local, hidden, 2, chunks, LANES).swapaxes(2, 3)
    gu = gu.reshape(local, hidden * 2 * chunks, LANES)
    done = ()
    for j in range(pieces):
        after = behind[j] if pieces > 1 else ()
        *done, token = (
            call(
                functools.partial(sort_kernel, j * local // pieces),
                8,
                (local // pieces // group,),
                [IN_HBM] + [IN_HBM] * len(done) + [ANYWHERE] * len(after),
                [IN_HBM, pl.BlockSpec((8, LANES), lambda e: (0, 0))],
                [
                    jax.ShapeDtypeStruct((local, 2, hidden, width), jnp.bfloat16),
                    jax.ShapeDtypeStruct((8, LANES), jnp.float32),
                ],
                [
                    pltpu.VMEM((2, group) + gu.shape[1:], jnp.bfloat16),
                    pltpu.VMEM((2, group, 2, hidden, width), jnp.bfloat16),
                    pltpu.VMEM((group,) + gu.shape[1:], jnp.float32),
                    pltpu.SemaphoreType.DMA((1, 2, group)),
                    pltpu.SemaphoreType.DMA((2,)),
                ],
                "sort",
                VMEM_SORT,
                {1: 0} if done else {},
            )(gu, *done, *after)
        )
    return done[0], token


def stack_kernel(a_ref, b_ref, *refs):
    rows = a_ref.shape[0]
    refs[-1][:rows, :] = a_ref[...]
    refs[-1][rows:, :] = b_ref[...]


def stack(a, b, before):
    rows, width = a.shape
    return call(
        stack_kernel,
        1,
        (1,),
        [whole(a), whole(b)] + [ANYWHERE] * len(before),
        pl.BlockSpec((2 * rows, width), lambda i: (0, 0)),
        jax.ShapeDtypeStruct((2 * rows, width), a.dtype),
        [],
        "stack",
    )(a, b, *before)


def expert_kernel(n, *refs):
    rows, weights = refs[:n], refs[n : 2 * n]
    gu_ref, down_ref = refs[2 * n : 2 * n + 2]
    outs, (gu, down, sem) = refs[-3 - n : -3], refs[-3:]
    group = gu.shape[1]
    size = rows[0].shape[1]
    slot = fetch(
        [gu_ref, down_ref],
        [gu, down],
        sem,
        pl.program_id(0),
        pl.num_programs(0),
        pl.program_id(1) == 0,
    )
    for e in range(group):
        held = jnp.concatenate([r[e] for r in rows], axis=0)
        g = lax.dot_general(held, gu[slot, e, 0], NT, preferred_element_type=jnp.float32)
        u = lax.dot_general(held, gu[slot, e, 1], NT, preferred_element_type=jnp.float32)
        inner = (g * lax.logistic(g) * u).astype(jnp.bfloat16)
        made = jnp.dot(inner, down[slot, e], preferred_element_type=jnp.float32)
        for i in range(n):
            w = weights[i][e]
            part = made[i * size : (i + 1) * size]
            for c in range(part.shape[1] // LANES):
                at = slice(c * LANES, (c + 1) * LANES)
                outs[i][e, :, at] = (part[:, at] * w).astype(jnp.bfloat16)


def experts(rows, weights, gu, down, after=()):
    n = len(rows)
    local, slots, width = rows[0].shape
    size = min(slots, EXPERT_ROWS)
    hidden = down.shape[1]
    group = 2 if local % 2 == 0 else 1
    rows_spec = pl.BlockSpec((group, size, width), lambda e, i: (e, i, 0))
    weight_spec = pl.BlockSpec((group, size, LANES), lambda e, i: (e, i, 0))
    return call(
        functools.partial(expert_kernel, n),
        6,
        (local // group, slots // size),
        [rows_spec] * n + [weight_spec] * n + [IN_HBM, IN_HBM] + [ANYWHERE] * len(after),
        [rows_spec] * n,
        [jax.ShapeDtypeStruct(r.shape, jnp.bfloat16) for r in rows],
        [
            pltpu.VMEM((DEPTH, group, 2, hidden, width), jnp.bfloat16),
            pltpu.VMEM((DEPTH, group, hidden, width), jnp.bfloat16),
            pltpu.SemaphoreType.DMA((2, DEPTH, group)),
        ],
        "experts",
        VMEM_EXPERTS,
    )(*rows, *weights, gu, down, *after)


def combine_kernel(n, *refs):
    picks, made, outs = refs[:n], refs[n : 2 * n], refs[-2:]
    local, _, width = made[0].shape
    parts = picks[0].shape[0]
    half = parts // 2
    for i in range(n):
        for p in range(parts):
            held = made[i][:, p * CAP : (p + 1) * CAP, :].reshape(local * CAP, width)
            mix = lax.dot_general(picks[i][p], held, TN, preferred_element_type=jnp.float32)
            at = ((p % half) * n + i) * BLOCK
            outs[p // half][0, at : at + BLOCK, :] = mix.astype(jnp.bfloat16)


def combine(picks, made, n_parts, after=()):
    n = len(picks)
    steps = picks[0].shape[0] // n_parts
    local, _, width = made[0].shape
    half = n_parts // 2 * n * BLOCK
    out = pl.BlockSpec((1, half, width), lambda i: (i, 0, 0))
    return call(
        functools.partial(combine_kernel, n),
        2 * steps,
        (steps,),
        [pl.BlockSpec((n_parts,) + picks[0].shape[1:], lambda i: (i, 0, 0))] * n
        + [pl.BlockSpec((local, n_parts * CAP, width), lambda i: (0, i, 0))] * n
        + [ANYWHERE] * len(after),
        [out, out],
        [jax.ShapeDtypeStruct((steps, half, width), jnp.bfloat16)] * 2,
        [],
        "combine",
    )(*picks, *made, *after)


def attend_kernel(starts, kdim, first_ref, last_ref, kpos_ref, q_ref, *refs):
    n = len(starts)
    parts, (out_ref, even, odd) = refs[:n], refs[n:]
    rows = q_ref.shape[0]
    start = max(parts[0].shape[1] - even.shape[1], 0)
    wide = even.shape[1]
    half = wide - kdim

    @pl.when(pl.program_id(0) == 0)
    def _():
        pad = jnp.zeros((rows, half), jnp.bfloat16)
        for i in range(n):
            at = slice(i * rows, (i + 1) * rows)
            keys = parts[i][starts[i] : starts[i] + rows, start : start + kdim]
            even[at, :] = jnp.concatenate([keys, pad], axis=1)
            odd[at, :] = jnp.concatenate([pad, keys], axis=1)

    allowed = (kpos_ref[...] >= first_ref[...]) & (kpos_ref[...] <= last_ref[...])
    for i, keys in enumerate((even, odd)):
        at = i * (kdim - half)
        scores = lax.dot_general(
            q_ref[:, at : at + wide], keys[...], NT, preferred_element_type=jnp.float32
        )
        scores = jnp.where(allowed, scores * qk_scale, -1e30)
        expo = jnp.exp(scores - jnp.max(scores, axis=-1, keepdims=True))
        probs = (expo / jnp.sum(expo, axis=-1, keepdims=True)).astype(jnp.bfloat16)
        out_ref[:, i * LATENT : (i + 1) * LATENT] = jnp.dot(
            probs, even[:, :LATENT], preferred_element_type=jnp.float32
        ).astype(jnp.bfloat16)


def attend(queries, parts, first, last, kpos):
    n = len(parts)
    rows, kdim = queries.shape[0], queries.shape[1] // HEADS
    wide = -(-kdim // LANES) * LANES
    return call(
        functools.partial(attend_kernel, [at for _, at in parts], kdim),
        6,
        (HEADS // 2,),
        [whole(first), whole(last), whole(kpos)]
        + [pl.BlockSpec((rows, 2 * kdim), lambda h: (0, h))]
        + [whole(p) for p, _ in parts],
        pl.BlockSpec((rows, 2 * LATENT), lambda h: (0, h)),
        jax.ShapeDtypeStruct((rows, HEADS * LATENT), jnp.bfloat16),
        [pltpu.VMEM((n * rows, wide), jnp.bfloat16)] * 2,
        "attention",
    )(first, last, kpos, queries, *[p for p, _ in parts])


def added(*terms):
    total = terms[0].astype(jnp.float32)
    for term in terms[1:]:
        total = total + term.astype(jnp.float32)
    return total.astype(jnp.bfloat16)


def shards(queries, latent_kv, doc_lengths, hidden_in, router_weight, expert_ids, gate_up, w_down):
    tok_rows, width = hidden_in.shape[1:]
    n_ctx, n_exp = lax.axis_size("ctx"), lax.axis_size("exp")
    ctx, exp = lax.axis_index("ctx"), lax.axis_index("exp")
    local = gate_up.shape[0]
    near = n_exp == 4
    shifts = [0, 1, 3, 2] if near else [0]
    tokens = hidden_in[0]

    def flip(a, bit):
        return lax.ppermute(a, "ctx", [(i, i ^ bit) for i in range(n_ctx)])

    def shift(a, d):
        return lax.ppermute(a, "exp", [(i, i ^ d) for i in range(n_exp)])

    def along_exp(a):
        if near:
            beside, across = shift(a, 1), shift(a, 3)
            return [a, beside, across, shift(across, 1)]
        return [lax.all_gather(a, "exp", axis=0, tiled=True)]

    masks = [0, 2, 1, 3]
    order = jnp.stack([ctx ^ m for m in masks])

    top = expert_ids.shape[2]
    picks = expert_ids[0].T.astype(jnp.bfloat16).reshape(1, top * tok_rows)
    picks = jnp.pad(picks, ((0, EXTRA - 1), (0, width - top * tok_rows)))
    packed = jnp.concatenate([tokens, picks], axis=0)

    keys = latent_kv[0]
    keys = jnp.concatenate([keys, flip(keys, 2)], axis=0)
    near_parts = along_exp(packed)
    arrived = near_parts
    crossed = [flip(a, 2) for a in near_parts[:3]]
    if near:
        crossed.append(shift(crossed[2], 1))
    kv = [(a, k * tok_rows) for a in (keys, flip(keys, 1)) for k in range(2)]
    if near:
        blocks = 1
        gu, token = sort_rows(gate_up, [(), (crossed[2],)])
        pairs = [
            stack(a, b, (token,)) if i == 1 else jnp.concatenate([a, b], axis=0)
            for i, (a, b) in enumerate(zip(near_parts, crossed))
        ]
        flipped = [flip(a, 1) for a in pairs]
        spread = [[(a, 0), (a, 1), (b, 0), (b, 1)] for a, b in zip(pairs, flipped)]
    else:
        gu, _ = sort_rows(gate_up, [(), ()])
        blocks = near_parts[0].shape[0] // (BLOCK + EXTRA)
        spread = [[(near_parts[0], 0), (crossed[0], 0)]]
        spread[0] = spread[0] + [(flip(a, 1), 0) for a, _ in spread[0]]
    lengths = doc_lengths[0]
    ends = jnp.cumsum(lengths)
    row_pos = order[:, None] * tok_rows + jnp.arange(tok_rows, dtype=jnp.int32)[None, :]
    pos = row_pos[0]
    passed = pos[:, None] >= ends[None, :]
    first = jnp.max(jnp.where(passed, ends[None, :], 0), axis=1)
    context = attend(queries[0], kv, first[:, None], pos[:, None], row_pos.reshape(1, -1))

    seg = jnp.sum((row_pos[..., None] >= ends).astype(jnp.int32), axis=-1)
    sizes = lengths.astype(jnp.float32)
    scale = jnp.broadcast_to((EXPERTS / (top * sizes * sizes))[:, None], (NDOC, LANES))

    base = (exp * local).reshape(1).astype(jnp.int32)
    rw = jnp.roll(router_weight.T, -exp * local, axis=0)
    balance = None
    sent = []
    for i in range(len(shifts)):
        row = (seg.reshape(-1, 1, BLOCK), scale) if near and i == 0 else None
        out = dispatch(spread[i], blocks, top, base, rw, local, row)
        sent.append(out[:3])
        if row is not None:
            balance = out[3]
    made = experts([a[0] for a in sent], [a[1] for a in sent], gu, w_down)
    back = []
    for i in [3, 1, 2, 0][-len(shifts) :]:
        keep, give = combine([sent[i][2]], [made[i]], n_ctx)
        got = flip(give, 1)
        far = added(keep[:, tok_rows:], got[:, tok_rows:])
        terms = [keep[:, :tok_rows], got[:, :tok_rows], flip(far, 2)]
        if shifts[i] == 2:
            joining = [shift(added(*terms), 1)]
        elif i:
            back.append(shift(added(*terms, *(joining if shifts[i] == 3 else [])), shifts[i]))
        else:
            back = back + terms
    if near:
        expert_mix = added(*back)
    else:
        expert_mix = lax.psum_scatter(
            added(*back).reshape(-1, width), "exp", scatter_dimension=0, tiled=True
        ).reshape(1, tok_rows, width)

    if balance is None:
        row = lax.all_gather(tokens, "ctx", axis=0, tiled=True)
        router = jax.nn.softmax(
            jnp.dot(row, router_weight, preferred_element_type=jnp.float32), axis=-1
        )
        row_ids = lax.all_gather(expert_ids[0], "ctx", axis=0, tiled=True)
        hot = (row_ids[:, :, None] == jnp.arange(EXPERTS, dtype=jnp.int32)).astype(jnp.float32)
        at = jnp.arange(row.shape[0], dtype=jnp.int32)
        seg_at = jnp.sum((at[:, None] >= ends[None, :]).astype(jnp.int32), axis=1)
        seg_hot = (seg_at[:, None] == jnp.arange(NDOC, dtype=jnp.int32)).astype(jnp.float32)
        exact = lax.Precision.HIGHEST
        counts = jnp.dot(seg_hot.T, hot.sum(axis=1), precision=exact)
        mass = jnp.dot(seg_hot.T, router, precision=exact)
        per_doc = jnp.sum(counts * mass, axis=1) * scale[:, 0]
    else:
        per_doc = balance[:, 0]
    return context[None], expert_mix, per_doc.reshape(1, NDOC)


def solution(mesh):
    rows = P(("group", "exp"), "ctx", None)
    docs = P(("group", "exp"), None)
    return jax.shard_map(
        shards,
        mesh=mesh,
        in_specs=(rows, rows, docs, rows, P(), rows, P("exp", "ctx", None, None), P("exp", "ctx", None)),
        out_specs=(rows, rows, docs),
        check_vma=False,
    )
```

```python
import functools

import jax
import jax.numpy as jnp
from jax import lax
from jax.experimental import pallas as pl
from jax.experimental.pallas import tpu as pltpu
from jax.sharding import PartitionSpec as P

EXPERTS = 64
HEADS = 8
LATENT = 512
CAP = 16
NDOC = 8
BLOCK = 128
LANES = 128
EXPERT_ROWS = 256
EXTRA = 16
VMEM = 14 * 2**20
VMEM_EXPERTS = 24 * 2**20
VMEM_SORT = 52 * 2**20
PIECES = (0.5, 0.75, 1.0)
DEPTH = 3
PEAK = 1.1e9

qk_scale = 192.0 ** (-0.5)
NT = (((1,), (1,)), ((), ()))
TN = (((0,), (0,)), ((), ()))


def call(kernel, micros, grid, in_specs, out_specs, out_shape, scratch, name, limit=VMEM, aliases={}):
    return pl.pallas_call(
        kernel,
        grid=grid,
        in_specs=in_specs,
        out_specs=out_specs,
        out_shape=out_shape,
        scratch_shapes=scratch,
        input_output_aliases=aliases,
        compiler_params=pltpu.CompilerParams(
            dimension_semantics=("arbitrary",) * len(grid) if grid else None, vmem_limit_bytes=limit
        ),
        cost_estimate=pl.CostEstimate(
            flops=int(micros * PEAK), bytes_accessed=0, transcendentals=0
        ),
        name=name,
    )


def dispatch_kernel(starts, n_row, top, base_ref, rw_ref, *refs):
    n_parts = len(starts)
    parts, refs = refs[:n_parts], refs[n_parts:]
    if n_row:
        seg_ref, scale_ref = refs[:2]
        refs = refs[2:]
    rows_ref, weight_ref, picks_ref = refs[:3]
    local = rows_ref.shape[0]
    width = rows_ref.shape[2]
    names = lax.broadcasted_iota(jnp.int32, (EXPERTS, BLOCK), 0).astype(jnp.float32)
    base = base_ref[0].astype(jnp.float32)
    before = (
        lax.broadcasted_iota(jnp.int32, (BLOCK, BLOCK), 0)
        < lax.broadcasted_iota(jnp.int32, (BLOCK, BLOCK), 1)
    ).astype(jnp.bfloat16)
    slot = lax.broadcasted_iota(jnp.int32, (local, CAP, BLOCK), 1).astype(jnp.float32)
    hots, probs = [], []
    for p in range(n_parts):
        s = starts[p]
        x = parts[p][s : s + BLOCK, :]
        ids = parts[p][s + BLOCK : s + BLOCK + EXTRA, :].astype(jnp.float32)[0:1] - base
        ids = jnp.where(ids < 0.0, ids + EXPERTS, ids)
        logits = lax.dot_general(rw_ref[...], x, NT, preferred_element_type=jnp.float32)
        expo = jnp.exp(logits - jnp.max(logits, axis=0, keepdims=True))
        prob = expo / jnp.sum(expo, axis=0, keepdims=True)
        hot = names == ids[:, :BLOCK]
        for k in range(1, top):
            hot = hot | (names == ids[:, k * BLOCK : (k + 1) * BLOCK])
        hot = hot.astype(jnp.float32)
        chosen = prob * hot
        gate = chosen[:local] / jnp.sum(chosen, axis=0, keepdims=True)
        own = hot[:local]
        rank = jnp.dot(own.astype(jnp.bfloat16), before, preferred_element_type=jnp.float32)
        key = jnp.where(own > 0.0, rank, -1.0)
        pick = (key[:, None, :] == slot).astype(jnp.float32)
        at = slice(p * CAP, (p + 1) * CAP)
        weight_ref[:, at, :] = jnp.broadcast_to(
            jnp.sum(pick * gate[:, None, :], axis=-1, keepdims=True), (local, CAP, LANES)
        )
        pick = pick.reshape(local * CAP, BLOCK).astype(jnp.bfloat16)
        picks_ref[p] = pick
        taken = jnp.dot(pick, x, preferred_element_type=jnp.float32)
        rows_ref[:, at, :] = taken.astype(jnp.bfloat16).reshape(local, CAP, width)
        hots.append(hot)
        probs.append(prob)
    if n_row:
        bal_ref = refs[3]
        for d in range(NDOC):
            counts = jnp.zeros((EXPERTS, BLOCK), jnp.float32)
            mass = jnp.zeros((EXPERTS, BLOCK), jnp.float32)
            for p in range(n_row):
                inside = seg_ref[p] == d
                counts = counts + jnp.where(inside, hots[p], 0.0)
                mass = mass + jnp.where(inside, probs[p], 0.0)
            both = jnp.sum(counts, axis=1, keepdims=True) * jnp.sum(mass, axis=1, keepdims=True)
            bal_ref[d : d + 1, :] = (
                jnp.broadcast_to(jnp.sum(both, axis=0, keepdims=True), (1, LANES))
                * scale_ref[d : d + 1, :]
            )


IN_HBM = pl.BlockSpec(memory_space=pltpu.HBM)
ANYWHERE = pl.BlockSpec(memory_space=pl.ANY)


IN_VMEM = pl.BlockSpec(memory_space=pltpu.VMEM)


def whole(a):
    return pl.BlockSpec(a.shape, lambda *i: (0,) * a.ndim)


def dispatch(parts, n, top, base, rw, local, row=None):
    n_parts = len(parts)
    width = rw.shape[1]
    slots = n_parts * CAP
    in_specs = [
        pl.BlockSpec(memory_space=pltpu.SMEM),
        whole(rw),
    ] + [
        pl.BlockSpec((BLOCK + EXTRA, width), lambda i, k=k: (k + i, 0)) for _, k in parts
    ]
    out_specs = [
        pl.BlockSpec((local, slots, width), lambda i: (0, i, 0)),
        pl.BlockSpec((local, slots, LANES), lambda i: (0, i, 0)),
        pl.BlockSpec((n_parts, local * CAP, BLOCK), lambda i: (i, 0, 0)),
    ]
    out_shape = [
        jax.ShapeDtypeStruct((local, n * slots, width), jnp.bfloat16),
        jax.ShapeDtypeStruct((local, n * slots, LANES), jnp.float32),
        jax.ShapeDtypeStruct((n * n_parts, local * CAP, BLOCK), jnp.bfloat16),
    ]
    extra = ()
    if row is not None:
        extra = row
        in_specs += [whole(a) for a in row]
        out_specs.append(pl.BlockSpec((NDOC, LANES), lambda i: (0, 0)))
        out_shape.append(jax.ShapeDtypeStruct((NDOC, LANES), jnp.float32))
    grid, starts = (n,), [0] * n_parts
    if n == 1:
        grid, starts = (), [k * (BLOCK + EXTRA) for _, k in parts]
        in_specs = in_specs[:1] + [IN_VMEM] * (len(in_specs) - 1)
        out_specs = [IN_VMEM] * len(out_specs)
    return call(
        functools.partial(dispatch_kernel, starts, n_parts if row is not None else 0, top),
        3 * n,
        grid,
        in_specs,
        out_specs,
        out_shape,
        [],
        "dispatch",
    )(base, rw, *[a for a, _ in parts], *extra)


def fetch(sources, slots, sem, step, steps, first, start=0):
    depth, group = slots[0].shape[:2]

    def copies(at):
        slot = lax.rem(at, depth)
        return [
            pltpu.make_async_copy(
                source.at[start + at * group + e], held.at[slot, e], sem.at[i, slot, e]
            )
            for i, (source, held) in enumerate(zip(sources, slots))
            for e in range(group)
        ]

    @pl.when(first & (step == 0))
    def _():
        for ahead in range(depth - 1):

            @pl.when(ahead < steps)
            def _():
                for copy in copies(step + ahead):
                    copy.start()

    @pl.when(first & (step + depth - 1 < steps))
    def _():
        for copy in copies(step + depth - 1):
            copy.start()

    @pl.when(first)
    def _():
        for copy in copies(step):
            copy.wait()

    return lax.rem(step, depth)


def sort_kernel(start, gu_ref, *refs):
    out_ref, token_ref, held, made, wide, in_sem, out_sem = refs[-7:]
    token_ref[...] = jnp.zeros_like(token_ref)
    step, steps = pl.program_id(0), pl.num_programs(0)
    _, group, _, hidden, width = made.shape
    chunks = width // LANES
    slot = fetch([gu_ref], [held], in_sem, step, steps, step >= 0, start)
    to = lax.rem(step, 2)

    def leave(at):
        to = lax.rem(at, 2)
        return pltpu.make_async_copy(
            made.at[to], out_ref.at[pl.ds(start + at * group, group)], out_sem.at[to]
        )

    @pl.when(step >= 2)
    def _():
        leave(step - 2).wait()

    for e in range(group):
        wide[e] = held[slot, e].astype(jnp.float32)
        for z in range(2):
            for c in range(chunks):
                part = wide[e, pl.ds(2 * c + z, hidden, stride=2 * chunks), :]
                made[to, e, z, :, c * LANES : (c + 1) * LANES] = part.astype(jnp.bfloat16)
    leave(step).start()

    @pl.when(step == steps - 1)
    def _():
        @pl.when(step >= 1)
        def _():
            leave(step - 1).wait()

        leave(step).wait()


def sort_rows(gate_up, behind):
    local, hidden, _, width = gate_up.shape
    ends = [int(local * p) for p in PIECES] if local % 8 == 0 else [local]
    group = 2 if local % 2 == 0 else 1
    chunks = width // LANES
    gu = gate_up.reshape(local, hidden, 2, chunks, LANES).swapaxes(2, 3)
    gu = gu.reshape(local, hidden * 2 * chunks, LANES)
    done = ()
    for j, end in enumerate(ends):
        start = ends[j - 1] if j else 0
        after = behind[j] if len(ends) > 1 else ()
        *done, token = (
            call(
                functools.partial(sort_kernel, start),
                8,
                ((end - start) // group,),
                [IN_HBM] + [IN_HBM] * len(done) + [ANYWHERE] * len(after),
                [IN_HBM, pl.BlockSpec((8, LANES), lambda e: (0, 0))],
                [
                    jax.ShapeDtypeStruct((local, 2, hidden, width), jnp.bfloat16),
                    jax.ShapeDtypeStruct((8, LANES), jnp.float32),
                ],
                [
                    pltpu.VMEM((2, group) + gu.shape[1:], jnp.bfloat16),
                    pltpu.VMEM((2, group, 2, hidden, width), jnp.bfloat16),
                    pltpu.VMEM((group,) + gu.shape[1:], jnp.float32),
                    pltpu.SemaphoreType.DMA((1, 2, group)),
                    pltpu.SemaphoreType.DMA((2,)),
                ],
                "sort",
                VMEM_SORT,
                {1: 0} if done else {},
            )(gu, *done, *after)
        )
    return done[0], token


def stack_kernel(a_ref, b_ref, *refs):
    rows = a_ref.shape[0]
    refs[-1][:rows, :] = a_ref[...]
    refs[-1][rows:, :] = b_ref[...]


def stack(a, b, before):
    rows, width = a.shape
    return call(
        stack_kernel,
        1,
        (1,),
        [whole(a), whole(b)] + [ANYWHERE] * len(before),
        pl.BlockSpec((2 * rows, width), lambda i: (0, 0)),
        jax.ShapeDtypeStruct((2 * rows, width), a.dtype),
        [],
        "stack",
    )(a, b, *before)


def expert_kernel(n, *refs):
    rows, weights = refs[:n], refs[n : 2 * n]
    gu_ref, down_ref = refs[2 * n : 2 * n + 2]
    outs, (gu, down, sem) = refs[-3 - n : -3], refs[-3:]
    group = gu.shape[1]
    size = rows[0].shape[1]
    slot = fetch(
        [gu_ref, down_ref],
        [gu, down],
        sem,
        pl.program_id(0),
        pl.num_programs(0),
        pl.program_id(1) == 0,
    )
    for e in range(group):
        held = jnp.concatenate([r[e] for r in rows], axis=0)
        g = lax.dot_general(held, gu[slot, e, 0], NT, preferred_element_type=jnp.float32)
        u = lax.dot_general(held, gu[slot, e, 1], NT, preferred_element_type=jnp.float32)
        inner = (g * lax.logistic(g) * u).astype(jnp.bfloat16)
        made = jnp.dot(inner, down[slot, e], preferred_element_type=jnp.float32)
        for i in range(n):
            w = weights[i][e]
            part = made[i * size : (i + 1) * size]
            for c in range(part.shape[1] // LANES):
                at = slice(c * LANES, (c + 1) * LANES)
                outs[i][e, :, at] = (part[:, at] * w).astype(jnp.bfloat16)


def experts(rows, weights, gu, down, after=()):
    n = len(rows)
    local, slots, width = rows[0].shape
    size = min(slots, EXPERT_ROWS)
    hidden = down.shape[1]
    group = 2 if local % 2 == 0 else 1
    rows_spec = pl.BlockSpec((group, size, width), lambda e, i: (e, i, 0))
    weight_spec = pl.BlockSpec((group, size, LANES), lambda e, i: (e, i, 0))
    return call(
        functools.partial(expert_kernel, n),
        6,
        (local // group, slots // size),
        [rows_spec] * n + [weight_spec] * n + [IN_HBM, IN_HBM] + [ANYWHERE] * len(after),
        [rows_spec] * n,
        [jax.ShapeDtypeStruct(r.shape, jnp.bfloat16) for r in rows],
        [
            pltpu.VMEM((DEPTH, group, 2, hidden, width), jnp.bfloat16),
            pltpu.VMEM((DEPTH, group, hidden, width), jnp.bfloat16),
            pltpu.SemaphoreType.DMA((2, DEPTH, group)),
        ],
        "experts",
        VMEM_EXPERTS,
    )(*rows, *weights, gu, down, *after)


def combine_kernel(n, *refs):
    picks, made, outs = refs[:n], refs[n : 2 * n], refs[-2:]
    local, _, width = made[0].shape
    parts = picks[0].shape[0]
    half = parts // 2
    for i in range(n):
        for p in range(parts):
            held = made[i][:, p * CAP : (p + 1) * CAP, :].reshape(local * CAP, width)
            mix = lax.dot_general(picks[i][p], held, TN, preferred_element_type=jnp.float32)
            at = ((p % half) * n + i) * BLOCK
            outs[p // half][0, at : at + BLOCK, :] = mix.astype(jnp.bfloat16)


def combine(picks, made, n_parts, after=()):
    n = len(picks)
    steps = picks[0].shape[0] // n_parts
    local, _, width = made[0].shape
    half = n_parts // 2 * n * BLOCK
    out = pl.BlockSpec((1, half, width), lambda i: (i, 0, 0))
    return call(
        functools.partial(combine_kernel, n),
        2 * steps,
        (steps,),
        [pl.BlockSpec((n_parts,) + picks[0].shape[1:], lambda i: (i, 0, 0))] * n
        + [pl.BlockSpec((local, n_parts * CAP, width), lambda i: (0, i, 0))] * n
        + [ANYWHERE] * len(after),
        [out, out],
        [jax.ShapeDtypeStruct((steps, half, width), jnp.bfloat16)] * 2,
        [],
        "combine",
    )(*picks, *made, *after)


def attend_kernel(starts, kdim, first_ref, last_ref, kpos_ref, q_ref, *refs):
    n = len(starts)
    parts, (out_ref, even, odd) = refs[:n], refs[n:]
    rows = q_ref.shape[0]
    start = max(parts[0].shape[1] - even.shape[1], 0)
    wide = even.shape[1]
    half = wide - kdim

    @pl.when(pl.program_id(0) == 0)
    def _():
        pad = jnp.zeros((rows, half), jnp.bfloat16)
        for i in range(n):
            at = slice(i * rows, (i + 1) * rows)
            keys = parts[i][starts[i] : starts[i] + rows, start : start + kdim]
            even[at, :] = jnp.concatenate([keys, pad], axis=1)
            odd[at, :] = jnp.concatenate([pad, keys], axis=1)

    allowed = (kpos_ref[...] >= first_ref[...]) & (kpos_ref[...] <= last_ref[...])
    for i, keys in enumerate((even, odd)):
        at = i * (kdim - half)
        scores = lax.dot_general(
            q_ref[:, at : at + wide], keys[...], NT, preferred_element_type=jnp.float32
        )
        scores = jnp.where(allowed, scores * qk_scale, -1e30)
        expo = jnp.exp(scores - jnp.max(scores, axis=-1, keepdims=True))
        probs = (expo / jnp.sum(expo, axis=-1, keepdims=True)).astype(jnp.bfloat16)
        out_ref[:, i * LATENT : (i + 1) * LATENT] = jnp.dot(
            probs, even[:, :LATENT], preferred_element_type=jnp.float32
        ).astype(jnp.bfloat16)


def attend(queries, parts, first, last, kpos):
    n = len(parts)
    rows, kdim = queries.shape[0], queries.shape[1] // HEADS
    wide = -(-kdim // LANES) * LANES
    return call(
        functools.partial(attend_kernel, [at for _, at in parts], kdim),
        6,
        (HEADS // 2,),
        [whole(first), whole(last), whole(kpos)]
        + [pl.BlockSpec((rows, 2 * kdim), lambda h: (0, h))]
        + [whole(p) for p, _ in parts],
        pl.BlockSpec((rows, 2 * LATENT), lambda h: (0, h)),
        jax.ShapeDtypeStruct((rows, HEADS * LATENT), jnp.bfloat16),
        [pltpu.VMEM((n * rows, wide), jnp.bfloat16)] * 2,
        "attention",
    )(first, last, kpos, queries, *[p for p, _ in parts])


def added(*terms):
    total = terms[0].astype(jnp.float32)
    for term in terms[1:]:
        total = total + term.astype(jnp.float32)
    return total.astype(jnp.bfloat16)


def shards(queries, latent_kv, doc_lengths, hidden_in, router_weight, expert_ids, gate_up, w_down):
    tok_rows, width = hidden_in.shape[1:]
    n_ctx, n_exp = lax.axis_size("ctx"), lax.axis_size("exp")
    ctx, exp = lax.axis_index("ctx"), lax.axis_index("exp")
    local = gate_up.shape[0]
    near = n_exp == 4
    shifts = [0, 1, 3, 2] if near else [0]
    tokens = hidden_in[0]

    def flip(a, bit):
        return lax.ppermute(a, "ctx", [(i, i ^ bit) for i in range(n_ctx)])

    def shift(a, d):
        return lax.ppermute(a, "exp", [(i, i ^ d) for i in range(n_exp)])

    def along_exp(a):
        if near:
            beside, across = shift(a, 1), shift(a, 3)
            return [a, beside, across, shift(across, 1)]
        return [lax.all_gather(a, "exp", axis=0, tiled=True)]

    masks = [0, 2, 1, 3]
    order = jnp.stack([ctx ^ m for m in masks])

    top = expert_ids.shape[2]
    picks = expert_ids[0].T.astype(jnp.bfloat16).reshape(1, top * tok_rows)
    picks = jnp.pad(picks, ((0, EXTRA - 1), (0, width - top * tok_rows)))
    packed = jnp.concatenate([tokens, picks], axis=0)

    keys = latent_kv[0]
    keys = jnp.concatenate([keys, flip(keys, 2)], axis=0)
    near_parts = along_exp(packed)
    arrived = near_parts
    crossed = [flip(a, 2) for a in near_parts[:3]]
    if near:
        crossed.append(shift(crossed[2], 1))
    kv = [(a, k * tok_rows) for a in (keys, flip(keys, 1)) for k in range(2)]
    if near:
        blocks = 1
        gu, token = sort_rows(gate_up, [(), (arrived[1],), (crossed[2],)])
        pairs = [
            stack(a, b, (token,)) if i == 1 else jnp.concatenate([a, b], axis=0)
            for i, (a, b) in enumerate(zip(near_parts, crossed))
        ]
        flipped = [flip(a, 1) for a in pairs]
        spread = [[(a, 0), (a, 1), (b, 0), (b, 1)] for a, b in zip(pairs, flipped)]
    else:
        gu, _ = sort_rows(gate_up, [(), (), ()])
        blocks = near_parts[0].shape[0] // (BLOCK + EXTRA)
        spread = [[(near_parts[0], 0), (crossed[0], 0)]]
        spread[0] = spread[0] + [(flip(a, 1), 0) for a, _ in spread[0]]
    lengths = doc_lengths[0]
    ends = jnp.cumsum(lengths)
    row_pos = order[:, None] * tok_rows + jnp.arange(tok_rows, dtype=jnp.int32)[None, :]
    pos = row_pos[0]
    passed = pos[:, None] >= ends[None, :]
    first = jnp.max(jnp.where(passed, ends[None, :], 0), axis=1)
    context = attend(queries[0], kv, first[:, None], pos[:, None], row_pos.reshape(1, -1))

    seg = jnp.sum((row_pos[..., None] >= ends).astype(jnp.int32), axis=-1)
    sizes = lengths.astype(jnp.float32)
    scale = jnp.broadcast_to((EXPERTS / (top * sizes * sizes))[:, None], (NDOC, LANES))

    base = (exp * local).reshape(1).astype(jnp.int32)
    rw = jnp.roll(router_weight.T, -exp * local, axis=0)
    balance = None
    sent = []
    for i in range(len(shifts)):
        row = (seg.reshape(-1, 1, BLOCK), scale) if near and i == 0 else None
        out = dispatch(spread[i], blocks, top, base, rw, local, row)
        sent.append(out[:3])
        if row is not None:
            balance = out[3]
    made = experts([a[0] for a in sent], [a[1] for a in sent], gu, w_down)
    back = []
    for i in [3, 1, 2, 0][-len(shifts) :]:
        keep, give = combine([sent[i][2]], [made[i]], n_ctx)
        got = flip(give, 1)
        far = added(keep[:, tok_rows:], got[:, tok_rows:])
        terms = [keep[:, :tok_rows], got[:, :tok_rows], flip(far, 2)]
        if shifts[i] == 2:
            joining = [shift(added(*terms), 1)]
        elif i:
            back.append(shift(added(*terms, *(joining if shifts[i] == 3 else [])), shifts[i]))
        else:
            back = back + terms
    if near:
        expert_mix = added(*back)
    else:
        expert_mix = lax.psum_scatter(
            added(*back).reshape(-1, width), "exp", scatter_dimension=0, tiled=True
        ).reshape(1, tok_rows, width)

    if balance is None:
        row = lax.all_gather(tokens, "ctx", axis=0, tiled=True)
        router = jax.nn.softmax(
            jnp.dot(row, router_weight, preferred_element_type=jnp.float32), axis=-1
        )
        row_ids = lax.all_gather(expert_ids[0], "ctx", axis=0, tiled=True)
        hot = (row_ids[:, :, None] == jnp.arange(EXPERTS, dtype=jnp.int32)).astype(jnp.float32)
        at = jnp.arange(row.shape[0], dtype=jnp.int32)
        seg_at = jnp.sum((at[:, None] >= ends[None, :]).astype(jnp.int32), axis=1)
        seg_hot = (seg_at[:, None] == jnp.arange(NDOC, dtype=jnp.int32)).astype(jnp.float32)
        exact = lax.Precision.HIGHEST
        counts = jnp.dot(seg_hot.T, hot.sum(axis=1), precision=exact)
        mass = jnp.dot(seg_hot.T, router, precision=exact)
        per_doc = jnp.sum(counts * mass, axis=1) * scale[:, 0]
    else:
        per_doc = balance[:, 0]
    return context[None], expert_mix, per_doc.reshape(1, NDOC)


def solution(mesh):
    rows = P(("group", "exp"), "ctx", None)
    docs = P(("group", "exp"), None)
    return jax.shard_map(
        shards,
        mesh=mesh,
        in_specs=(rows, rows, docs, rows, P(), rows, P("exp", "ctx", None, None), P("exp", "ctx", None)),
        out_specs=(rows, rows, docs),
        check_vma=False,
    )
```

```python
import functools

import jax
import jax.numpy as jnp
from jax import lax
from jax.experimental import pallas as pl
from jax.experimental.pallas import tpu as pltpu
from jax.sharding import PartitionSpec as P

EXPERTS = 64
HEADS = 8
LATENT = 512
CAP = 16
NDOC = 8
BLOCK = 128
LANES = 128
EXPERT_ROWS = 256
EXTRA = 16
VMEM = 14 * 2**20
VMEM_EXPERTS = 24 * 2**20
VMEM_SORT = 52 * 2**20
PIECES = (0.5, 0.75, 1.0)
DEPTH = 3
PEAK = 1.1e9

qk_scale = 192.0 ** (-0.5)
NT = (((1,), (1,)), ((), ()))
TN = (((0,), (0,)), ((), ()))


def call(kernel, micros, grid, in_specs, out_specs, out_shape, scratch, name, limit=VMEM, aliases={}):
    return pl.pallas_call(
        kernel,
        grid=grid,
        in_specs=in_specs,
        out_specs=out_specs,
        out_shape=out_shape,
        scratch_shapes=scratch,
        input_output_aliases=aliases,
        compiler_params=pltpu.CompilerParams(
            dimension_semantics=("arbitrary",) * len(grid) if grid else None, vmem_limit_bytes=limit
        ),
        cost_estimate=pl.CostEstimate(
            flops=int(micros * PEAK), bytes_accessed=0, transcendentals=0
        ),
        name=name,
    )


def dispatch_kernel(starts, n_row, top, base_ref, rw_ref, *refs):
    n_parts = len(starts)
    parts, refs = refs[:n_parts], refs[n_parts:]
    if n_row:
        seg_ref, scale_ref = refs[:2]
        refs = refs[2:]
    rows_ref, weight_ref, picks_ref = refs[:3]
    local = rows_ref.shape[0]
    width = rows_ref.shape[2]
    names = lax.broadcasted_iota(jnp.int32, (EXPERTS, BLOCK), 0).astype(jnp.float32)
    base = base_ref[0].astype(jnp.float32)
    before = (
        lax.broadcasted_iota(jnp.int32, (BLOCK, BLOCK), 0)
        < lax.broadcasted_iota(jnp.int32, (BLOCK, BLOCK), 1)
    ).astype(jnp.bfloat16)
    slot = lax.broadcasted_iota(jnp.int32, (local, CAP, BLOCK), 1).astype(jnp.float32)
    hots, probs = [], []
    for p in range(n_parts):
        s = starts[p]
        x = parts[p][s : s + BLOCK, :]
        ids = parts[p][s + BLOCK : s + BLOCK + EXTRA, :].astype(jnp.float32)[0:1] - base
        ids = jnp.where(ids < 0.0, ids + EXPERTS, ids)
        logits = lax.dot_general(rw_ref[...], x, NT, preferred_element_type=jnp.float32)
        expo = jnp.exp(logits - jnp.max(logits, axis=0, keepdims=True))
        prob = expo / jnp.sum(expo, axis=0, keepdims=True)
        hot = names == ids[:, :BLOCK]
        for k in range(1, top):
            hot = hot | (names == ids[:, k * BLOCK : (k + 1) * BLOCK])
        hot = hot.astype(jnp.float32)
        chosen = prob * hot
        gate = chosen[:local] / jnp.sum(chosen, axis=0, keepdims=True)
        own = hot[:local]
        rank = jnp.dot(own.astype(jnp.bfloat16), before, preferred_element_type=jnp.float32)
        key = jnp.where(own > 0.0, rank, -1.0)
        pick = (key[:, None, :] == slot).astype(jnp.float32)
        at = slice(p * CAP, (p + 1) * CAP)
        weight_ref[:, at, :] = jnp.broadcast_to(
            jnp.sum(pick * gate[:, None, :], axis=-1, keepdims=True), (local, CAP, LANES)
        )
        pick = pick.reshape(local * CAP, BLOCK).astype(jnp.bfloat16)
        picks_ref[p] = pick
        taken = jnp.dot(pick, x, preferred_element_type=jnp.float32)
        rows_ref[:, at, :] = taken.astype(jnp.bfloat16).reshape(local, CAP, width)
        hots.append(hot)
        probs.append(prob)
    if n_row:
        bal_ref = refs[3]
        for d in range(NDOC):
            counts = jnp.zeros((EXPERTS, BLOCK), jnp.float32)
            mass = jnp.zeros((EXPERTS, BLOCK), jnp.float32)
            for p in range(n_row):
                inside = seg_ref[p] == d
                counts = counts + jnp.where(inside, hots[p], 0.0)
                mass = mass + jnp.where(inside, probs[p], 0.0)
            both = jnp.sum(counts, axis=1, keepdims=True) * jnp.sum(mass, axis=1, keepdims=True)
            bal_ref[d : d + 1, :] = (
                jnp.broadcast_to(jnp.sum(both, axis=0, keepdims=True), (1, LANES))
                * scale_ref[d : d + 1, :]
            )


IN_HBM = pl.BlockSpec(memory_space=pltpu.HBM)
ANYWHERE = pl.BlockSpec(memory_space=pl.ANY)


IN_VMEM = pl.BlockSpec(memory_space=pltpu.VMEM)


def whole(a):
    return pl.BlockSpec(a.shape, lambda *i: (0,) * a.ndim)


def dispatch(parts, n, top, base, rw, local, row=None):
    n_parts = len(parts)
    width = rw.shape[1]
    slots = n_parts * CAP
    in_specs = [
        pl.BlockSpec(memory_space=pltpu.SMEM),
        whole(rw),
    ] + [
        pl.BlockSpec((BLOCK + EXTRA, width), lambda i, k=k: (k + i, 0)) for _, k in parts
    ]
    out_specs = [
        pl.BlockSpec((local, slots, width), lambda i: (0, i, 0)),
        pl.BlockSpec((local, slots, LANES), lambda i: (0, i, 0)),
        pl.BlockSpec((n_parts, local * CAP, BLOCK), lambda i: (i, 0, 0)),
    ]
    out_shape = [
        jax.ShapeDtypeStruct((local, n * slots, width), jnp.bfloat16),
        jax.ShapeDtypeStruct((local, n * slots, LANES), jnp.float32),
        jax.ShapeDtypeStruct((n * n_parts, local * CAP, BLOCK), jnp.bfloat16),
    ]
    extra = ()
    if row is not None:
        extra = row
        in_specs += [whole(a) for a in row]
        out_specs.append(pl.BlockSpec((NDOC, LANES), lambda i: (0, 0)))
        out_shape.append(jax.ShapeDtypeStruct((NDOC, LANES), jnp.float32))
    grid, starts = (n,), [0] * n_parts
    if n == 1:
        grid, starts = (), [k * (BLOCK + EXTRA) for _, k in parts]
        in_specs = in_specs[:1] + [IN_VMEM] * (len(in_specs) - 1)
        out_specs = [IN_VMEM] * len(out_specs)
    return call(
        functools.partial(dispatch_kernel, starts, n_parts if row is not None else 0, top),
        3 * n,
        grid,
        in_specs,
        out_specs,
        out_shape,
        [],
        "dispatch",
    )(base, rw, *[a for a, _ in parts], *extra)


def fetch(sources, slots, sem, step, steps, first, start=0):
    depth, group = slots[0].shape[:2]

    def copies(at):
        slot = lax.rem(at, depth)
        return [
            pltpu.make_async_copy(
                source.at[start + at * group + e], held.at[slot, e], sem.at[i, slot, e]
            )
            for i, (source, held) in enumerate(zip(sources, slots))
            for e in range(group)
        ]

    @pl.when(first & (step == 0))
    def _():
        for ahead in range(depth - 1):

            @pl.when(ahead < steps)
            def _():
                for copy in copies(step + ahead):
                    copy.start()

    @pl.when(first & (step + depth - 1 < steps))
    def _():
        for copy in copies(step + depth - 1):
            copy.start()

    @pl.when(first)
    def _():
        for copy in copies(step):
            copy.wait()

    return lax.rem(step, depth)


def sort_kernel(start, gu_ref, *refs):
    out_ref, token_ref, held, made, wide, in_sem, out_sem = refs[-7:]
    token_ref[...] = jnp.zeros_like(token_ref)
    step, steps = pl.program_id(0), pl.num_programs(0)
    _, group, _, hidden, width = made.shape
    chunks = width // LANES
    slot = fetch([gu_ref], [held], in_sem, step, steps, step >= 0, start)
    to = lax.rem(step, 2)

    def leave(at):
        to = lax.rem(at, 2)
        return pltpu.make_async_copy(
            made.at[to], out_ref.at[pl.ds(start + at * group, group)], out_sem.at[to]
        )

    @pl.when(step >= 2)
    def _():
        leave(step - 2).wait()

    for e in range(group):
        wide[e] = held[slot, e].astype(jnp.float32)
        for z in range(2):
            for c in range(chunks):
                part = wide[e, pl.ds(2 * c + z, hidden, stride=2 * chunks), :]
                made[to, e, z, :, c * LANES : (c + 1) * LANES] = part.astype(jnp.bfloat16)
    leave(step).start()

    @pl.when(step == steps - 1)
    def _():
        @pl.when(step >= 1)
        def _():
            leave(step - 1).wait()

        leave(step).wait()


def sort_rows(gate_up, behind):
    local, hidden, _, width = gate_up.shape
    ends = [int(local * p) for p in PIECES] if local % 8 == 0 else [local]
    group = 2 if local % 2 == 0 else 1
    chunks = width // LANES
    gu = gate_up.reshape(local, hidden, 2, chunks, LANES).swapaxes(2, 3)
    gu = gu.reshape(local, hidden * 2 * chunks, LANES)
    done = ()
    for j, end in enumerate(ends):
        start = ends[j - 1] if j else 0
        after = behind[j] if len(ends) > 1 else ()
        *done, token = (
            call(
                functools.partial(sort_kernel, start),
                8,
                ((end - start) // group,),
                [IN_HBM] + [IN_HBM] * len(done) + [ANYWHERE] * len(after),
                [IN_HBM, pl.BlockSpec((8, LANES), lambda e: (0, 0))],
                [
                    jax.ShapeDtypeStruct((local, 2, hidden, width), jnp.bfloat16),
                    jax.ShapeDtypeStruct((8, LANES), jnp.float32),
                ],
                [
                    pltpu.VMEM((DEPTH, group) + gu.shape[1:], jnp.bfloat16),
                    pltpu.VMEM((2, group, 2, hidden, width), jnp.bfloat16),
                    pltpu.VMEM((group,) + gu.shape[1:], jnp.float32),
                    pltpu.SemaphoreType.DMA((1, DEPTH, group)),
                    pltpu.SemaphoreType.DMA((2,)),
                ],
                "sort",
                VMEM_SORT,
                {1: 0} if done else {},
            )(gu, *done, *after)
        )
    return done[0], token


def stack_kernel(a_ref, b_ref, *refs):
    rows = a_ref.shape[0]
    refs[-1][:rows, :] = a_ref[...]
    refs[-1][rows:, :] = b_ref[...]


def stack(a, b, before):
    rows, width = a.shape
    return call(
        stack_kernel,
        1,
        (1,),
        [whole(a), whole(b)] + [ANYWHERE] * len(before),
        pl.BlockSpec((2 * rows, width), lambda i: (0, 0)),
        jax.ShapeDtypeStruct((2 * rows, width), a.dtype),
        [],
        "stack",
    )(a, b, *before)


def expert_kernel(n, *refs):
    rows, weights = refs[:n], refs[n : 2 * n]
    gu_ref, down_ref = refs[2 * n : 2 * n + 2]
    outs, (gu, down, sem) = refs[-3 - n : -3], refs[-3:]
    group = gu.shape[1]
    size = rows[0].shape[1]
    slot = fetch(
        [gu_ref, down_ref],
        [gu, down],
        sem,
        pl.program_id(0),
        pl.num_programs(0),
        pl.program_id(1) == 0,
    )
    for e in range(group):
        held = jnp.concatenate([r[e] for r in rows], axis=0)
        g = lax.dot_general(held, gu[slot, e, 0], NT, preferred_element_type=jnp.float32)
        u = lax.dot_general(held, gu[slot, e, 1], NT, preferred_element_type=jnp.float32)
        inner = (g * lax.logistic(g) * u).astype(jnp.bfloat16)
        made = jnp.dot(inner, down[slot, e], preferred_element_type=jnp.float32)
        for i in range(n):
            w = weights[i][e]
            part = made[i * size : (i + 1) * size]
            for c in range(part.shape[1] // LANES):
                at = slice(c * LANES, (c + 1) * LANES)
                outs[i][e, :, at] = (part[:, at] * w).astype(jnp.bfloat16)


def experts(rows, weights, gu, down, after=()):
    n = len(rows)
    local, slots, width = rows[0].shape
    size = min(slots, EXPERT_ROWS)
    hidden = down.shape[1]
    group = 2 if local % 2 == 0 else 1
    rows_spec = pl.BlockSpec((group, size, width), lambda e, i: (e, i, 0))
    weight_spec = pl.BlockSpec((group, size, LANES), lambda e, i: (e, i, 0))
    return call(
        functools.partial(expert_kernel, n),
        6,
        (local // group, slots // size),
        [rows_spec] * n + [weight_spec] * n + [IN_HBM, IN_HBM] + [ANYWHERE] * len(after),
        [rows_spec] * n,
        [jax.ShapeDtypeStruct(r.shape, jnp.bfloat16) for r in rows],
        [
            pltpu.VMEM((DEPTH, group, 2, hidden, width), jnp.bfloat16),
            pltpu.VMEM((DEPTH, group, hidden, width), jnp.bfloat16),
            pltpu.SemaphoreType.DMA((2, DEPTH, group)),
        ],
        "experts",
        VMEM_EXPERTS,
    )(*rows, *weights, gu, down, *after)


def combine_kernel(n, *refs):
    picks, made, outs = refs[:n], refs[n : 2 * n], refs[-2:]
    local, _, width = made[0].shape
    parts = picks[0].shape[0]
    half = parts // 2
    for i in range(n):
        for p in range(parts):
            held = made[i][:, p * CAP : (p + 1) * CAP, :].reshape(local * CAP, width)
            mix = lax.dot_general(picks[i][p], held, TN, preferred_element_type=jnp.float32)
            at = ((p % half) * n + i) * BLOCK
            outs[p // half][0, at : at + BLOCK, :] = mix.astype(jnp.bfloat16)


def combine(picks, made, n_parts, after=()):
    n = len(picks)
    steps = picks[0].shape[0] // n_parts
    local, _, width = made[0].shape
    half = n_parts // 2 * n * BLOCK
    out = pl.BlockSpec((1, half, width), lambda i: (i, 0, 0))
    return call(
        functools.partial(combine_kernel, n),
        2 * steps,
        (steps,),
        [pl.BlockSpec((n_parts,) + picks[0].shape[1:], lambda i: (i, 0, 0))] * n
        + [pl.BlockSpec((local, n_parts * CAP, width), lambda i: (0, i, 0))] * n
        + [ANYWHERE] * len(after),
        [out, out],
        [jax.ShapeDtypeStruct((steps, half, width), jnp.bfloat16)] * 2,
        [],
        "combine",
    )(*picks, *made, *after)


def join_kernel(a_ref, b_ref, c_ref, *refs):
    rows = c_ref.shape[1]
    total = a_ref[:, :rows, :].astype(jnp.float32) + b_ref[:, :rows, :].astype(jnp.float32)
    refs[-1][...] = (total + c_ref[...].astype(jnp.float32)).astype(jnp.bfloat16)


def join(a, b, c, before):
    return call(
        join_kernel,
        1,
        (),
        [IN_VMEM] * 3 + [ANYWHERE] * len(before),
        IN_VMEM,
        jax.ShapeDtypeStruct(c.shape, c.dtype),
        [],
        "join",
    )(a, b, c, *before)


def attend_kernel(starts, kdim, first_ref, last_ref, kpos_ref, q_ref, *refs):
    n = len(starts)
    parts, (out_ref, even, odd) = refs[:n], refs[n:]
    rows = q_ref.shape[0]
    start = max(parts[0].shape[1] - even.shape[1], 0)
    wide = even.shape[1]
    half = wide - kdim

    @pl.when(pl.program_id(0) == 0)
    def _():
        pad = jnp.zeros((rows, half), jnp.bfloat16)
        for i in range(n):
            at = slice(i * rows, (i + 1) * rows)
            keys = parts[i][starts[i] : starts[i] + rows, start : start + kdim]
            even[at, :] = jnp.concatenate([keys, pad], axis=1)
            odd[at, :] = jnp.concatenate([pad, keys], axis=1)

    allowed = (kpos_ref[...] >= first_ref[...]) & (kpos_ref[...] <= last_ref[...])
    for i, keys in enumerate((even, odd)):
        at = i * (kdim - half)
        scores = lax.dot_general(
            q_ref[:, at : at + wide], keys[...], NT, preferred_element_type=jnp.float32
        )
        scores = jnp.where(allowed, scores * qk_scale, -1e30)
        expo = jnp.exp(scores - jnp.max(scores, axis=-1, keepdims=True))
        probs = (expo / jnp.sum(expo, axis=-1, keepdims=True)).astype(jnp.bfloat16)
        out_ref[:, i * LATENT : (i + 1) * LATENT] = jnp.dot(
            probs, even[:, :LATENT], preferred_element_type=jnp.float32
        ).astype(jnp.bfloat16)


def attend(queries, parts, first, last, kpos):
    n = len(parts)
    rows, kdim = queries.shape[0], queries.shape[1] // HEADS
    wide = -(-kdim // LANES) * LANES
    return call(
        functools.partial(attend_kernel, [at for _, at in parts], kdim),
        6,
        (HEADS // 2,),
        [whole(first), whole(last), whole(kpos)]
        + [pl.BlockSpec((rows, 2 * kdim), lambda h: (0, h))]
        + [whole(p) for p, _ in parts],
        pl.BlockSpec((rows, 2 * LATENT), lambda h: (0, h)),
        jax.ShapeDtypeStruct((rows, HEADS * LATENT), jnp.bfloat16),
        [pltpu.VMEM((n * rows, wide), jnp.bfloat16)] * 2,
        "attention",
    )(first, last, kpos, queries, *[p for p, _ in parts])


def added(*terms):
    total = terms[0].astype(jnp.float32)
    for term in terms[1:]:
        total = total + term.astype(jnp.float32)
    return total.astype(jnp.bfloat16)


def shards(queries, latent_kv, doc_lengths, hidden_in, router_weight, expert_ids, gate_up, w_down):
    tok_rows, width = hidden_in.shape[1:]
    n_ctx, n_exp = lax.axis_size("ctx"), lax.axis_size("exp")
    ctx, exp = lax.axis_index("ctx"), lax.axis_index("exp")
    local = gate_up.shape[0]
    near = n_exp == 4
    shifts = [0, 1, 3, 2] if near else [0]
    tokens = hidden_in[0]

    def flip(a, bit):
        return lax.ppermute(a, "ctx", [(i, i ^ bit) for i in range(n_ctx)])

    def shift(a, d):
        return lax.ppermute(a, "exp", [(i, i ^ d) for i in range(n_exp)])

    def along_exp(a):
        if near:
            beside, across = shift(a, 1), shift(a, 3)
            return [a, beside, across, shift(across, 1)]
        return [lax.all_gather(a, "exp", axis=0, tiled=True)]

    masks = [0, 2, 1, 3]
    order = jnp.stack([ctx ^ m for m in masks])

    top = expert_ids.shape[2]
    picks = expert_ids[0].T.astype(jnp.bfloat16).reshape(1, top * tok_rows)
    picks = jnp.pad(picks, ((0, EXTRA - 1), (0, width - top * tok_rows)))
    packed = jnp.concatenate([tokens, picks], axis=0)

    keys = latent_kv[0]
    keys = jnp.concatenate([keys, flip(keys, 2)], axis=0)
    near_parts = along_exp(packed)
    arrived = near_parts
    crossed = [flip(a, 2) for a in near_parts[:3]]
    if near:
        crossed.append(shift(crossed[2], 1))
    kv = [(a, k * tok_rows) for a in (keys, flip(keys, 1)) for k in range(2)]
    if near:
        blocks = 1
        gu, token = sort_rows(gate_up, [(), (arrived[1],), (crossed[2],)])
        pairs = [
            stack(a, b, (token,)) if i == 1 else jnp.concatenate([a, b], axis=0)
            for i, (a, b) in enumerate(zip(near_parts, crossed))
        ]
        flipped = [flip(a, 1) for a in pairs]
        spread = [[(a, 0), (a, 1), (b, 0), (b, 1)] for a, b in zip(pairs, flipped)]
    else:
        gu, _ = sort_rows(gate_up, [(), (), ()])
        blocks = near_parts[0].shape[0] // (BLOCK + EXTRA)
        spread = [[(near_parts[0], 0), (crossed[0], 0)]]
        spread[0] = spread[0] + [(flip(a, 1), 0) for a, _ in spread[0]]
    lengths = doc_lengths[0]
    ends = jnp.cumsum(lengths)
    row_pos = order[:, None] * tok_rows + jnp.arange(tok_rows, dtype=jnp.int32)[None, :]
    pos = row_pos[0]
    passed = pos[:, None] >= ends[None, :]
    first = jnp.max(jnp.where(passed, ends[None, :], 0), axis=1)
    context = attend(queries[0], kv, first[:, None], pos[:, None], row_pos.reshape(1, -1))

    seg = jnp.sum((row_pos[..., None] >= ends).astype(jnp.int32), axis=-1)
    sizes = lengths.astype(jnp.float32)
    scale = jnp.broadcast_to((EXPERTS / (top * sizes * sizes))[:, None], (NDOC, LANES))

    base = (exp * local).reshape(1).astype(jnp.int32)
    rw = jnp.roll(router_weight.T, -exp * local, axis=0)
    balance = None
    sent = []
    for i in range(len(shifts)):
        row = (seg.reshape(-1, 1, BLOCK), scale) if near and i == 0 else None
        out = dispatch(spread[i], blocks, top, base, rw, local, row)
        sent.append(out[:3])
        if row is not None:
            balance = out[3]
    made = experts([a[0] for a in sent], [a[1] for a in sent], gu, w_down)
    back = []
    for i in reversed(range(len(shifts))):
        keep, give = combine([sent[i][2]], [made[i]], n_ctx)
        got = flip(give, 1)
        far = added(keep[:, tok_rows:], got[:, tok_rows:])
        crossed_sum = flip(far, 2)
        terms = [keep[:, :tok_rows], got[:, :tok_rows], crossed_sum]
        if shifts[i] == 2:
            joining = shift(added(*terms), 1)
        elif shifts[i] == 3:
            across = added(*terms, joining)
            back.append(shift(across, 3))
        elif i:
            back.append(shift(join(keep, got, crossed_sum, (across,)), 1))
        else:
            back = back + terms
    if near:
        expert_mix = added(*back)
    else:
        expert_mix = lax.psum_scatter(
            added(*back).reshape(-1, width), "exp", scatter_dimension=0, tiled=True
        ).reshape(1, tok_rows, width)

    if balance is None:
        row = lax.all_gather(tokens, "ctx", axis=0, tiled=True)
        router = jax.nn.softmax(
            jnp.dot(row, router_weight, preferred_element_type=jnp.float32), axis=-1
        )
        row_ids = lax.all_gather(expert_ids[0], "ctx", axis=0, tiled=True)
        hot = (row_ids[:, :, None] == jnp.arange(EXPERTS, dtype=jnp.int32)).astype(jnp.float32)
        at = jnp.arange(row.shape[0], dtype=jnp.int32)
        seg_at = jnp.sum((at[:, None] >= ends[None, :]).astype(jnp.int32), axis=1)
        seg_hot = (seg_at[:, None] == jnp.arange(NDOC, dtype=jnp.int32)).astype(jnp.float32)
        exact = lax.Precision.HIGHEST
        counts = jnp.dot(seg_hot.T, hot.sum(axis=1), precision=exact)
        mass = jnp.dot(seg_hot.T, router, precision=exact)
        per_doc = jnp.sum(counts * mass, axis=1) * scale[:, 0]
    else:
        per_doc = balance[:, 0]
    return context[None], expert_mix, per_doc.reshape(1, NDOC)


def solution(mesh):
    rows = P(("group", "exp"), "ctx", None)
    docs = P(("group", "exp"), None)
    return jax.shard_map(
        shards,
        mesh=mesh,
        in_specs=(rows, rows, docs, rows, P(), rows, P("exp", "ctx", None, None), P("exp", "ctx", None)),
        out_specs=(rows, rows, docs),
        check_vma=False,
    )
```

```python
import functools

import jax
import jax.numpy as jnp
from jax import lax
from jax.experimental import pallas as pl
from jax.experimental.pallas import tpu as pltpu
from jax.sharding import PartitionSpec as P

EXPERTS = 64
HEADS = 8
LATENT = 512
CAP = 16
NDOC = 8
BLOCK = 128
LANES = 128
EXPERT_ROWS = 256
EXTRA = 16
VMEM = 14 * 2**20
VMEM_EXPERTS = 24 * 2**20
VMEM_SORT = 52 * 2**20
PIECES = (0.5, 0.75, 1.0)
DEPTH = 3
PEAK = 1.1e9

qk_scale = 192.0 ** (-0.5)
NT = (((1,), (1,)), ((), ()))
TN = (((0,), (0,)), ((), ()))


def call(kernel, micros, grid, in_specs, out_specs, out_shape, scratch, name, limit=VMEM, aliases={}):
    return pl.pallas_call(
        kernel,
        grid=grid,
        in_specs=in_specs,
        out_specs=out_specs,
        out_shape=out_shape,
        scratch_shapes=scratch,
        input_output_aliases=aliases,
        compiler_params=pltpu.CompilerParams(
            dimension_semantics=("arbitrary",) * len(grid) if grid else None, vmem_limit_bytes=limit
        ),
        cost_estimate=pl.CostEstimate(
            flops=int(micros * PEAK), bytes_accessed=0, transcendentals=0
        ),
        name=name,
    )


def dispatch_kernel(starts, n_row, top, base_ref, rw_ref, *refs):
    n_parts = len(starts)
    parts, refs = refs[:n_parts], refs[n_parts:]
    if n_row:
        seg_ref, scale_ref = refs[:2]
        refs = refs[2:]
    rows_ref, weight_ref, picks_ref = refs[:3]
    local = rows_ref.shape[0]
    width = rows_ref.shape[2]
    names = lax.broadcasted_iota(jnp.int32, (EXPERTS, BLOCK), 0).astype(jnp.float32)
    base = base_ref[0].astype(jnp.float32)
    before = (
        lax.broadcasted_iota(jnp.int32, (BLOCK, BLOCK), 0)
        < lax.broadcasted_iota(jnp.int32, (BLOCK, BLOCK), 1)
    ).astype(jnp.bfloat16)
    slot = lax.broadcasted_iota(jnp.int32, (local, CAP, BLOCK), 1).astype(jnp.float32)
    hots, probs = [], []
    for p in range(n_parts):
        s = starts[p]
        x = parts[p][s : s + BLOCK, :]
        ids = parts[p][s + BLOCK : s + BLOCK + EXTRA, :].astype(jnp.float32)[0:1] - base
        ids = jnp.where(ids < 0.0, ids + EXPERTS, ids)
        logits = lax.dot_general(rw_ref[...], x, NT, preferred_element_type=jnp.float32)
        expo = jnp.exp(logits - jnp.max(logits, axis=0, keepdims=True))
        prob = expo / jnp.sum(expo, axis=0, keepdims=True)
        hot = names == ids[:, :BLOCK]
        for k in range(1, top):
            hot = hot | (names == ids[:, k * BLOCK : (k + 1) * BLOCK])
        hot = hot.astype(jnp.float32)
        chosen = prob * hot
        gate = chosen[:local] / jnp.sum(chosen, axis=0, keepdims=True)
        own = hot[:local]
        rank = jnp.dot(own.astype(jnp.bfloat16), before, preferred_element_type=jnp.float32)
        key = jnp.where(own > 0.0, rank, -1.0)
        pick = (key[:, None, :] == slot).astype(jnp.float32)
        at = slice(p * CAP, (p + 1) * CAP)
        weight_ref[:, at, :] = jnp.broadcast_to(
            jnp.sum(pick * gate[:, None, :], axis=-1, keepdims=True), (local, CAP, LANES)
        )
        pick = pick.reshape(local * CAP, BLOCK).astype(jnp.bfloat16)
        picks_ref[p] = pick
        taken = jnp.dot(pick, x, preferred_element_type=jnp.float32)
        rows_ref[:, at, :] = taken.astype(jnp.bfloat16).reshape(local, CAP, width)
        hots.append(hot)
        probs.append(prob)
    if n_row:
        bal_ref = refs[3]
        for d in range(NDOC):
            counts = jnp.zeros((EXPERTS, BLOCK), jnp.float32)
            mass = jnp.zeros((EXPERTS, BLOCK), jnp.float32)
            for p in range(n_row):
                inside = seg_ref[p] == d
                counts = counts + jnp.where(inside, hots[p], 0.0)
                mass = mass + jnp.where(inside, probs[p], 0.0)
            both = jnp.sum(counts, axis=1, keepdims=True) * jnp.sum(mass, axis=1, keepdims=True)
            bal_ref[d : d + 1, :] = (
                jnp.broadcast_to(jnp.sum(both, axis=0, keepdims=True), (1, LANES))
                * scale_ref[d : d + 1, :]
            )


IN_HBM = pl.BlockSpec(memory_space=pltpu.HBM)
ANYWHERE = pl.BlockSpec(memory_space=pl.ANY)


IN_VMEM = pl.BlockSpec(memory_space=pltpu.VMEM)


def whole(a):
    return pl.BlockSpec(a.shape, lambda *i: (0,) * a.ndim)


def dispatch(parts, n, top, base, rw, local, row=None):
    n_parts = len(parts)
    width = rw.shape[1]
    slots = n_parts * CAP
    in_specs = [
        pl.BlockSpec(memory_space=pltpu.SMEM),
        whole(rw),
    ] + [
        pl.BlockSpec((BLOCK + EXTRA, width), lambda i, k=k: (k + i, 0)) for _, k in parts
    ]
    out_specs = [
        pl.BlockSpec((local, slots, width), lambda i: (0, i, 0)),
        pl.BlockSpec((local, slots, LANES), lambda i: (0, i, 0)),
        pl.BlockSpec((n_parts, local * CAP, BLOCK), lambda i: (i, 0, 0)),
    ]
    out_shape = [
        jax.ShapeDtypeStruct((local, n * slots, width), jnp.bfloat16),
        jax.ShapeDtypeStruct((local, n * slots, LANES), jnp.float32),
        jax.ShapeDtypeStruct((n * n_parts, local * CAP, BLOCK), jnp.bfloat16),
    ]
    extra = ()
    if row is not None:
        extra = row
        in_specs += [whole(a) for a in row]
        out_specs.append(pl.BlockSpec((NDOC, LANES), lambda i: (0, 0)))
        out_shape.append(jax.ShapeDtypeStruct((NDOC, LANES), jnp.float32))
    grid, starts = (n,), [0] * n_parts
    if n == 1:
        grid, starts = (), [k * (BLOCK + EXTRA) for _, k in parts]
        in_specs = in_specs[:1] + [IN_VMEM] * (len(in_specs) - 1)
        out_specs = [IN_VMEM] * len(out_specs)
    return call(
        functools.partial(dispatch_kernel, starts, n_parts if row is not None else 0, top),
        3 * n,
        grid,
        in_specs,
        out_specs,
        out_shape,
        [],
        "dispatch",
    )(base, rw, *[a for a, _ in parts], *extra)


def fetch(sources, slots, sem, step, steps, first, start=0):
    depth, group = slots[0].shape[:2]

    def copies(at, e):
        slot = lax.rem(at, depth)
        return [
            pltpu.make_async_copy(
                source.at[start + at * group + e], held.at[slot, e], sem.at[i, slot, e]
            )
            for i, (source, held) in enumerate(zip(sources, slots))
        ]

    def begin(at):
        for e in range(group):
            for copy in copies(at, e):
                copy.start()

    @pl.when(first & (step == 0))
    def _():
        for ahead in range(depth - 1):

            @pl.when(ahead < steps)
            def _():
                begin(step + ahead)

    @pl.when(first & (step + depth - 1 < steps))
    def _():
        begin(step + depth - 1)

    def ready(e):
        if first is True:
            for copy in copies(step, e):
                copy.wait()
            return

        @pl.when(first)
        def _():
            for copy in copies(step, e):
                copy.wait()

    return lax.rem(step, depth), ready


def sort_kernel(start, gu_ref, *refs):
    out_ref, token_ref, held, made, wide, in_sem, out_sem = refs[-7:]
    token_ref[...] = jnp.zeros_like(token_ref)
    step, steps = pl.program_id(0), pl.num_programs(0)
    _, group, _, hidden, width = made.shape
    chunks = width // LANES
    slot, ready = fetch([gu_ref], [held], in_sem, step, steps, True, start)
    to = lax.rem(step, 2)

    def leave(at, e):
        to = lax.rem(at, 2)
        return pltpu.make_async_copy(
            made.at[to, e], out_ref.at[start + at * group + e], out_sem.at[to, e]
        )

    @pl.when(step >= 2)
    def _():
        for e in range(group):
            leave(step - 2, e).wait()

    for e in range(group):
        ready(e)
        wide[e] = held[slot, e].astype(jnp.float32)
        for z in range(2):
            for c in range(chunks):
                part = wide[e, pl.ds(2 * c + z, hidden, stride=2 * chunks), :]
                made[to, e, z, :, c * LANES : (c + 1) * LANES] = part.astype(jnp.bfloat16)
        leave(step, e).start()

    @pl.when(step == steps - 1)
    def _():
        @pl.when(step >= 1)
        def _():
            for e in range(group):
                leave(step - 1, e).wait()

        for e in range(group):
            leave(step, e).wait()


def sort_rows(gate_up, behind):
    local, hidden, _, width = gate_up.shape
    ends = [int(local * p) for p in PIECES] if local % 8 == 0 else [local]
    group = 2 if local % 2 == 0 else 1
    chunks = width // LANES
    gu = gate_up.reshape(local, hidden, 2, chunks, LANES).swapaxes(2, 3)
    gu = gu.reshape(local, hidden * 2 * chunks, LANES)
    done = ()
    for j, end in enumerate(ends):
        start = ends[j - 1] if j else 0
        after = behind[j] if len(ends) > 1 else ()
        *done, token = (
            call(
                functools.partial(sort_kernel, start),
                8,
                ((end - start) // group,),
                [IN_HBM] + [IN_HBM] * len(done) + [ANYWHERE] * len(after),
                [IN_HBM, pl.BlockSpec((8, LANES), lambda e: (0, 0))],
                [
                    jax.ShapeDtypeStruct((local, 2, hidden, width), jnp.bfloat16),
                    jax.ShapeDtypeStruct((8, LANES), jnp.float32),
                ],
                [
                    pltpu.VMEM((DEPTH, group) + gu.shape[1:], jnp.bfloat16),
                    pltpu.VMEM((2, group, 2, hidden, width), jnp.bfloat16),
                    pltpu.VMEM((group,) + gu.shape[1:], jnp.float32),
                    pltpu.SemaphoreType.DMA((1, DEPTH, group)),
                    pltpu.SemaphoreType.DMA((2, group)),
                ],
                "sort",
                VMEM_SORT,
                {1: 0} if done else {},
            )(gu, *done, *after)
        )
    return done[0], token


def stack_kernel(a_ref, b_ref, *refs):
    rows = a_ref.shape[0]
    refs[-1][:rows, :] = a_ref[...]
    refs[-1][rows:, :] = b_ref[...]


def stack(a, b, before):
    rows, width = a.shape
    return call(
        stack_kernel,
        1,
        (1,),
        [whole(a), whole(b)] + [ANYWHERE] * len(before),
        pl.BlockSpec((2 * rows, width), lambda i: (0, 0)),
        jax.ShapeDtypeStruct((2 * rows, width), a.dtype),
        [],
        "stack",
    )(a, b, *before)


def expert_kernel(n, *refs):
    rows, weights = refs[:n], refs[n : 2 * n]
    gu_ref, down_ref = refs[2 * n : 2 * n + 2]
    outs, (gu, down, sem) = refs[-3 - n : -3], refs[-3:]
    group = gu.shape[1]
    size = rows[0].shape[1]
    slot, ready = fetch(
        [gu_ref, down_ref],
        [gu, down],
        sem,
        pl.program_id(0),
        pl.num_programs(0),
        pl.program_id(1) == 0,
    )
    for e in range(group):
        ready(e)
    for e in range(group):
        held = jnp.concatenate([r[e] for r in rows], axis=0)
        g = lax.dot_general(held, gu[slot, e, 0], NT, preferred_element_type=jnp.float32)
        u = lax.dot_general(held, gu[slot, e, 1], NT, preferred_element_type=jnp.float32)
        inner = (g * lax.logistic(g) * u).astype(jnp.bfloat16)
        made = jnp.dot(inner, down[slot, e], preferred_element_type=jnp.float32)
        for i in range(n):
            w = weights[i][e]
            part = made[i * size : (i + 1) * size]
            for c in range(part.shape[1] // LANES):
                at = slice(c * LANES, (c + 1) * LANES)
                outs[i][e, :, at] = (part[:, at] * w).astype(jnp.bfloat16)


def experts(rows, weights, gu, down, after=()):
    n = len(rows)
    local, slots, width = rows[0].shape
    size = min(slots, EXPERT_ROWS)
    hidden = down.shape[1]
    group = 4 if local % 4 == 0 else 1
    rows_spec = pl.BlockSpec((group, size, width), lambda e, i: (e, i, 0))
    weight_spec = pl.BlockSpec((group, size, LANES), lambda e, i: (e, i, 0))
    return call(
        functools.partial(expert_kernel, n),
        6,
        (local // group, slots // size),
        [rows_spec] * n + [weight_spec] * n + [IN_HBM, IN_HBM] + [ANYWHERE] * len(after),
        [rows_spec] * n,
        [jax.ShapeDtypeStruct(r.shape, jnp.bfloat16) for r in rows],
        [
            pltpu.VMEM((2, group, 2, hidden, width), jnp.bfloat16),
            pltpu.VMEM((2, group, hidden, width), jnp.bfloat16),
            pltpu.SemaphoreType.DMA((2, 2, group)),
        ],
        "experts",
        VMEM_EXPERTS,
    )(*rows, *weights, gu, down, *after)


def combine_kernel(n, *refs):
    picks, made, outs = refs[:n], refs[n : 2 * n], refs[-2:]
    local, _, width = made[0].shape
    parts = picks[0].shape[0]
    half = parts // 2
    for i in range(n):
        for p in range(parts):
            held = made[i][:, p * CAP : (p + 1) * CAP, :].reshape(local * CAP, width)
            mix = lax.dot_general(picks[i][p], held, TN, preferred_element_type=jnp.float32)
            at = ((p % half) * n + i) * BLOCK
            outs[p // half][0, at : at + BLOCK, :] = mix.astype(jnp.bfloat16)


def combine(picks, made, n_parts, after=()):
    n = len(picks)
    steps = picks[0].shape[0] // n_parts
    local, _, width = made[0].shape
    half = n_parts // 2 * n * BLOCK
    out = pl.BlockSpec((1, half, width), lambda i: (i, 0, 0))
    return call(
        functools.partial(combine_kernel, n),
        2 * steps,
        (steps,),
        [pl.BlockSpec((n_parts,) + picks[0].shape[1:], lambda i: (i, 0, 0))] * n
        + [pl.BlockSpec((local, n_parts * CAP, width), lambda i: (0, i, 0))] * n
        + [ANYWHERE] * len(after),
        [out, out],
        [jax.ShapeDtypeStruct((steps, half, width), jnp.bfloat16)] * 2,
        [],
        "combine",
    )(*picks, *made, *after)


def join_kernel(a_ref, b_ref, c_ref, *refs):
    rows = c_ref.shape[1]
    total = a_ref[:, :rows, :].astype(jnp.float32) + b_ref[:, :rows, :].astype(jnp.float32)
    refs[-1][...] = (total + c_ref[...].astype(jnp.float32)).astype(jnp.bfloat16)


def join(a, b, c, before):
    return call(
        join_kernel,
        1,
        (),
        [IN_VMEM] * 3 + [ANYWHERE] * len(before),
        IN_VMEM,
        jax.ShapeDtypeStruct(c.shape, c.dtype),
        [],
        "join",
    )(a, b, c, *before)


def attend_kernel(starts, kdim, first_ref, last_ref, kpos_ref, q_ref, *refs):
    n = len(starts)
    parts, (out_ref, even, odd) = refs[:n], refs[n:]
    rows = q_ref.shape[0]
    start = max(parts[0].shape[1] - even.shape[1], 0)
    wide = even.shape[1]
    half = wide - kdim

    @pl.when(pl.program_id(0) == 0)
    def _():
        pad = jnp.zeros((rows, half), jnp.bfloat16)
        for i in range(n):
            at = slice(i * rows, (i + 1) * rows)
            keys = parts[i][starts[i] : starts[i] + rows, start : start + kdim]
            even[at, :] = jnp.concatenate([keys, pad], axis=1)
            odd[at, :] = jnp.concatenate([pad, keys], axis=1)

    allowed = (kpos_ref[...] >= first_ref[...]) & (kpos_ref[...] <= last_ref[...])
    for i, keys in enumerate((even, odd)):
        at = i * (kdim - half)
        scores = lax.dot_general(
            q_ref[:, at : at + wide], keys[...], NT, preferred_element_type=jnp.float32
        )
        scores = jnp.where(allowed, scores * qk_scale, -1e30)
        expo = jnp.exp(scores - jnp.max(scores, axis=-1, keepdims=True))
        probs = (expo / jnp.sum(expo, axis=-1, keepdims=True)).astype(jnp.bfloat16)
        out_ref[:, i * LATENT : (i + 1) * LATENT] = jnp.dot(
            probs, even[:, :LATENT], preferred_element_type=jnp.float32
        ).astype(jnp.bfloat16)


def attend(queries, parts, first, last, kpos):
    n = len(parts)
    rows, kdim = queries.shape[0], queries.shape[1] // HEADS
    wide = -(-kdim // LANES) * LANES
    return call(
        functools.partial(attend_kernel, [at for _, at in parts], kdim),
        6,
        (HEADS // 2,),
        [whole(first), whole(last), whole(kpos)]
        + [pl.BlockSpec((rows, 2 * kdim), lambda h: (0, h))]
        + [whole(p) for p, _ in parts],
        pl.BlockSpec((rows, 2 * LATENT), lambda h: (0, h)),
        jax.ShapeDtypeStruct((rows, HEADS * LATENT), jnp.bfloat16),
        [pltpu.VMEM((n * rows, wide), jnp.bfloat16)] * 2,
        "attention",
    )(first, last, kpos, queries, *[p for p, _ in parts])


def added(*terms):
    total = terms[0].astype(jnp.float32)
    for term in terms[1:]:
        total = total + term.astype(jnp.float32)
    return total.astype(jnp.bfloat16)


def shards(queries, latent_kv, doc_lengths, hidden_in, router_weight, expert_ids, gate_up, w_down):
    tok_rows, width = hidden_in.shape[1:]
    n_ctx, n_exp = lax.axis_size("ctx"), lax.axis_size("exp")
    ctx, exp = lax.axis_index("ctx"), lax.axis_index("exp")
    local = gate_up.shape[0]
    near = n_exp == 4
    shifts = [0, 1, 3, 2] if near else [0]
    tokens = hidden_in[0]

    def flip(a, bit):
        return lax.ppermute(a, "ctx", [(i, i ^ bit) for i in range(n_ctx)])

    def shift(a, d):
        return lax.ppermute(a, "exp", [(i, i ^ d) for i in range(n_exp)])

    def along_exp(a):
        if near:
            beside, across = shift(a, 1), shift(a, 3)
            return [a, beside, across, shift(across, 1)]
        return [lax.all_gather(a, "exp", axis=0, tiled=True)]

    masks = [0, 2, 1, 3]
    order = jnp.stack([ctx ^ m for m in masks])

    top = expert_ids.shape[2]
    picks = expert_ids[0].T.astype(jnp.bfloat16).reshape(1, top * tok_rows)
    picks = jnp.pad(picks, ((0, EXTRA - 1), (0, width - top * tok_rows)))
    packed = jnp.concatenate([tokens, picks], axis=0)

    keys = latent_kv[0]
    keys = jnp.concatenate([keys, flip(keys, 2)], axis=0)
    near_parts = along_exp(packed)
    arrived = near_parts
    crossed = [flip(a, 2) for a in near_parts[:3]]
    if near:
        crossed.append(shift(crossed[2], 1))
    kv = [(a, k * tok_rows) for a in (keys, flip(keys, 1)) for k in range(2)]
    if near:
        blocks = 1
        gu, token = sort_rows(gate_up, [(), (arrived[1],), (crossed[2],)])
        pairs = [
            stack(a, b, (token,)) if i == 1 else jnp.concatenate([a, b], axis=0)
            for i, (a, b) in enumerate(zip(near_parts, crossed))
        ]
        flipped = [flip(a, 1) for a in pairs]
        spread = [[(a, 0), (a, 1), (b, 0), (b, 1)] for a, b in zip(pairs, flipped)]
    else:
        gu, _ = sort_rows(gate_up, [(), (), ()])
        blocks = near_parts[0].shape[0] // (BLOCK + EXTRA)
        spread = [[(near_parts[0], 0), (crossed[0], 0)]]
        spread[0] = spread[0] + [(flip(a, 1), 0) for a, _ in spread[0]]
    lengths = doc_lengths[0]
    ends = jnp.cumsum(lengths)
    row_pos = order[:, None] * tok_rows + jnp.arange(tok_rows, dtype=jnp.int32)[None, :]
    pos = row_pos[0]
    passed = pos[:, None] >= ends[None, :]
    first = jnp.max(jnp.where(passed, ends[None, :], 0), axis=1)
    context = attend(queries[0], kv, first[:, None], pos[:, None], row_pos.reshape(1, -1))

    seg = jnp.sum((row_pos[..., None] >= ends).astype(jnp.int32), axis=-1)
    sizes = lengths.astype(jnp.float32)
    scale = jnp.broadcast_to((EXPERTS / (top * sizes * sizes))[:, None], (NDOC, LANES))

    base = (exp * local).reshape(1).astype(jnp.int32)
    rw = jnp.roll(router_weight.T, -exp * local, axis=0)
    balance = None
    sent = []
    for i in range(len(shifts)):
        row = (seg.reshape(-1, 1, BLOCK), scale) if near and i == 0 else None
        out = dispatch(spread[i], blocks, top, base, rw, local, row)
        sent.append(out[:3])
        if row is not None:
            balance = out[3]
    made = experts([a[0] for a in sent], [a[1] for a in sent], gu, w_down)
    back = []
    for i in reversed(range(len(shifts))):
        keep, give = combine([sent[i][2]], [made[i]], n_ctx)
        got = flip(give, 1)
        far = added(keep[:, tok_rows:], got[:, tok_rows:])
        crossed_sum = flip(far, 2)
        terms = [keep[:, :tok_rows], got[:, :tok_rows], crossed_sum]
        if shifts[i] == 2:
            joining = shift(added(*terms), 1)
        elif shifts[i] == 3:
            across = added(*terms, joining)
            back.append(shift(across, 3))
        elif i:
            back.append(shift(join(keep, got, crossed_sum, (across,)), 1))
        else:
            back = back + terms
    if near:
        expert_mix = added(*back)
    else:
        expert_mix = lax.psum_scatter(
            added(*back).reshape(-1, width), "exp", scatter_dimension=0, tiled=True
        ).reshape(1, tok_rows, width)

    if balance is None:
        row = lax.all_gather(tokens, "ctx", axis=0, tiled=True)
        router = jax.nn.softmax(
            jnp.dot(row, router_weight, preferred_element_type=jnp.float32), axis=-1
        )
        row_ids = lax.all_gather(expert_ids[0], "ctx", axis=0, tiled=True)
        hot = (row_ids[:, :, None] == jnp.arange(EXPERTS, dtype=jnp.int32)).astype(jnp.float32)
        at = jnp.arange(row.shape[0], dtype=jnp.int32)
        seg_at = jnp.sum((at[:, None] >= ends[None, :]).astype(jnp.int32), axis=1)
        seg_hot = (seg_at[:, None] == jnp.arange(NDOC, dtype=jnp.int32)).astype(jnp.float32)
        exact = lax.Precision.HIGHEST
        counts = jnp.dot(seg_hot.T, hot.sum(axis=1), precision=exact)
        mass = jnp.dot(seg_hot.T, router, precision=exact)
        per_doc = jnp.sum(counts * mass, axis=1) * scale[:, 0]
    else:
        per_doc = balance[:, 0]
    return context[None], expert_mix, per_doc.reshape(1, NDOC)


def solution(mesh):
    rows = P(("group", "exp"), "ctx", None)
    docs = P(("group", "exp"), None)
    return jax.shard_map(
        shards,
        mesh=mesh,
        in_specs=(rows, rows, docs, rows, P(), rows, P("exp", "ctx", None, None), P("exp", "ctx", None)),
        out_specs=(rows, rows, docs),
        check_vma=False,
    )
```

```python
import functools

import jax
import jax.numpy as jnp
from jax import lax
from jax.experimental import pallas as pl
from jax.experimental.pallas import tpu as pltpu
from jax.sharding import PartitionSpec as P

EXPERTS = 64
HEADS = 8
LATENT = 512
CAP = 16
NDOC = 8
BLOCK = 128
LANES = 128
EXPERT_ROWS = 256
EXTRA = 16
VMEM = 14 * 2**20
VMEM_EXPERTS = 24 * 2**20
VMEM_SORT = 52 * 2**20
PIECES = (0.625, 0.875, 1.0)
DEPTH = 3
PEAK = 1.1e9

qk_scale = 192.0 ** (-0.5)
NT = (((1,), (1,)), ((), ()))
TN = (((0,), (0,)), ((), ()))


def call(kernel, micros, grid, in_specs, out_specs, out_shape, scratch, name, limit=VMEM, aliases={}):
    return pl.pallas_call(
        kernel,
        grid=grid,
        in_specs=in_specs,
        out_specs=out_specs,
        out_shape=out_shape,
        scratch_shapes=scratch,
        input_output_aliases=aliases,
        compiler_params=pltpu.CompilerParams(
            dimension_semantics=("arbitrary",) * len(grid) if grid else None, vmem_limit_bytes=limit
        ),
        cost_estimate=pl.CostEstimate(
            flops=int(micros * PEAK), bytes_accessed=0, transcendentals=0
        ),
        name=name,
    )


def dispatch_kernel(starts, n_row, top, base_ref, rw_ref, *refs):
    n_parts = len(starts)
    parts, refs = refs[:n_parts], refs[n_parts:]
    if n_row:
        seg_ref, scale_ref = refs[:2]
        refs = refs[2:]
    rows_ref, weight_ref, picks_ref = refs[:3]
    local = rows_ref.shape[0]
    width = rows_ref.shape[2]
    names = lax.broadcasted_iota(jnp.int32, (EXPERTS, BLOCK), 0).astype(jnp.float32)
    base = base_ref[0].astype(jnp.float32)
    before = (
        lax.broadcasted_iota(jnp.int32, (BLOCK, BLOCK), 0)
        < lax.broadcasted_iota(jnp.int32, (BLOCK, BLOCK), 1)
    ).astype(jnp.bfloat16)
    slot = lax.broadcasted_iota(jnp.int32, (local, CAP, BLOCK), 1).astype(jnp.float32)
    hots, probs = [], []
    for p in range(n_parts):
        s = starts[p]
        x = parts[p][s : s + BLOCK, :]
        ids = parts[p][s + BLOCK : s + BLOCK + EXTRA, :].astype(jnp.float32)[0:1] - base
        ids = jnp.where(ids < 0.0, ids + EXPERTS, ids)
        logits = lax.dot_general(rw_ref[...], x, NT, preferred_element_type=jnp.float32)
        expo = jnp.exp(logits - jnp.max(logits, axis=0, keepdims=True))
        prob = expo / jnp.sum(expo, axis=0, keepdims=True)
        hot = names == ids[:, :BLOCK]
        for k in range(1, top):
            hot = hot | (names == ids[:, k * BLOCK : (k + 1) * BLOCK])
        hot = hot.astype(jnp.float32)
        chosen = prob * hot
        gate = chosen[:local] / jnp.sum(chosen, axis=0, keepdims=True)
        own = hot[:local]
        rank = jnp.dot(own.astype(jnp.bfloat16), before, preferred_element_type=jnp.float32)
        key = jnp.where(own > 0.0, rank, -1.0)
        pick = (key[:, None, :] == slot).astype(jnp.float32)
        at = slice(p * CAP, (p + 1) * CAP)
        weight_ref[:, at, :] = jnp.broadcast_to(
            jnp.sum(pick * gate[:, None, :], axis=-1, keepdims=True), (local, CAP, LANES)
        )
        pick = pick.reshape(local * CAP, BLOCK).astype(jnp.bfloat16)
        picks_ref[p] = pick
        taken = jnp.dot(pick, x, preferred_element_type=jnp.float32)
        rows_ref[:, at, :] = taken.astype(jnp.bfloat16).reshape(local, CAP, width)
        hots.append(hot)
        probs.append(prob)
    if n_row:
        bal_ref = refs[3]
        for d in range(NDOC):
            counts = jnp.zeros((EXPERTS, BLOCK), jnp.float32)
            mass = jnp.zeros((EXPERTS, BLOCK), jnp.float32)
            for p in range(n_row):
                inside = seg_ref[p] == d
                counts = counts + jnp.where(inside, hots[p], 0.0)
                mass = mass + jnp.where(inside, probs[p], 0.0)
            both = jnp.sum(counts, axis=1, keepdims=True) * jnp.sum(mass, axis=1, keepdims=True)
            bal_ref[d : d + 1, :] = (
                jnp.broadcast_to(jnp.sum(both, axis=0, keepdims=True), (1, LANES))
                * scale_ref[d : d + 1, :]
            )


IN_HBM = pl.BlockSpec(memory_space=pltpu.HBM)
ANYWHERE = pl.BlockSpec(memory_space=pl.ANY)


IN_VMEM = pl.BlockSpec(memory_space=pltpu.VMEM)


def whole(a):
    return pl.BlockSpec(a.shape, lambda *i: (0,) * a.ndim)


def dispatch(parts, n, top, base, rw, local, row=None):
    n_parts = len(parts)
    width = rw.shape[1]
    slots = n_parts * CAP
    in_specs = [
        pl.BlockSpec(memory_space=pltpu.SMEM),
        whole(rw),
    ] + [
        pl.BlockSpec((BLOCK + EXTRA, width), lambda i, k=k: (k + i, 0)) for _, k in parts
    ]
    out_specs = [
        pl.BlockSpec((local, slots, width), lambda i: (0, i, 0)),
        pl.BlockSpec((local, slots, LANES), lambda i: (0, i, 0)),
        pl.BlockSpec((n_parts, local * CAP, BLOCK), lambda i: (i, 0, 0)),
    ]
    out_shape = [
        jax.ShapeDtypeStruct((local, n * slots, width), jnp.bfloat16),
        jax.ShapeDtypeStruct((local, n * slots, LANES), jnp.float32),
        jax.ShapeDtypeStruct((n * n_parts, local * CAP, BLOCK), jnp.bfloat16),
    ]
    extra = ()
    if row is not None:
        extra = row
        in_specs += [whole(a) for a in row]
        out_specs.append(pl.BlockSpec((NDOC, LANES), lambda i: (0, 0)))
        out_shape.append(jax.ShapeDtypeStruct((NDOC, LANES), jnp.float32))
    grid, starts = (n,), [0] * n_parts
    if n == 1:
        grid, starts = (), [k * (BLOCK + EXTRA) for _, k in parts]
        in_specs = in_specs[:1] + [IN_VMEM] * (len(in_specs) - 1)
        out_specs = [IN_VMEM] * len(out_specs)
    return call(
        functools.partial(dispatch_kernel, starts, n_parts if row is not None else 0, top),
        3 * n,
        grid,
        in_specs,
        out_specs,
        out_shape,
        [],
        "dispatch",
    )(base, rw, *[a for a, _ in parts], *extra)


def fetch(sources, slots, sem, step, steps, first, start=0):
    depth, group = slots[0].shape[:2]

    def copies(at, e):
        slot = lax.rem(at, depth)
        return [
            pltpu.make_async_copy(
                source.at[start + at * group + e], held.at[slot, e], sem.at[i, slot, e]
            )
            for i, (source, held) in enumerate(zip(sources, slots))
        ]

    def begin(at):
        for e in range(group):
            for copy in copies(at, e):
                copy.start()

    @pl.when(first & (step == 0))
    def _():
        for ahead in range(depth - 1):

            @pl.when(ahead < steps)
            def _():
                begin(step + ahead)

    @pl.when(first & (step + depth - 1 < steps))
    def _():
        begin(step + depth - 1)

    def ready(e):
        if first is True:
            for copy in copies(step, e):
                copy.wait()
            return

        @pl.when(first)
        def _():
            for copy in copies(step, e):
                copy.wait()

    return lax.rem(step, depth), ready


def sort_kernel(start, gu_ref, *refs):
    out_ref, token_ref, held, made, wide, in_sem, out_sem = refs[-7:]
    token_ref[...] = jnp.zeros_like(token_ref)
    step, steps = pl.program_id(0), pl.num_programs(0)
    _, group, _, hidden, width = made.shape
    chunks = width // LANES
    slot, ready = fetch([gu_ref], [held], in_sem, step, steps, True, start)
    to = lax.rem(step, 2)

    def leave(at, e):
        to = lax.rem(at, 2)
        return pltpu.make_async_copy(
            made.at[to, e], out_ref.at[start + at * group + e], out_sem.at[to, e]
        )

    @pl.when(step >= 2)
    def _():
        for e in range(group):
            leave(step - 2, e).wait()

    for e in range(group):
        ready(e)
        wide[e] = held[slot, e].astype(jnp.float32)
        for z in range(2):
            for c in range(chunks):
                part = wide[e, pl.ds(2 * c + z, hidden, stride=2 * chunks), :]
                made[to, e, z, :, c * LANES : (c + 1) * LANES] = part.astype(jnp.bfloat16)
        leave(step, e).start()

    @pl.when(step == steps - 1)
    def _():
        @pl.when(step >= 1)
        def _():
            for e in range(group):
                leave(step - 1, e).wait()

        for e in range(group):
            leave(step, e).wait()


def sort_rows(gate_up, behind):
    local, hidden, _, width = gate_up.shape
    ends = [int(local * p) for p in PIECES] if local % 8 == 0 else [local]
    group = 2 if local % 2 == 0 else 1
    chunks = width // LANES
    gu = gate_up.reshape(local, hidden, 2, chunks, LANES).swapaxes(2, 3)
    gu = gu.reshape(local, hidden * 2 * chunks, LANES)
    done = ()
    for j, end in enumerate(ends):
        start = ends[j - 1] if j else 0
        after = behind[j] if len(ends) > 1 else ()
        *done, token = (
            call(
                functools.partial(sort_kernel, start),
                8,
                ((end - start) // group,),
                [IN_HBM] + [IN_HBM] * len(done) + [ANYWHERE] * len(after),
                [IN_HBM, pl.BlockSpec((8, LANES), lambda e: (0, 0))],
                [
                    jax.ShapeDtypeStruct((local, 2, hidden, width), jnp.bfloat16),
                    jax.ShapeDtypeStruct((8, LANES), jnp.float32),
                ],
                [
                    pltpu.VMEM((DEPTH, group) + gu.shape[1:], jnp.bfloat16),
                    pltpu.VMEM((2, group, 2, hidden, width), jnp.bfloat16),
                    pltpu.VMEM((group,) + gu.shape[1:], jnp.float32),
                    pltpu.SemaphoreType.DMA((1, DEPTH, group)),
                    pltpu.SemaphoreType.DMA((2, group)),
                ],
                "sort",
                VMEM_SORT,
                {1: 0} if done else {},
            )(gu, *done, *after)
        )
    return done[0], token


def stack_kernel(a_ref, b_ref, *refs):
    rows = a_ref.shape[0]
    refs[-1][:rows, :] = a_ref[...]
    refs[-1][rows:, :] = b_ref[...]


def stack(a, b, before):
    rows, width = a.shape
    return call(
        stack_kernel,
        1,
        (1,),
        [whole(a), whole(b)] + [ANYWHERE] * len(before),
        pl.BlockSpec((2 * rows, width), lambda i: (0, 0)),
        jax.ShapeDtypeStruct((2 * rows, width), a.dtype),
        [],
        "stack",
    )(a, b, *before)


def expert_kernel(n, *refs):
    rows, weights = refs[:n], refs[n : 2 * n]
    gu_ref, down_ref = refs[2 * n : 2 * n + 2]
    outs, (gu, down, sem) = refs[-3 - n : -3], refs[-3:]
    group = gu.shape[1]
    size = rows[0].shape[1]
    slot, ready = fetch(
        [gu_ref, down_ref],
        [gu, down],
        sem,
        pl.program_id(0),
        pl.num_programs(0),
        pl.program_id(1) == 0,
    )
    for e in range(group):
        ready(e)
    for e in range(group):
        held = jnp.concatenate([r[e] for r in rows], axis=0)
        g = lax.dot_general(held, gu[slot, e, 0], NT, preferred_element_type=jnp.float32)
        u = lax.dot_general(held, gu[slot, e, 1], NT, preferred_element_type=jnp.float32)
        inner = (g * lax.logistic(g) * u).astype(jnp.bfloat16)
        made = jnp.dot(inner, down[slot, e], preferred_element_type=jnp.float32)
        for i in range(n):
            w = weights[i][e]
            part = made[i * size : (i + 1) * size]
            for c in range(part.shape[1] // LANES):
                at = slice(c * LANES, (c + 1) * LANES)
                outs[i][e, :, at] = (part[:, at] * w).astype(jnp.bfloat16)


def experts(rows, weights, gu, down, after=()):
    n = len(rows)
    local, slots, width = rows[0].shape
    size = min(slots, EXPERT_ROWS)
    hidden = down.shape[1]
    group = 4 if local % 4 == 0 else 1
    rows_spec = pl.BlockSpec((group, size, width), lambda e, i: (e, i, 0))
    weight_spec = pl.BlockSpec((group, size, LANES), lambda e, i: (e, i, 0))
    return call(
        functools.partial(expert_kernel, n),
        6,
        (local // group, slots // size),
        [rows_spec] * n + [weight_spec] * n + [IN_HBM, IN_HBM] + [ANYWHERE] * len(after),
        [rows_spec] * n,
        [jax.ShapeDtypeStruct(r.shape, jnp.bfloat16) for r in rows],
        [
            pltpu.VMEM((2, group, 2, hidden, width), jnp.bfloat16),
            pltpu.VMEM((2, group, hidden, width), jnp.bfloat16),
            pltpu.SemaphoreType.DMA((2, 2, group)),
        ],
        "experts",
        VMEM_EXPERTS,
    )(*rows, *weights, gu, down, *after)


def combine_kernel(n, *refs):
    picks, made, outs = refs[:n], refs[n : 2 * n], refs[-2:]
    local, _, width = made[0].shape
    parts = picks[0].shape[0]
    half = parts // 2
    for i in range(n):
        for p in range(parts):
            held = made[i][:, p * CAP : (p + 1) * CAP, :].reshape(local * CAP, width)
            mix = lax.dot_general(picks[i][p], held, TN, preferred_element_type=jnp.float32)
            at = ((p % half) * n + i) * BLOCK
            outs[p // half][0, at : at + BLOCK, :] = mix.astype(jnp.bfloat16)


def combine(picks, made, n_parts, after=()):
    n = len(picks)
    steps = picks[0].shape[0] // n_parts
    local, _, width = made[0].shape
    half = n_parts // 2 * n * BLOCK
    out = pl.BlockSpec((1, half, width), lambda i: (i, 0, 0))
    return call(
        functools.partial(combine_kernel, n),
        2 * steps,
        (steps,),
        [pl.BlockSpec((n_parts,) + picks[0].shape[1:], lambda i: (i, 0, 0))] * n
        + [pl.BlockSpec((local, n_parts * CAP, width), lambda i: (0, i, 0))] * n
        + [ANYWHERE] * len(after),
        [out, out],
        [jax.ShapeDtypeStruct((steps, half, width), jnp.bfloat16)] * 2,
        [],
        "combine",
    )(*picks, *made, *after)


def join_kernel(a_ref, b_ref, c_ref, *refs):
    rows = c_ref.shape[1]
    total = a_ref[:, :rows, :].astype(jnp.float32) + b_ref[:, :rows, :].astype(jnp.float32)
    refs[-1][...] = (total + c_ref[...].astype(jnp.float32)).astype(jnp.bfloat16)


def join(a, b, c, before):
    return call(
        join_kernel,
        1,
        (),
        [IN_VMEM] * 3 + [ANYWHERE] * len(before),
        IN_VMEM,
        jax.ShapeDtypeStruct(c.shape, c.dtype),
        [],
        "join",
    )(a, b, c, *before)


def attend_kernel(starts, kdim, first_ref, last_ref, kpos_ref, q_ref, *refs):
    n = len(starts)
    parts, (out_ref, even, odd) = refs[:n], refs[n:]
    rows = q_ref.shape[0]
    start = max(parts[0].shape[1] - even.shape[1], 0)
    wide = even.shape[1]
    half = wide - kdim

    @pl.when(pl.program_id(0) == 0)
    def _():
        pad = jnp.zeros((rows, half), jnp.bfloat16)
        for i in range(n):
            at = slice(i * rows, (i + 1) * rows)
            keys = parts[i][starts[i] : starts[i] + rows, start : start + kdim]
            even[at, :] = jnp.concatenate([keys, pad], axis=1)
            odd[at, :] = jnp.concatenate([pad, keys], axis=1)

    allowed = (kpos_ref[...] >= first_ref[...]) & (kpos_ref[...] <= last_ref[...])
    for i, keys in enumerate((even, odd)):
        at = i * (kdim - half)
        scores = lax.dot_general(
            q_ref[:, at : at + wide], keys[...], NT, preferred_element_type=jnp.float32
        )
        scores = jnp.where(allowed, scores * qk_scale, -1e30)
        expo = jnp.exp(scores - jnp.max(scores, axis=-1, keepdims=True))
        probs = (expo / jnp.sum(expo, axis=-1, keepdims=True)).astype(jnp.bfloat16)
        out_ref[:, i * LATENT : (i + 1) * LATENT] = jnp.dot(
            probs, even[:, :LATENT], preferred_element_type=jnp.float32
        ).astype(jnp.bfloat16)


def attend(queries, parts, first, last, kpos):
    n = len(parts)
    rows, kdim = queries.shape[0], queries.shape[1] // HEADS
    wide = -(-kdim // LANES) * LANES
    return call(
        functools.partial(attend_kernel, [at for _, at in parts], kdim),
        6,
        (HEADS // 2,),
        [whole(first), whole(last), whole(kpos)]
        + [pl.BlockSpec((rows, 2 * kdim), lambda h: (0, h))]
        + [whole(p) for p, _ in parts],
        pl.BlockSpec((rows, 2 * LATENT), lambda h: (0, h)),
        jax.ShapeDtypeStruct((rows, HEADS * LATENT), jnp.bfloat16),
        [pltpu.VMEM((n * rows, wide), jnp.bfloat16)] * 2,
        "attention",
    )(first, last, kpos, queries, *[p for p, _ in parts])


def added(*terms):
    total = terms[0].astype(jnp.float32)
    for term in terms[1:]:
        total = total + term.astype(jnp.float32)
    return total.astype(jnp.bfloat16)


def shards(queries, latent_kv, doc_lengths, hidden_in, router_weight, expert_ids, gate_up, w_down):
    tok_rows, width = hidden_in.shape[1:]
    n_ctx, n_exp = lax.axis_size("ctx"), lax.axis_size("exp")
    ctx, exp = lax.axis_index("ctx"), lax.axis_index("exp")
    local = gate_up.shape[0]
    near = n_exp == 4
    shifts = [0, 1, 3, 2] if near else [0]
    tokens = hidden_in[0]

    def flip(a, bit):
        return lax.ppermute(a, "ctx", [(i, i ^ bit) for i in range(n_ctx)])

    def shift(a, d):
        return lax.ppermute(a, "exp", [(i, i ^ d) for i in range(n_exp)])

    def along_exp(a):
        if near:
            beside, across = shift(a, 1), shift(a, 3)
            return [a, beside, across, shift(across, 1)]
        return [lax.all_gather(a, "exp", axis=0, tiled=True)]

    masks = [0, 2, 1, 3]
    order = jnp.stack([ctx ^ m for m in masks])

    top = expert_ids.shape[2]
    picks = expert_ids[0].T.astype(jnp.bfloat16).reshape(1, top * tok_rows)
    picks = jnp.pad(picks, ((0, EXTRA - 1), (0, width - top * tok_rows)))
    packed = jnp.concatenate([tokens, picks], axis=0)

    keys = latent_kv[0]
    keys = jnp.concatenate([keys, flip(keys, 2)], axis=0)
    near_parts = along_exp(packed)
    arrived = near_parts
    crossed = [flip(a, 2) for a in near_parts[:3]]
    if near:
        crossed.append(shift(crossed[2], 1))
    kv = [(a, k * tok_rows) for a in (keys, flip(keys, 1)) for k in range(2)]
    if near:
        blocks = 1
        gu, token = sort_rows(gate_up, [(), (arrived[1],), (crossed[2],)])
        pairs = [
            stack(a, b, (token,)) if i == 1 else jnp.concatenate([a, b], axis=0)
            for i, (a, b) in enumerate(zip(near_parts, crossed))
        ]
        flipped = [flip(a, 1) for a in pairs]
        spread = [[(a, 0), (a, 1), (b, 0), (b, 1)] for a, b in zip(pairs, flipped)]
    else:
        gu, _ = sort_rows(gate_up, [(), (), ()])
        blocks = near_parts[0].shape[0] // (BLOCK + EXTRA)
        spread = [[(near_parts[0], 0), (crossed[0], 0)]]
        spread[0] = spread[0] + [(flip(a, 1), 0) for a, _ in spread[0]]
    lengths = doc_lengths[0]
    ends = jnp.cumsum(lengths)
    row_pos = order[:, None] * tok_rows + jnp.arange(tok_rows, dtype=jnp.int32)[None, :]
    pos = row_pos[0]
    passed = pos[:, None] >= ends[None, :]
    first = jnp.max(jnp.where(passed, ends[None, :], 0), axis=1)
    context = attend(queries[0], kv, first[:, None], pos[:, None], row_pos.reshape(1, -1))

    seg = jnp.sum((row_pos[..., None] >= ends).astype(jnp.int32), axis=-1)
    sizes = lengths.astype(jnp.float32)
    scale = jnp.broadcast_to((EXPERTS / (top * sizes * sizes))[:, None], (NDOC, LANES))

    base = (exp * local).reshape(1).astype(jnp.int32)
    rw = jnp.roll(router_weight.T, -exp * local, axis=0)
    balance = None
    sent = []
    for i in range(len(shifts)):
        row = (seg.reshape(-1, 1, BLOCK), scale) if near and i == 0 else None
        out = dispatch(spread[i], blocks, top, base, rw, local, row)
        sent.append(out[:3])
        if row is not None:
            balance = out[3]
    made = experts([a[0] for a in sent], [a[1] for a in sent], gu, w_down)
    back = []
    for i in reversed(range(len(shifts))):
        keep, give = combine([sent[i][2]], [made[i]], n_ctx)
        got = flip(give, 1)
        far = added(keep[:, tok_rows:], got[:, tok_rows:])
        crossed_sum = flip(far, 2)
        terms = [keep[:, :tok_rows], got[:, :tok_rows], crossed_sum]
        if shifts[i] == 2:
            joining = shift(added(*terms), 1)
        elif shifts[i] == 3:
            across = added(*terms, joining)
            back.append(shift(across, 3))
        elif i:
            back.append(shift(join(keep, got, crossed_sum, (across,)), 1))
        else:
            back = back + terms
    if near:
        expert_mix = added(*back)
    else:
        expert_mix = lax.psum_scatter(
            added(*back).reshape(-1, width), "exp", scatter_dimension=0, tiled=True
        ).reshape(1, tok_rows, width)

    if balance is None:
        row = lax.all_gather(tokens, "ctx", axis=0, tiled=True)
        router = jax.nn.softmax(
            jnp.dot(row, router_weight, preferred_element_type=jnp.float32), axis=-1
        )
        row_ids = lax.all_gather(expert_ids[0], "ctx", axis=0, tiled=True)
        hot = (row_ids[:, :, None] == jnp.arange(EXPERTS, dtype=jnp.int32)).astype(jnp.float32)
        at = jnp.arange(row.shape[0], dtype=jnp.int32)
        seg_at = jnp.sum((at[:, None] >= ends[None, :]).astype(jnp.int32), axis=1)
        seg_hot = (seg_at[:, None] == jnp.arange(NDOC, dtype=jnp.int32)).astype(jnp.float32)
        exact = lax.Precision.HIGHEST
        counts = jnp.dot(seg_hot.T, hot.sum(axis=1), precision=exact)
        mass = jnp.dot(seg_hot.T, router, precision=exact)
        per_doc = jnp.sum(counts * mass, axis=1) * scale[:, 0]
    else:
        per_doc = balance[:, 0]
    return context[None], expert_mix, per_doc.reshape(1, NDOC)


def solution(mesh):
    rows = P(("group", "exp"), "ctx", None)
    docs = P(("group", "exp"), None)
    return jax.shard_map(
        shards,
        mesh=mesh,
        in_specs=(rows, rows, docs, rows, P(), rows, P("exp", "ctx", None, None), P("exp", "ctx", None)),
        out_specs=(rows, rows, docs),
        check_vma=False,
    )
```

```python
import functools

import jax
import jax.numpy as jnp
from jax import lax
from jax.experimental import pallas as pl
from jax.experimental.pallas import tpu as pltpu
from jax.sharding import PartitionSpec as P

EXPERTS = 64
HEADS = 8
LATENT = 512
CAP = 16
NDOC = 8
BLOCK = 128
LANES = 128
EXPERT_ROWS = 256
EXTRA = 16
VMEM = 14 * 2**20
VMEM_EXPERTS = 24 * 2**20
VMEM_SORT = 52 * 2**20
PIECES = (0.5, 0.75, 1.0)
DEPTH = 4
PEAK = 1.1e9

qk_scale = 192.0 ** (-0.5)
NT = (((1,), (1,)), ((), ()))
TN = (((0,), (0,)), ((), ()))


def call(kernel, micros, grid, in_specs, out_specs, out_shape, scratch, name, limit=VMEM, aliases={}):
    return pl.pallas_call(
        kernel,
        grid=grid,
        in_specs=in_specs,
        out_specs=out_specs,
        out_shape=out_shape,
        scratch_shapes=scratch,
        input_output_aliases=aliases,
        compiler_params=pltpu.CompilerParams(
            dimension_semantics=("arbitrary",) * len(grid) if grid else None, vmem_limit_bytes=limit
        ),
        cost_estimate=pl.CostEstimate(
            flops=int(micros * PEAK), bytes_accessed=0, transcendentals=0
        ),
        name=name,
    )


def dispatch_kernel(starts, n_row, top, base_ref, rw_ref, *refs):
    n_parts = len(starts)
    parts, refs = refs[:n_parts], refs[n_parts:]
    if n_row:
        seg_ref, scale_ref = refs[:2]
        refs = refs[2:]
    rows_ref, weight_ref, picks_ref = refs[:3]
    local = rows_ref.shape[0]
    width = rows_ref.shape[2]
    names = lax.broadcasted_iota(jnp.int32, (EXPERTS, BLOCK), 0).astype(jnp.float32)
    base = base_ref[0].astype(jnp.float32)
    before = (
        lax.broadcasted_iota(jnp.int32, (BLOCK, BLOCK), 0)
        < lax.broadcasted_iota(jnp.int32, (BLOCK, BLOCK), 1)
    ).astype(jnp.bfloat16)
    slot = lax.broadcasted_iota(jnp.int32, (local, CAP, BLOCK), 1).astype(jnp.float32)
    hots, probs = [], []
    for p in range(n_parts):
        s = starts[p]
        x = parts[p][s : s + BLOCK, :]
        ids = parts[p][s + BLOCK : s + BLOCK + EXTRA, :].astype(jnp.float32)[0:1] - base
        ids = jnp.where(ids < 0.0, ids + EXPERTS, ids)
        logits = lax.dot_general(rw_ref[...], x, NT, preferred_element_type=jnp.float32)
        expo = jnp.exp(logits - jnp.max(logits, axis=0, keepdims=True))
        prob = expo / jnp.sum(expo, axis=0, keepdims=True)
        hot = names == ids[:, :BLOCK]
        for k in range(1, top):
            hot = hot | (names == ids[:, k * BLOCK : (k + 1) * BLOCK])
        hot = hot.astype(jnp.float32)
        chosen = prob * hot
        gate = chosen[:local] / jnp.sum(chosen, axis=0, keepdims=True)
        own = hot[:local]
        rank = jnp.dot(own.astype(jnp.bfloat16), before, preferred_element_type=jnp.float32)
        key = jnp.where(own > 0.0, rank, -1.0)
        pick = (key[:, None, :] == slot).astype(jnp.float32)
        at = slice(p * CAP, (p + 1) * CAP)
        weight_ref[:, at, :] = jnp.broadcast_to(
            jnp.sum(pick * gate[:, None, :], axis=-1, keepdims=True), (local, CAP, LANES)
        )
        pick = pick.reshape(local * CAP, BLOCK).astype(jnp.bfloat16)
        picks_ref[p] = pick
        taken = jnp.dot(pick, x, preferred_element_type=jnp.float32)
        rows_ref[:, at, :] = taken.astype(jnp.bfloat16).reshape(local, CAP, width)
        hots.append(hot)
        probs.append(prob)
    if n_row:
        bal_ref = refs[3]
        for d in range(NDOC):
            counts = jnp.zeros((EXPERTS, BLOCK), jnp.float32)
            mass = jnp.zeros((EXPERTS, BLOCK), jnp.float32)
            for p in range(n_row):
                inside = seg_ref[p] == d
                counts = counts + jnp.where(inside, hots[p], 0.0)
                mass = mass + jnp.where(inside, probs[p], 0.0)
            both = jnp.sum(counts, axis=1, keepdims=True) * jnp.sum(mass, axis=1, keepdims=True)
            bal_ref[d : d + 1, :] = (
                jnp.broadcast_to(jnp.sum(both, axis=0, keepdims=True), (1, LANES))
                * scale_ref[d : d + 1, :]
            )


IN_HBM = pl.BlockSpec(memory_space=pltpu.HBM)
ANYWHERE = pl.BlockSpec(memory_space=pl.ANY)


IN_VMEM = pl.BlockSpec(memory_space=pltpu.VMEM)


def whole(a):
    return pl.BlockSpec(a.shape, lambda *i: (0,) * a.ndim)


def dispatch(parts, n, top, base, rw, local, row=None):
    n_parts = len(parts)
    width = rw.shape[1]
    slots = n_parts * CAP
    in_specs = [
        pl.BlockSpec(memory_space=pltpu.SMEM),
        whole(rw),
    ] + [
        pl.BlockSpec((BLOCK + EXTRA, width), lambda i, k=k: (k + i, 0)) for _, k in parts
    ]
    out_specs = [
        pl.BlockSpec((local, slots, width), lambda i: (0, i, 0)),
        pl.BlockSpec((local, slots, LANES), lambda i: (0, i, 0)),
        pl.BlockSpec((n_parts, local * CAP, BLOCK), lambda i: (i, 0, 0)),
    ]
    out_shape = [
        jax.ShapeDtypeStruct((local, n * slots, width), jnp.bfloat16),
        jax.ShapeDtypeStruct((local, n * slots, LANES), jnp.float32),
        jax.ShapeDtypeStruct((n * n_parts, local * CAP, BLOCK), jnp.bfloat16),
    ]
    extra = ()
    if row is not None:
        extra = row
        in_specs += [whole(a) for a in row]
        out_specs.append(pl.BlockSpec((NDOC, LANES), lambda i: (0, 0)))
        out_shape.append(jax.ShapeDtypeStruct((NDOC, LANES), jnp.float32))
    grid, starts = (n,), [0] * n_parts
    if n == 1:
        grid, starts = (), [k * (BLOCK + EXTRA) for _, k in parts]
        in_specs = in_specs[:1] + [IN_VMEM] * (len(in_specs) - 1)
        out_specs = [IN_VMEM] * len(out_specs)
    return call(
        functools.partial(dispatch_kernel, starts, n_parts if row is not None else 0, top),
        3 * n,
        grid,
        in_specs,
        out_specs,
        out_shape,
        [],
        "dispatch",
    )(base, rw, *[a for a, _ in parts], *extra)


def fetch(sources, slots, sem, step, steps, first, start=0):
    depth, group = slots[0].shape[:2]

    def copies(at, e):
        slot = lax.rem(at, depth)
        return [
            pltpu.make_async_copy(
                source.at[start + at * group + e], held.at[slot, e], sem.at[i, slot, e]
            )
            for i, (source, held) in enumerate(zip(sources, slots))
        ]

    def begin(at):
        for e in range(group):
            for copy in copies(at, e):
                copy.start()

    @pl.when(first & (step == 0))
    def _():
        for ahead in range(depth - 1):

            @pl.when(ahead < steps)
            def _():
                begin(step + ahead)

    @pl.when(first & (step + depth - 1 < steps))
    def _():
        begin(step + depth - 1)

    def ready(e):
        if first is True:
            for copy in copies(step, e):
                copy.wait()
            return

        @pl.when(first)
        def _():
            for copy in copies(step, e):
                copy.wait()

    return lax.rem(step, depth), ready


def sort_kernel(start, gu_ref, *refs):
    out_ref, token_ref, held, made, wide, in_sem, out_sem = refs[-7:]
    token_ref[...] = jnp.zeros_like(token_ref)
    step, steps = pl.program_id(0), pl.num_programs(0)
    _, group, _, hidden, width = made.shape
    chunks = width // LANES
    slot, ready = fetch([gu_ref], [held], in_sem, step, steps, True, start)
    to = lax.rem(step, 2)

    def leave(at, e):
        to = lax.rem(at, 2)
        return pltpu.make_async_copy(
            made.at[to, e], out_ref.at[start + at * group + e], out_sem.at[to, e]
        )

    @pl.when(step >= 2)
    def _():
        for e in range(group):
            leave(step - 2, e).wait()

    for e in range(group):
        ready(e)
        wide[e] = held[slot, e].astype(jnp.float32)
        for z in range(2):
            for c in range(chunks):
                part = wide[e, pl.ds(2 * c + z, hidden, stride=2 * chunks), :]
                made[to, e, z, :, c * LANES : (c + 1) * LANES] = part.astype(jnp.bfloat16)
        leave(step, e).start()

    @pl.when(step == steps - 1)
    def _():
        @pl.when(step >= 1)
        def _():
            for e in range(group):
                leave(step - 1, e).wait()

        for e in range(group):
            leave(step, e).wait()


def sort_rows(gate_up, behind):
    local, hidden, _, width = gate_up.shape
    ends = [int(local * p) for p in PIECES] if local % 8 == 0 else [local]
    group = 2 if local % 2 == 0 else 1
    chunks = width // LANES
    gu = gate_up.reshape(local, hidden, 2, chunks, LANES).swapaxes(2, 3)
    gu = gu.reshape(local, hidden * 2 * chunks, LANES)
    done = ()
    for j, end in enumerate(ends):
        start = ends[j - 1] if j else 0
        after = behind[j] if len(ends) > 1 else ()
        *done, token = (
            call(
                functools.partial(sort_kernel, start),
                8,
                ((end - start) // group,),
                [IN_HBM] + [IN_HBM] * len(done) + [ANYWHERE] * len(after),
                [IN_HBM, pl.BlockSpec((8, LANES), lambda e: (0, 0))],
                [
                    jax.ShapeDtypeStruct((local, 2, hidden, width), jnp.bfloat16),
                    jax.ShapeDtypeStruct((8, LANES), jnp.float32),
                ],
                [
                    pltpu.VMEM((DEPTH, group) + gu.shape[1:], jnp.bfloat16),
                    pltpu.VMEM((2, group, 2, hidden, width), jnp.bfloat16),
                    pltpu.VMEM((group,) + gu.shape[1:], jnp.float32),
                    pltpu.SemaphoreType.DMA((1, DEPTH, group)),
                    pltpu.SemaphoreType.DMA((2, group)),
                ],
                "sort",
                VMEM_SORT,
                {1: 0} if done else {},
            )(gu, *done, *after)
        )
    return done[0], token


def stack_kernel(a_ref, b_ref, *refs):
    rows = a_ref.shape[0]
    refs[-1][:rows, :] = a_ref[...]
    refs[-1][rows:, :] = b_ref[...]


def stack(a, b, before):
    rows, width = a.shape
    return call(
        stack_kernel,
        1,
        (1,),
        [whole(a), whole(b)] + [ANYWHERE] * len(before),
        pl.BlockSpec((2 * rows, width), lambda i: (0, 0)),
        jax.ShapeDtypeStruct((2 * rows, width), a.dtype),
        [],
        "stack",
    )(a, b, *before)


def expert_kernel(n, *refs):
    rows, weights = refs[:n], refs[n : 2 * n]
    gu_ref, down_ref = refs[2 * n : 2 * n + 2]
    outs, (gu, down, sem) = refs[-3 - n : -3], refs[-3:]
    group = gu.shape[1]
    size = rows[0].shape[1]
    slot, ready = fetch(
        [gu_ref, down_ref],
        [gu, down],
        sem,
        pl.program_id(0),
        pl.num_programs(0),
        pl.program_id(1) == 0,
    )
    for e in range(group):
        ready(e)
    for e in range(group):
        held = jnp.concatenate([r[e] for r in rows], axis=0)
        g = lax.dot_general(held, gu[slot, e, 0], NT, preferred_element_type=jnp.float32)
        u = lax.dot_general(held, gu[slot, e, 1], NT, preferred_element_type=jnp.float32)
        inner = (g * lax.logistic(g) * u).astype(jnp.bfloat16)
        made = jnp.dot(inner, down[slot, e], preferred_element_type=jnp.float32)
        for i in range(n):
            w = weights[i][e]
            part = made[i * size : (i + 1) * size]
            for c in range(part.shape[1] // LANES):
                at = slice(c * LANES, (c + 1) * LANES)
                outs[i][e, :, at] = (part[:, at] * w).astype(jnp.bfloat16)


def experts(rows, weights, gu, down, after=()):
    n = len(rows)
    local, slots, width = rows[0].shape
    size = min(slots, EXPERT_ROWS)
    hidden = down.shape[1]
    group = 4 if local % 4 == 0 else 1
    rows_spec = pl.BlockSpec((group, size, width), lambda e, i: (e, i, 0))
    weight_spec = pl.BlockSpec((group, size, LANES), lambda e, i: (e, i, 0))
    return call(
        functools.partial(expert_kernel, n),
        6,
        (local // group, slots // size),
        [rows_spec] * n + [weight_spec] * n + [IN_HBM, IN_HBM] + [ANYWHERE] * len(after),
        [rows_spec] * n,
        [jax.ShapeDtypeStruct(r.shape, jnp.bfloat16) for r in rows],
        [
            pltpu.VMEM((2, group, 2, hidden, width), jnp.bfloat16),
            pltpu.VMEM((2, group, hidden, width), jnp.bfloat16),
            pltpu.SemaphoreType.DMA((2, 2, group)),
        ],
        "experts",
        VMEM_EXPERTS,
    )(*rows, *weights, gu, down, *after)


def combine_kernel(n, *refs):
    picks, made, outs = refs[:n], refs[n : 2 * n], refs[-2:]
    local, _, width = made[0].shape
    parts = picks[0].shape[0]
    half = parts // 2
    for i in range(n):
        for p in range(parts):
            held = made[i][:, p * CAP : (p + 1) * CAP, :].reshape(local * CAP, width)
            mix = lax.dot_general(picks[i][p], held, TN, preferred_element_type=jnp.float32)
            at = ((p % half) * n + i) * BLOCK
            outs[p // half][0, at : at + BLOCK, :] = mix.astype(jnp.bfloat16)


def combine(picks, made, n_parts, after=()):
    n = len(picks)
    steps = picks[0].shape[0] // n_parts
    local, _, width = made[0].shape
    half = n_parts // 2 * n * BLOCK
    out = pl.BlockSpec((1, half, width), lambda i: (i, 0, 0))
    return call(
        functools.partial(combine_kernel, n),
        2 * steps,
        (steps,),
        [pl.BlockSpec((n_parts,) + picks[0].shape[1:], lambda i: (i, 0, 0))] * n
        + [pl.BlockSpec((local, n_parts * CAP, width), lambda i: (0, i, 0))] * n
        + [ANYWHERE] * len(after),
        [out, out],
        [jax.ShapeDtypeStruct((steps, half, width), jnp.bfloat16)] * 2,
        [],
        "combine",
    )(*picks, *made, *after)


def join_kernel(a_ref, b_ref, c_ref, *refs):
    rows = c_ref.shape[1]
    total = a_ref[:, :rows, :].astype(jnp.float32) + b_ref[:, :rows, :].astype(jnp.float32)
    refs[-1][...] = (total + c_ref[...].astype(jnp.float32)).astype(jnp.bfloat16)


def join(a, b, c, before):
    return call(
        join_kernel,
        1,
        (),
        [IN_VMEM] * 3 + [ANYWHERE] * len(before),
        IN_VMEM,
        jax.ShapeDtypeStruct(c.shape, c.dtype),
        [],
        "join",
    )(a, b, c, *before)


def attend_kernel(starts, kdim, first_ref, last_ref, kpos_ref, q_ref, *refs):
    n = len(starts)
    parts, (out_ref, even, odd) = refs[:n], refs[n:]
    rows = q_ref.shape[0]
    start = max(parts[0].shape[1] - even.shape[1], 0)
    wide = even.shape[1]
    half = wide - kdim

    @pl.when(pl.program_id(0) == 0)
    def _():
        pad = jnp.zeros((rows, half), jnp.bfloat16)
        for i in range(n):
            at = slice(i * rows, (i + 1) * rows)
            keys = parts[i][starts[i] : starts[i] + rows, start : start + kdim]
            even[at, :] = jnp.concatenate([keys, pad], axis=1)
            odd[at, :] = jnp.concatenate([pad, keys], axis=1)

    allowed = (kpos_ref[...] >= first_ref[...]) & (kpos_ref[...] <= last_ref[...])
    for i, keys in enumerate((even, odd)):
        at = i * (kdim - half)
        scores = lax.dot_general(
            q_ref[:, at : at + wide], keys[...], NT, preferred_element_type=jnp.float32
        )
        scores = jnp.where(allowed, scores * qk_scale, -1e30)
        expo = jnp.exp(scores - jnp.max(scores, axis=-1, keepdims=True))
        probs = (expo / jnp.sum(expo, axis=-1, keepdims=True)).astype(jnp.bfloat16)
        out_ref[:, i * LATENT : (i + 1) * LATENT] = jnp.dot(
            probs, even[:, :LATENT], preferred_element_type=jnp.float32
        ).astype(jnp.bfloat16)


def attend(queries, parts, first, last, kpos):
    n = len(parts)
    rows, kdim = queries.shape[0], queries.shape[1] // HEADS
    wide = -(-kdim // LANES) * LANES
    return call(
        functools.partial(attend_kernel, [at for _, at in parts], kdim),
        6,
        (HEADS // 2,),
        [whole(first), whole(last), whole(kpos)]
        + [pl.BlockSpec((rows, 2 * kdim), lambda h: (0, h))]
        + [whole(p) for p, _ in parts],
        pl.BlockSpec((rows, 2 * LATENT), lambda h: (0, h)),
        jax.ShapeDtypeStruct((rows, HEADS * LATENT), jnp.bfloat16),
        [pltpu.VMEM((n * rows, wide), jnp.bfloat16)] * 2,
        "attention",
    )(first, last, kpos, queries, *[p for p, _ in parts])


def added(*terms):
    total = terms[0].astype(jnp.float32)
    for term in terms[1:]:
        total = total + term.astype(jnp.float32)
    return total.astype(jnp.bfloat16)


def shards(queries, latent_kv, doc_lengths, hidden_in, router_weight, expert_ids, gate_up, w_down):
    tok_rows, width = hidden_in.shape[1:]
    n_ctx, n_exp = lax.axis_size("ctx"), lax.axis_size("exp")
    ctx, exp = lax.axis_index("ctx"), lax.axis_index("exp")
    local = gate_up.shape[0]
    near = n_exp == 4
    shifts = [0, 1, 3, 2] if near else [0]
    tokens = hidden_in[0]

    def flip(a, bit):
        return lax.ppermute(a, "ctx", [(i, i ^ bit) for i in range(n_ctx)])

    def shift(a, d):
        return lax.ppermute(a, "exp", [(i, i ^ d) for i in range(n_exp)])

    def along_exp(a):
        if near:
            beside, across = shift(a, 1), shift(a, 3)
            return [a, beside, across, shift(across, 1)]
        return [lax.all_gather(a, "exp", axis=0, tiled=True)]

    masks = [0, 2, 1, 3]
    order = jnp.stack([ctx ^ m for m in masks])

    top = expert_ids.shape[2]
    picks = expert_ids[0].T.astype(jnp.bfloat16).reshape(1, top * tok_rows)
    picks = jnp.pad(picks, ((0, EXTRA - 1), (0, width - top * tok_rows)))
    packed = jnp.concatenate([tokens, picks], axis=0)

    keys = latent_kv[0]
    keys = jnp.concatenate([keys, flip(keys, 2)], axis=0)
    near_parts = along_exp(packed)
    arrived = near_parts
    crossed = [flip(a, 2) for a in near_parts[:3]]
    if near:
        crossed.append(shift(crossed[2], 1))
    kv = [(a, k * tok_rows) for a in (keys, flip(keys, 1)) for k in range(2)]
    if near:
        blocks = 1
        gu, token = sort_rows(gate_up, [(), (arrived[1],), (crossed[2],)])
        pairs = [
            stack(a, b, (token,)) if i == 1 else jnp.concatenate([a, b], axis=0)
            for i, (a, b) in enumerate(zip(near_parts, crossed))
        ]
        flipped = [flip(a, 1) for a in pairs]
        spread = [[(a, 0), (a, 1), (b, 0), (b, 1)] for a, b in zip(pairs, flipped)]
    else:
        gu, _ = sort_rows(gate_up, [(), (), ()])
        blocks = near_parts[0].shape[0] // (BLOCK + EXTRA)
        spread = [[(near_parts[0], 0), (crossed[0], 0)]]
        spread[0] = spread[0] + [(flip(a, 1), 0) for a, _ in spread[0]]
    lengths = doc_lengths[0]
    ends = jnp.cumsum(lengths)
    row_pos = order[:, None] * tok_rows + jnp.arange(tok_rows, dtype=jnp.int32)[None, :]
    pos = row_pos[0]
    passed = pos[:, None] >= ends[None, :]
    first = jnp.max(jnp.where(passed, ends[None, :], 0), axis=1)
    context = attend(queries[0], kv, first[:, None], pos[:, None], row_pos.reshape(1, -1))

    seg = jnp.sum((row_pos[..., None] >= ends).astype(jnp.int32), axis=-1)
    sizes = lengths.astype(jnp.float32)
    scale = jnp.broadcast_to((EXPERTS / (top * sizes * sizes))[:, None], (NDOC, LANES))

    base = (exp * local).reshape(1).astype(jnp.int32)
    rw = jnp.roll(router_weight.T, -exp * local, axis=0)
    balance = None
    sent = []
    for i in range(len(shifts)):
        row = (seg.reshape(-1, 1, BLOCK), scale) if near and i == 0 else None
        out = dispatch(spread[i], blocks, top, base, rw, local, row)
        sent.append(out[:3])
        if row is not None:
            balance = out[3]
    made = experts([a[0] for a in sent], [a[1] for a in sent], gu, w_down)
    back = []
    for i in reversed(range(len(shifts))):
        keep, give = combine([sent[i][2]], [made[i]], n_ctx)
        got = flip(give, 1)
        far = added(keep[:, tok_rows:], got[:, tok_rows:])
        crossed_sum = flip(far, 2)
        terms = [keep[:, :tok_rows], got[:, :tok_rows], crossed_sum]
        if shifts[i] == 2:
            joining = shift(added(*terms), 1)
        elif shifts[i] == 3:
            across = added(*terms, joining)
            back.append(shift(across, 3))
        elif i:
            back.append(shift(join(keep, got, crossed_sum, (across,)), 1))
        else:
            back = back + terms
    if near:
        expert_mix = added(*back)
    else:
        expert_mix = lax.psum_scatter(
            added(*back).reshape(-1, width), "exp", scatter_dimension=0, tiled=True
        ).reshape(1, tok_rows, width)

    if balance is None:
        row = lax.all_gather(tokens, "ctx", axis=0, tiled=True)
        router = jax.nn.softmax(
            jnp.dot(row, router_weight, preferred_element_type=jnp.float32), axis=-1
        )
        row_ids = lax.all_gather(expert_ids[0], "ctx", axis=0, tiled=True)
        hot = (row_ids[:, :, None] == jnp.arange(EXPERTS, dtype=jnp.int32)).astype(jnp.float32)
        at = jnp.arange(row.shape[0], dtype=jnp.int32)
        seg_at = jnp.sum((at[:, None] >= ends[None, :]).astype(jnp.int32), axis=1)
        seg_hot = (seg_at[:, None] == jnp.arange(NDOC, dtype=jnp.int32)).astype(jnp.float32)
        exact = lax.Precision.HIGHEST
        counts = jnp.dot(seg_hot.T, hot.sum(axis=1), precision=exact)
        mass = jnp.dot(seg_hot.T, router, precision=exact)
        per_doc = jnp.sum(counts * mass, axis=1) * scale[:, 0]
    else:
        per_doc = balance[:, 0]
    return context[None], expert_mix, per_doc.reshape(1, NDOC)


def solution(mesh):
    rows = P(("group", "exp"), "ctx", None)
    docs = P(("group", "exp"), None)
    return jax.shard_map(
        shards,
        mesh=mesh,
        in_specs=(rows, rows, docs, rows, P(), rows, P("exp", "ctx", None, None), P("exp", "ctx", None)),
        out_specs=(rows, rows, docs),
        check_vma=False,
    )
```
